256 devices in a mesh: dp: 16 (over x, y), tensor: 16 (over z, core).
Axes of the slice: x: 4, y: 4, z: 8, core: 2. Of those that a mesh axis runs over, the one named last changes fastest.
Arguments:
- activations: bfloat16 [32, 256, 8192], P('dp', None, 'tensor'), may hold values from -16 to 16
- out_grads: bfloat16 [32, 256, 8192], P('dp', None, 'tensor'), may hold values from -8 to 8
- lengths: int32 [32], P('dp'), may hold values from 64 to 256, as said below
Outputs:
- grad_weight: bfloat16 [8192, 8192], P('dp', 'tensor')
- seq_norms: float32 [32], P('dp')
The draws below stay inside these ranges and needn't reach their ends.
Inputs may be any that keep to these rules, and one draw needn't show every extreme that they name: `lengths`: every sequence has at least 64 live positions; some sequence has exactly 256 and some exactly 64 in every draw.
All inputs are finite; a program needn't handle non-finite values.
Results may differ from the reference program's by a relative error of at most 0.019.
Values may be sent and summed in bfloat16 or wider, within the bound.
A program may use at most 192 MiB of HBM per device.

```python
import math
import jax
import jax.numpy as jnp
from jax import lax

D = 8192
SLOTS = 2
SLOT_LEN = 256
K = 8192
SEQS = 32
N_DP = 16


def draw_activations(key, part):
    key = jax.random.fold_in(key, 11)
    key_values, key_spread, key_rows, key_shared, key_weight = jax.random.split(key, 5)
    full_shape = (SEQS, SLOT_LEN, K)
    values = jax.random.normal(key_values, full_shape, jnp.float32)
    shared_direction = jax.random.normal(key_shared, (SEQS, 1, K), jnp.float32)
    token_weight = jax.random.uniform(key_weight, (SEQS, SLOT_LEN, 1), jnp.float32, 0.3, 1.7)
    values = values + 0.4 * token_weight * shared_direction
    column_rise = jnp.exp(jnp.log(3.0) * jnp.arange(K, dtype=jnp.float32) / K)
    column_spread = jnp.exp(jnp.log(3.0) * jax.random.uniform(key_spread, (K,), jnp.float32))
    row_scale = jnp.exp(jnp.log(10.0) * jax.random.uniform(key_rows, (SEQS, SLOT_LEN, 1), jnp.float32))
    result = values * column_rise * column_spread * row_scale * 0.025
    return jnp.clip(result, -16.0, 16.0).astype(jnp.bfloat16)


def draw_out_grads(key, part):
    key = jax.random.fold_in(key, 37)
    key_values, key_shared, key_weight = jax.random.split(key, 3)
    full_shape = (SEQS, SLOT_LEN, D)
    values = jax.random.normal(key_values, full_shape, jnp.float32)
    shared_direction = jax.random.normal(key_shared, (SEQS, 1, D), jnp.float32)
    token_weight = jax.random.uniform(key_weight, (SEQS, SLOT_LEN, 1), jnp.float32, 0.3, 1.7)
    result = values + 0.4 * token_weight * shared_direction
    return jnp.clip(result, -8.0, 8.0).astype(jnp.bfloat16)


def draw_lengths(key, part):
    key = jax.random.fold_in(key, 23)
    key_base, key_heavy, key_pick = jax.random.split(key, 3)
    minimal_length = SLOT_LEN // 4
    extent = SLOT_LEN - minimal_length
    random_base_sample = jax.random.randint(key_base, (SEQS // SLOTS, SLOTS), 0, extent + 1)
    heaviness = jax.random.randint(key_heavy, (SEQS // SLOTS, 1), 1, 5)
    scaled = random_base_sample * heaviness // 4
    result = minimal_length + scaled.reshape(SEQS)
    selected_entry = jax.random.randint(key_pick, (), 0, SEQS)
    other_pick = (selected_entry + 1) % SEQS
    places = jnp.arange(SEQS, dtype=jnp.int32)
    result = jnp.where(places == selected_entry, SLOT_LEN, result)
    result = jnp.where(places == other_pick, minimal_length, result)
    return result.astype(jnp.int32)


def setup_inputs(seed: int = 0) -> dict:
    seeds = jax.random.split(jax.random.key(seed), 4)
    activations = draw_activations(jax.random.fold_in(seeds[3], 71), 0)
    out_grads = draw_out_grads(jax.random.fold_in(seeds[3], 71), 0)
    lengths = draw_lengths(jax.random.fold_in(seeds[3], 71), 0)
    return {"activations": activations, "out_grads": out_grads, "lengths": lengths}


def reference(activations, out_grads, lengths):
    positions = jnp.arange(SLOT_LEN, dtype=jnp.int32)
    clip_bound = math.sqrt(K * D * SLOT_LEN / 2.0)

    def one_square(slot_item):
        acts_slot, grads_slot, length_slot = slot_item
        live_mask = (positions < length_slot).astype(jnp.float32)[:, None]
        acts_wide = acts_slot.astype(jnp.float32) * live_mask
        broad_gradient_rows = grads_slot.astype(jnp.float32) * live_mask
        act_gram = jnp.dot(acts_wide, acts_wide.T, precision=lax.Precision.HIGHEST)
        grad_gram = jnp.dot(broad_gradient_rows, broad_gradient_rows.T, precision=lax.Precision.HIGHEST)
        return jnp.sum(act_gram * grad_gram)
    squares = lax.map(one_square, (activations, out_grads, lengths))
    seq_norms = jnp.sqrt(squares + 1e-06)
    factors = jnp.minimum(1.0, clip_bound / seq_norms)
    live_all = (positions[None, :] < lengths[:, None]).astype(jnp.float32)
    weights = factors[:, None] * live_all
    group_rows = SLOTS * SLOT_LEN
    acts_groups = activations.reshape(N_DP, group_rows, K)
    column_width = min(512, D)

    def column_block(block_index):
        grads_block = lax.dynamic_slice_in_dim(out_grads, (block_index * column_width).astype(jnp.int32), column_width, 2).astype(jnp.float32)
        scaled_groups = (grads_block * weights[:, :, None]).reshape(N_DP, group_rows, column_width)

        def add_group(group_index, total):
            single_scaled_gradient = lax.dynamic_index_in_dim(scaled_groups, group_index, 0, keepdims=False)
            acts_one = lax.dynamic_index_in_dim(acts_groups, group_index, 0, keepdims=False).astype(jnp.float32)
            partial_value = jnp.dot(single_scaled_gradient.T, acts_one, precision=lax.Precision.HIGHEST) / SEQS
            partial_value = lax.optimization_barrier(partial_value.astype(jnp.bfloat16))
            return total + partial_value.astype(jnp.float32)
        return lax.fori_loop(0, N_DP, add_group, jnp.zeros((column_width, K), jnp.float32))
    blocks = lax.map(column_block, jnp.arange(D // column_width, dtype=jnp.int32))
    grad_weight = blocks.reshape(D, K).astype(jnp.bfloat16)
    return (grad_weight, seq_norms)
```

```python
import math

import jax
import jax.numpy as jnp
from jax import lax
from jax.experimental import pallas as pl
from jax.experimental.pallas import tpu as pltpu
from jax.sharding import PartitionSpec as P

D = 8192
K = 8192
SLOT_LEN = 256
SEQS = 32
X, Y, Z = 4, 4, 8
NQ = 4
W = 128
F = 512
BOUND = math.sqrt(K * D * SLOT_LEN / 2.0)
F32 = jnp.float32
BF16 = jnp.bfloat16


def rcopy(src, dst, send, recv, device):
    return pltpu.make_async_remote_copy(
        src_ref=src,
        dst_ref=dst,
        send_sem=send,
        recv_sem=recv,
        device_id=device,
        device_id_type=pl.DeviceIdType.MESH,
    )


def kernel(
    len_ref, a_ref, g_ref, out_ref, norm_ref,
    gbuf, at, ats, gpack, gpair, gsum, gz, sz, sy, hold, own, s1, s2, s3, rl, rr, fl, fr,
    ysend, yrecv, upsend, dnsend, zrecv, psend, precv, asend, arecv, afsend,
    gpsend, gprecv, gsend, grecv, szsend, szrecv, sysend, syrecv,
    rlsend, rrsend, rlrecv, rrrecv, flsend, frsend, flrecv, frrecv,
):
    dp = lax.axis_index("dp")
    tn = lax.axis_index("tensor")
    x, y = lax.div(dp, Y), lax.rem(dp, Y)
    z, c = lax.div(tn, 2), lax.rem(tn, 2)

    def dev(x_, y_, z_, c_):
        return (x_ * Y + y_, z_ * 2 + c_)

    def xs(k):
        return lax.rem(x + k, X)

    def ys(k):
        return lax.rem(y + k, Y)

    def zs(k):
        return lax.rem(z + k, Z)

    partner = dev(x, y, z, 1 - c)
    z_up, z_dn = dev(x, y, zs(1), c), dev(x, y, zs(Z - 1), c)
    x_up, x_dn = dev(xs(1), y, z, c), dev(xs(X - 1), y, z, c)
    y_up, y_dn = dev(x, ys(1), z, c), dev(x, ys(Y - 1), z, c)
    y_others = [(ys(k), c) for k in (1, 2, 3)] + [(ys(k), 1 - c) for k in (0, 1, 2, 3)]

    barrier = pltpu.get_barrier_semaphore()
    peers = [dev(x, y2, z, c2) for y2, c2 in y_others]
    peers += [dev(x, y, zs(k), c) for k in range(1, Z)] + [x_up, x_dn]
    for peer in peers:
        pl.semaphore_signal(barrier, inc=1, device_id=peer, device_id_type=pl.DeviceIdType.MESH)
    pl.semaphore_wait(barrier, len(peers))

    xb0 = lax.div(z, 2)
    yt = 2 * lax.rem(z, 2) + c
    is_src = lax.rem(z, 2) == lax.div(y, 2)

    def first(q, h):
        return rcopy(
            g_ref.at[h, :, pl.ds(q * W, W)], gbuf.at[xb0, q, h, y], ysend.at[q, h], yrecv.at[q, y],
            dev(x, yt, z, h),
        )

    for q in range(NQ):
        for h in range(2):
            stays = jnp.logical_and(y == yt, c == h)

            @pl.when(jnp.logical_not(stays))
            def _():
                first(q, h).start()

            @pl.when(stays)
            def _():
                pltpu.make_async_copy(
                    g_ref.at[h, :, pl.ds(q * W, W)], gbuf.at[xb0, q, h, y], yrecv.at[q, y]
                ).start()

    rows = lax.broadcasted_iota(jnp.int32, (SLOT_LEN, F), 0)
    contract = (((1,), (1,)), ((), ()))
    for s in range(2):
        am = jnp.where(rows < len_ref[s], a_ref[s].astype(F32), 0.0)
        at[y, s] = am.T.astype(BF16)
        am = am.astype(BF16)
        g = g_ref[s]
        for m, v in enumerate((am, g)):
            gram = lax.dot_general(v, v, contract, preferred_element_type=F32)
            gpack[s, :, m, 0] = gram[:128, :128].reshape(Z, 16, 128)
            gpack[s, :, m, 1] = gram[:128, 128:].reshape(Z, 16, 128)
            gpack[s, :, m, 2] = gram[128:, 128:].reshape(Z, 16, 128)
    pair = rcopy(gpack.at[1 - c], gpair, gpsend, gprecv, partner)
    pair.start()

    def whole(xb, q):
        return gbuf.at[xb, q, c]

    def to_partner(xb, q):
        return rcopy(whole(xb, q), whole(xb, q), psend.at[xb, q], precv.at[xb, q], partner)

    def to_up(xb, q):
        return rcopy(whole(xb, q), whole(xb, q), upsend.at[xb, q], zrecv.at[xb, q], z_up)

    def to_dn(xb, q):
        return rcopy(whole(xb, q), whole(xb, q), dnsend.at[xb, q], zrecv.at[xb, q], z_dn)

    def start_own(q):
        @pl.when(is_src)
        def _():
            for y2 in range(Y):
                pltpu.make_async_copy(
                    gbuf.at[xb0, q, c, y2], gbuf.at[xb0, q, c, y2], yrecv.at[q, y2]
                ).wait()
            to_up(xb0, q).start()
            to_dn(xb0, q).start()
            to_partner(xb0, q).start()

    def info(p):
        i = p // 2
        q_n, d_n, side_n = i % 4, 1 + 2 * (i // 4), p % 2
        last = p >= 12
        k = p % 3
        q_s = jnp.where(last, p - 12, p // 3)
        d_s = jnp.where(last, 4, jnp.where(k == 0, 0, 2))
        side_s = jnp.where(last, q_s % 2, jnp.where(k == 2, 1, 0))
        q = jnp.where(is_src, q_s, q_n)
        d = jnp.where(is_src, d_s, d_n)
        side = jnp.where(is_src, side_s, side_n)
        z_from = lax.rem(jnp.where(side == 0, z + Z - d, z + d), Z)
        return lax.div(z_from, 2), q, d, side

    def onward(q, d, side):
        far = jnp.logical_and(d == 3, lax.rem(q, 2) == side)
        return jnp.logical_or(jnp.logical_or(d == 1, d == 2), far)

    def receive(p):
        xb, q, d, side = info(p)

        @pl.when(d > 0)
        def _():
            to_up(xb, q).wait_recv()

            @pl.when(jnp.logical_and(onward(q, d, side), side == 0))
            def _():
                to_up(xb, q).start()

            @pl.when(jnp.logical_and(onward(q, d, side), side == 1))
            def _():
                to_dn(xb, q).start()

            to_partner(xb, q).start()

    start_own(0)

    pair.wait_recv()
    gsum[...] = gpack[c] + gpair[...]
    gz[z] = gsum[z]

    def gram_to(k):
        return rcopy(gsum.at[zs(k)], gz.at[z], gsend.at[k - 1], grecv.at[z], dev(x, y, zs(k), c))

    for k in range(1, Z):
        gram_to(k).start()

    start_own(1)

    def act_to(h, side):
        return rcopy(at.at[y, h], at.at[y, h], asend.at[h, side], arecv.at[y, h], (y_up, y_dn)[side])

    for h in range(2):
        for side in range(2):
            act_to(h, side).start()

    start_own(2)
    start_own(3)
    for p in range(3):
        receive(p)

    def from_z(k):
        return rcopy(gsum.at[z], gz.at[zs(k)], gsend.at[k - 1], grecv.at[zs(k)], partner)

    for k in range(1, Z):
        from_z(k).wait_recv()
    total = gz[0]
    for k in range(1, Z):
        total = total + gz[k]
    prod = total[0] * total[1]
    square = jnp.sum(prod[0] + 2.0 * prod[1] + prod[2])
    sz[z] = jnp.full((8, 128), square, F32)

    def square_to(k):
        return rcopy(sz.at[z], sz.at[z], szsend.at[k - 1], szrecv.at[z], dev(x, y, zs(k), c))

    for k in range(1, Z):
        square_to(k).start()

    receive(3)

    for k in range(1, Z):
        rcopy(sz.at[zs(k)], sz.at[zs(k)], szsend.at[k - 1], szrecv.at[zs(k)], partner).wait_recv()
    tile = sz[0]
    for k in range(1, Z):
        tile = tile + sz[k]
    sy[y, c] = tile

    def norm_to(k):
        y2, c2 = y_others[k]
        return rcopy(sy.at[y, c], sy.at[y, c], sysend.at[k], syrecv.at[y, c], dev(x, y2, z, c2))

    for k in range(7):
        norm_to(k).start()

    def act_from(y2, h):
        return rcopy(at.at[y2, h], at.at[y2, h], afsend.at[h], arecv.at[y2, h], (y_up, y_dn)[h])

    act_from(ys(3), 0).wait_recv()
    act_from(ys(3), 0).start()
    act_from(ys(1), 1).wait_recv()
    act_from(ys(1), 1).start()

    receive(4)
    receive(5)

    for k in range(7):
        y2, c2 = y_others[k]
        rcopy(sy.at[y2, c2], sy.at[y2, c2], sysend.at[k], syrecv.at[y2, c2], partner).wait_recv()
    for h in range(2):
        norm_ref[h] = jnp.max(jnp.sqrt(sy[y, h] + 1e-6))
    for y2, h in ((ys(3), 1), (ys(1), 0), (ys(2), 0), (ys(2), 1)):
        act_from(y2, h).wait_recv()
    for h in range(2):
        for y2 in range(Y):
            factor = jnp.max(jnp.minimum(1.0, BOUND / jnp.sqrt(sy[y2, h] + 1e-6)))
            scaled = (at[y2, h].astype(F32) * factor).astype(BF16)
            ats[:, pl.ds((h * Y + y2) * SLOT_LEN, SLOT_LEN)] = scaled

    def relay_up(q):
        return rcopy(s2.at[q, pl.ds(0, 256)], rl.at[q], rlsend.at[q], rlrecv.at[q], x_up)

    def relay_dn(q):
        return rcopy(s2.at[q, pl.ds(256, 256)], rr.at[q], rrsend.at[q], rrrecv.at[q], x_dn)

    def final_up(q):
        return rcopy(s1.at[q], fl.at[q], flsend.at[q], flrecv.at[q], x_up)

    def final_dn(q):
        return rcopy(s3.at[q], fr.at[q], frsend.at[q], frrecv.at[q], x_dn)

    def consume(p):
        xb, q, _, _ = info(p)
        to_other = rcopy(
            gbuf.at[xb, q, 1 - c], gbuf.at[xb, q, 1 - c], psend.at[xb, q], precv.at[xb, q], partner
        )
        to_other.wait_recv()
        piece = gbuf[xb, q].reshape(2 * Y * SLOT_LEN, W)
        part = jnp.dot(ats[...], piece, preferred_element_type=F32) * (1.0 / SEQS)
        o = lax.rem(xb + X - x, X)

        @pl.when(o == 0)
        def _():
            own[q] = part

        @pl.when(o == 2)
        def _():
            s2[q] = part.astype(BF16)
            relay_up(q).start()
            relay_dn(q).start()

        @pl.when(o % 2 == 1)
        def _():
            hold[p % 2] = part

    def finish(p):
        xb, q, _, _ = info(p)
        o = lax.rem(xb + X - x, X)

        @pl.when(o == 1)
        def _():
            relay_up(q).wait_recv()
            s1[q, pl.ds(0, 256)] = (hold[p % 2, pl.ds(0, 256)] + rl[q].astype(F32)).astype(BF16)
            s1[q, pl.ds(256, 256)] = hold[p % 2, pl.ds(256, 256)].astype(BF16)
            final_up(q).start()

        @pl.when(o == 3)
        def _():
            relay_dn(q).wait_recv()
            s3[q, pl.ds(0, 256)] = hold[p % 2, pl.ds(0, 256)].astype(BF16)
            s3[q, pl.ds(256, 256)] = (hold[p % 2, pl.ds(256, 256)] + rr[q].astype(F32)).astype(BF16)
            final_dn(q).start()

    def step(t, _):
        @pl.when(jnp.logical_and(t < 9, t % 2 == 0))
        def _():
            receive(6 + t // 2)

        @pl.when(jnp.logical_and(t >= 9, t < 14))
        def _():
            receive(t + 2)

        consume(t)

        @pl.when(t > 0)
        def _():
            finish(t - 1)

        return 0

    lax.fori_loop(0, 4 * NQ, step, 0)
    finish(4 * NQ - 1)
    for q in range(NQ):
        final_up(q).wait_recv()
        final_dn(q).wait_recv()
        block = own[q] + fl[q].astype(F32) + fr[q].astype(F32)
        out_ref[pl.ds(q * W, W), :] = block.T.astype(BF16)

    for q in range(NQ):
        for h in range(2):
            @pl.when(jnp.logical_not(jnp.logical_and(y == yt, c == h)))
            def _():
                first(q, h).wait_send()

        @pl.when(is_src)
        def _():
            to_up(xb0, q).wait_send()
            to_dn(xb0, q).wait_send()

        relay_up(q).wait_send()
        relay_dn(q).wait_send()
        final_up(q).wait_send()
        final_dn(q).wait_send()
    pair.wait_send()
    for k in range(1, Z):
        gram_to(k).wait_send()
        square_to(k).wait_send()
    for k in range(7):
        norm_to(k).wait_send()
    for h in range(2):
        for side in range(2):
            act_to(h, side).wait_send()
        act_from((ys(3), ys(1))[h], h).wait_send()

    def drain(p, _):
        xb, q, d, side = info(p)
        to_partner(xb, q).wait_send()

        @pl.when(jnp.logical_and(onward(q, d, side), side == 0))
        def _():
            to_up(xb, q).wait_send()

        @pl.when(jnp.logical_and(onward(q, d, side), side == 1))
        def _():
            to_dn(xb, q).wait_send()

        return 0

    lax.fori_loop(0, 4 * NQ, drain, 0)


def local(activations, out_grads, lengths):
    dma, vmem = pltpu.SemaphoreType.DMA, pltpu.VMEM
    scratch = [
        vmem((X, NQ, 2, Y, SLOT_LEN, W), BF16),
        vmem((Y, 2, F, SLOT_LEN), BF16),
        vmem((F, 2 * Y * SLOT_LEN), BF16),
        vmem((2, Z, 2, 3, 16, 128), F32),
        vmem((Z, 2, 3, 16, 128), F32),
        vmem((Z, 2, 3, 16, 128), F32),
        vmem((Z, 2, 3, 16, 128), F32),
        vmem((Z, 8, 128), F32),
        vmem((Y, 2, 8, 128), F32),
        vmem((2, F, W), F32),
        vmem((NQ, F, W), F32),
        vmem((NQ, F, W), BF16),
        vmem((NQ, F, W), BF16),
        vmem((NQ, F, W), BF16),
        vmem((NQ, 256, W), BF16),
        vmem((NQ, 256, W), BF16),
        vmem((NQ, F, W), BF16),
        vmem((NQ, F, W), BF16),
        dma((NQ, 2)), dma((NQ, Y)), dma((X, NQ)), dma((X, NQ)), dma((X, NQ)),
        dma((X, NQ)), dma((X, NQ)), dma((2, 2)), dma((Y, 2)), dma((2,)),
        dma, dma, dma((7,)), dma((Z,)), dma((7,)), dma((Z,)), dma((7,)), dma((Y, 2)),
        dma((NQ,)), dma((NQ,)), dma((NQ,)), dma((NQ,)), dma((NQ,)), dma((NQ,)), dma((NQ,)), dma((NQ,)),
    ]
    return pl.pallas_call(
        kernel,
        out_shape=(
            jax.ShapeDtypeStruct((F, F), BF16),
            jax.ShapeDtypeStruct((2,), F32),
        ),
        in_specs=[
            pl.BlockSpec(memory_space=pltpu.SMEM),
            pl.BlockSpec(memory_space=pltpu.VMEM),
            pl.BlockSpec(memory_space=pltpu.VMEM),
        ],
        out_specs=(
            pl.BlockSpec(memory_space=pltpu.VMEM),
            pl.BlockSpec(memory_space=pltpu.SMEM),
        ),
        scratch_shapes=scratch,
        compiler_params=pltpu.CompilerParams(
            collective_id=0, has_side_effects=True, vmem_limit_bytes=48 * 1024 * 1024
        ),
        cost_estimate=pl.CostEstimate(flops=2 * 512 * 512 * 8192, bytes_accessed=3 * 2**19, transcendentals=0),
    )(lengths, activations, out_grads)


def solution(mesh):
    placed = (P("dp", None, "tensor"), P("dp", None, "tensor"), P("dp"))
    return jax.shard_map(
        local, mesh=mesh, in_specs=placed, out_specs=(P("dp", "tensor"), P("dp")), check_vma=False
    )
```

```python
import math

import jax
import jax.numpy as jnp
from jax import lax
from jax.experimental import pallas as pl
from jax.experimental.pallas import tpu as pltpu
from jax.sharding import PartitionSpec as P

D = 8192
K = 8192
SLOT_LEN = 256
SEQS = 32
X, Y, Z = 4, 4, 8
NQ = 4
W = 128
F = 512
BOUND = math.sqrt(K * D * SLOT_LEN / 2.0)
F32 = jnp.float32
BF16 = jnp.bfloat16


def rcopy(src, dst, send, recv, device):
    return pltpu.make_async_remote_copy(
        src_ref=src,
        dst_ref=dst,
        send_sem=send,
        recv_sem=recv,
        device_id=device,
        device_id_type=pl.DeviceIdType.MESH,
    )


def kernel(
    len_ref, a_hbm, g_hbm, out_ref, norm_ref,
    a_ref, g_ref, loads, gbuf, at, ats, gpack, gpair, gsum, gz, sz, sy, hold, own, s1, s2, s3, rl, rr, fl, fr,
    ysend, yrecv, upsend, dnsend, zrecv, psend, precv, asend, arecv, afsend,
    gpsend, gprecv, gsend, grecv, szsend, szrecv, sysend, syrecv,
    rlsend, rrsend, rlrecv, rrrecv, flsend, frsend, flrecv, frrecv,
):
    dp = lax.axis_index("dp")
    tn = lax.axis_index("tensor")
    x, y = lax.div(dp, Y), lax.rem(dp, Y)
    z, c = lax.div(tn, 2), lax.rem(tn, 2)

    def dev(x_, y_, z_, c_):
        return (x_ * Y + y_, z_ * 2 + c_)

    def xs(k):
        return lax.rem(x + k, X)

    def ys(k):
        return lax.rem(y + k, Y)

    def zs(k):
        return lax.rem(z + k, Z)

    partner = dev(x, y, z, 1 - c)
    z_up, z_dn = dev(x, y, zs(1), c), dev(x, y, zs(Z - 1), c)
    x_up, x_dn = dev(xs(1), y, z, c), dev(xs(X - 1), y, z, c)
    y_up, y_dn = dev(x, ys(1), z, c), dev(x, ys(Y - 1), z, c)
    y_others = [(ys(k), c) for k in (1, 2, 3)] + [(ys(k), 1 - c) for k in (0, 1, 2, 3)]

    load_a = pltpu.make_async_copy(a_hbm, a_ref, loads.at[0])
    load_g = pltpu.make_async_copy(g_hbm, g_ref, loads.at[1])
    load_g.start()
    load_a.start()

    barrier = pltpu.get_barrier_semaphore()
    peers = [dev(x, y2, z, c2) for y2, c2 in y_others]
    peers += [dev(x, y, zs(k), c) for k in range(1, Z)] + [x_up, x_dn]
    for peer in peers:
        pl.semaphore_signal(barrier, inc=1, device_id=peer, device_id_type=pl.DeviceIdType.MESH)
    pl.semaphore_wait(barrier, len(peers))

    xb0 = lax.div(z, 2)
    yt = 2 * lax.rem(z, 2) + c
    is_src = lax.rem(z, 2) == lax.div(y, 2)

    def first(q, h):
        return rcopy(
            g_hbm.at[h, :, pl.ds(q * W, W)], gbuf.at[xb0, q, h, y], ysend.at[q, h], yrecv.at[q, y],
            dev(x, yt, z, h),
        )

    def start_first(q):
        for h in range(2):
            stays = jnp.logical_and(y == yt, c == h)

            @pl.when(jnp.logical_not(stays))
            def _():
                first(q, h).start()

            @pl.when(stays)
            def _():
                pltpu.make_async_copy(
                    g_hbm.at[h, :, pl.ds(q * W, W)], gbuf.at[xb0, q, h, y], yrecv.at[q, y]
                ).start()

    def wait_first(q):
        for h in range(2):
            @pl.when(jnp.logical_not(jnp.logical_and(y == yt, c == h)))
            def _():
                first(q, h).wait_send()

    start_first(0)
    start_first(1)
    load_g.wait()
    load_a.wait()

    rows = lax.broadcasted_iota(jnp.int32, (SLOT_LEN, F), 0)
    contract = (((1,), (1,)), ((), ()))
    for s in range(2):
        am = jnp.where(rows < len_ref[s], a_ref[s].astype(F32), 0.0)
        at[y, s] = am.T.astype(BF16)
        am = am.astype(BF16)
        g = g_ref[s]
        for m, v in enumerate((am, g)):
            gram = lax.dot_general(v, v, contract, preferred_element_type=F32)
            gpack[s, :, m, 0] = gram[:128, :128].reshape(Z, 16, 128)
            gpack[s, :, m, 1] = gram[:128, 128:].reshape(Z, 16, 128)
            gpack[s, :, m, 2] = gram[128:, 128:].reshape(Z, 16, 128)
    pair = rcopy(gpack.at[1 - c], gpair, gpsend, gprecv, partner)
    pair.start()

    def whole(xb, q):
        return gbuf.at[xb, q, c]

    def to_partner(xb, q):
        return rcopy(whole(xb, q), whole(xb, q), psend.at[xb, q], precv.at[xb, q], partner)

    def to_up(xb, q):
        return rcopy(whole(xb, q), whole(xb, q), upsend.at[xb, q], zrecv.at[xb, q], z_up)

    def to_dn(xb, q):
        return rcopy(whole(xb, q), whole(xb, q), dnsend.at[xb, q], zrecv.at[xb, q], z_dn)

    def start_own(q):
        @pl.when(is_src)
        def _():
            for y2 in range(Y):
                pltpu.make_async_copy(
                    gbuf.at[xb0, q, c, y2], gbuf.at[xb0, q, c, y2], yrecv.at[q, y2]
                ).wait()
            to_up(xb0, q).start()
            to_dn(xb0, q).start()
            to_partner(xb0, q).start()

    def info(p):
        i = p // 2
        q_n, d_n, side_n = i % 4, 1 + 2 * (i // 4), p % 2
        last = p >= 12
        k = p % 3
        q_s = jnp.where(last, p - 12, p // 3)
        d_s = jnp.where(last, 4, jnp.where(k == 0, 0, 2))
        side_s = jnp.where(last, q_s % 2, jnp.where(k == 2, 1, 0))
        q = jnp.where(is_src, q_s, q_n)
        d = jnp.where(is_src, d_s, d_n)
        side = jnp.where(is_src, side_s, side_n)
        z_from = lax.rem(jnp.where(side == 0, z + Z - d, z + d), Z)
        return lax.div(z_from, 2), q, d, side

    def onward(q, d, side):
        far = jnp.logical_and(d == 3, lax.rem(q, 2) == side)
        return jnp.logical_or(jnp.logical_or(d == 1, d == 2), far)

    def receive(p):
        xb, q, d, side = info(p)

        @pl.when(d > 0)
        def _():
            to_up(xb, q).wait_recv()

            @pl.when(jnp.logical_and(onward(q, d, side), side == 0))
            def _():
                to_up(xb, q).start()

            @pl.when(jnp.logical_and(onward(q, d, side), side == 1))
            def _():
                to_dn(xb, q).start()

            to_partner(xb, q).start()

    def own_left(q):
        @pl.when(is_src)
        def _():
            to_up(xb0, q).wait_send()
            to_dn(xb0, q).wait_send()

    def receive_as(src, *pieces):
        @pl.when(is_src == src)
        def _():
            for p in pieces:
                receive(p)

    wait_first(0)
    start_first(2)
    start_own(0)

    pair.wait_recv()
    gsum[...] = gpack[c] + gpair[...]
    gz[z] = gsum[z]

    def gram_to(k):
        return rcopy(gsum.at[zs(k)], gz.at[z], gsend.at[k - 1], grecv.at[z], dev(x, y, zs(k), c))

    for k in range(1, Z):
        gram_to(k).start()

    wait_first(1)
    start_first(3)
    own_left(0)
    start_own(1)
    receive_as(False, 0, 1)

    def act_to(h, side):
        return rcopy(at.at[y, h], at.at[y, h], asend.at[h, side], arecv.at[y, h], (y_up, y_dn)[side])

    wait_first(2)
    for h in range(2):
        for side in range(2):
            act_to(h, side).start()

    def from_z(k):
        return rcopy(gsum.at[z], gz.at[zs(k)], gsend.at[k - 1], grecv.at[zs(k)], partner)

    for k in range(1, Z):
        from_z(k).wait_recv()
    total = gz[0]
    for k in range(1, Z):
        total = total + gz[k]
    prod = total[0] * total[1]
    square = jnp.sum(prod[0] + 2.0 * prod[1] + prod[2])
    sz[z] = jnp.full((8, 128), square, F32)

    def square_to(k):
        return rcopy(sz.at[z], sz.at[z], szsend.at[k - 1], szrecv.at[z], dev(x, y, zs(k), c))

    for k in range(1, Z):
        square_to(k).start()

    own_left(1)
    start_own(2)
    receive_as(False, 2, 3)
    receive_as(True, 0, 1, 2)

    for k in range(1, Z):
        rcopy(sz.at[zs(k)], sz.at[zs(k)], szsend.at[k - 1], szrecv.at[zs(k)], partner).wait_recv()
    tile = sz[0]
    for k in range(1, Z):
        tile = tile + sz[k]
    sy[y, c] = tile

    def norm_to(k):
        y2, c2 = y_others[k]
        return rcopy(sy.at[y, c], sy.at[y, c], sysend.at[k], syrecv.at[y, c], dev(x, y2, z, c2))

    for k in range(7):
        norm_to(k).start()

    def act_from(y2, h):
        return rcopy(at.at[y2, h], at.at[y2, h], afsend.at[h], arecv.at[y2, h], (y_up, y_dn)[h])

    act_from(ys(3), 0).wait_recv()
    act_from(ys(3), 0).start()
    act_from(ys(1), 1).wait_recv()
    act_from(ys(1), 1).start()

    own_left(2)
    start_own(3)
    receive_as(False, 4, 5)
    receive_as(True, 3, 4, 5)

    for k in range(7):
        y2, c2 = y_others[k]
        rcopy(sy.at[y2, c2], sy.at[y2, c2], sysend.at[k], syrecv.at[y2, c2], partner).wait_recv()
    for h in range(2):
        norm_ref[h] = jnp.max(jnp.sqrt(sy[y, h] + 1e-6))
    for y2, h in ((ys(3), 1), (ys(1), 0), (ys(2), 0), (ys(2), 1)):
        act_from(y2, h).wait_recv()
    for h in range(2):
        for y2 in range(Y):
            factor = jnp.max(jnp.minimum(1.0, BOUND / jnp.sqrt(sy[y2, h] + 1e-6)))
            scaled = (at[y2, h].astype(F32) * factor).astype(BF16)
            ats[:, pl.ds((h * Y + y2) * SLOT_LEN, SLOT_LEN)] = scaled

    def relay_up(q):
        return rcopy(s2.at[q, pl.ds(0, 256)], rl.at[q], rlsend.at[q], rlrecv.at[q], x_up)

    def relay_dn(q):
        return rcopy(s2.at[q, pl.ds(256, 256)], rr.at[q], rrsend.at[q], rrrecv.at[q], x_dn)

    def final_up(q):
        return rcopy(s1.at[q], fl.at[q], flsend.at[q], flrecv.at[q], x_up)

    def final_dn(q):
        return rcopy(s3.at[q], fr.at[q], frsend.at[q], frrecv.at[q], x_dn)

    def consume(p):
        xb, q, _, _ = info(p)
        to_other = rcopy(
            gbuf.at[xb, q, 1 - c], gbuf.at[xb, q, 1 - c], psend.at[xb, q], precv.at[xb, q], partner
        )
        to_other.wait_recv()
        piece = gbuf[xb, q].reshape(2 * Y * SLOT_LEN, W)
        part = jnp.dot(ats[...], piece, preferred_element_type=F32) * (1.0 / SEQS)
        o = lax.rem(xb + X - x, X)

        @pl.when(o == 0)
        def _():
            own[q] = part

        @pl.when(o == 2)
        def _():
            s2[q] = part.astype(BF16)
            relay_up(q).start()
            relay_dn(q).start()

        @pl.when(o % 2 == 1)
        def _():
            hold[p % 2] = part

    def finish(p):
        xb, q, _, _ = info(p)
        o = lax.rem(xb + X - x, X)

        @pl.when(o == 1)
        def _():
            relay_up(q).wait_recv()
            s1[q, pl.ds(0, 256)] = (hold[p % 2, pl.ds(0, 256)] + rl[q].astype(F32)).astype(BF16)
            s1[q, pl.ds(256, 256)] = hold[p % 2, pl.ds(256, 256)].astype(BF16)
            final_up(q).start()

        @pl.when(o == 3)
        def _():
            relay_dn(q).wait_recv()
            s3[q, pl.ds(0, 256)] = hold[p % 2, pl.ds(0, 256)].astype(BF16)
            s3[q, pl.ds(256, 256)] = (hold[p % 2, pl.ds(256, 256)] + rr[q].astype(F32)).astype(BF16)
            final_dn(q).start()

    def step(t, _):
        @pl.when(jnp.logical_and(t < 9, t % 2 == 0))
        def _():
            receive(6 + t // 2)

        @pl.when(jnp.logical_and(t >= 9, t < 14))
        def _():
            receive(t + 2)

        consume(t)

        @pl.when(t > 0)
        def _():
            finish(t - 1)

        return 0

    lax.fori_loop(0, 4 * NQ, step, 0)
    finish(4 * NQ - 1)
    for q in range(NQ):
        final_up(q).wait_recv()
        final_dn(q).wait_recv()
        block = own[q] + fl[q].astype(F32) + fr[q].astype(F32)
        out_ref[pl.ds(q * W, W), :] = block.T.astype(BF16)

    wait_first(3)
    own_left(3)
    for q in range(NQ):
        relay_up(q).wait_send()
        relay_dn(q).wait_send()
        final_up(q).wait_send()
        final_dn(q).wait_send()
    pair.wait_send()
    for k in range(1, Z):
        gram_to(k).wait_send()
        square_to(k).wait_send()
    for k in range(7):
        norm_to(k).wait_send()
    for h in range(2):
        for side in range(2):
            act_to(h, side).wait_send()
        act_from((ys(3), ys(1))[h], h).wait_send()

    def drain(p, _):
        xb, q, d, side = info(p)
        to_partner(xb, q).wait_send()

        @pl.when(jnp.logical_and(onward(q, d, side), side == 0))
        def _():
            to_up(xb, q).wait_send()

        @pl.when(jnp.logical_and(onward(q, d, side), side == 1))
        def _():
            to_dn(xb, q).wait_send()

        return 0

    lax.fori_loop(0, 4 * NQ, drain, 0)


def local(activations, out_grads, lengths):
    dma, vmem = pltpu.SemaphoreType.DMA, pltpu.VMEM
    scratch = [
        vmem((2, SLOT_LEN, F), BF16),
        vmem((2, SLOT_LEN, F), BF16),
        dma((2,)),
        vmem((X, NQ, 2, Y, SLOT_LEN, W), BF16),
        vmem((Y, 2, F, SLOT_LEN), BF16),
        vmem((F, 2 * Y * SLOT_LEN), BF16),
        vmem((2, Z, 2, 3, 16, 128), F32),
        vmem((Z, 2, 3, 16, 128), F32),
        vmem((Z, 2, 3, 16, 128), F32),
        vmem((Z, 2, 3, 16, 128), F32),
        vmem((Z, 8, 128), F32),
        vmem((Y, 2, 8, 128), F32),
        vmem((2, F, W), F32),
        vmem((NQ, F, W), F32),
        vmem((NQ, F, W), BF16),
        vmem((NQ, F, W), BF16),
        vmem((NQ, F, W), BF16),
        vmem((NQ, 256, W), BF16),
        vmem((NQ, 256, W), BF16),
        vmem((NQ, F, W), BF16),
        vmem((NQ, F, W), BF16),
        dma((NQ, 2)), dma((NQ, Y)), dma((X, NQ)), dma((X, NQ)), dma((X, NQ)),
        dma((X, NQ)), dma((X, NQ)), dma((2, 2)), dma((Y, 2)), dma((2,)),
        dma, dma, dma((7,)), dma((Z,)), dma((7,)), dma((Z,)), dma((7,)), dma((Y, 2)),
        dma((NQ,)), dma((NQ,)), dma((NQ,)), dma((NQ,)), dma((NQ,)), dma((NQ,)), dma((NQ,)), dma((NQ,)),
    ]
    return pl.pallas_call(
        kernel,
        out_shape=(
            jax.ShapeDtypeStruct((F, F), BF16),
            jax.ShapeDtypeStruct((2,), F32),
        ),
        in_specs=[
            pl.BlockSpec(memory_space=pltpu.SMEM),
            pl.BlockSpec(memory_space=pl.ANY),
            pl.BlockSpec(memory_space=pl.ANY),
        ],
        out_specs=(
            pl.BlockSpec(memory_space=pltpu.VMEM),
            pl.BlockSpec(memory_space=pltpu.SMEM),
        ),
        scratch_shapes=scratch,
        compiler_params=pltpu.CompilerParams(
            collective_id=0, has_side_effects=True, vmem_limit_bytes=63 * 1024 * 1024 + 768 * 1024
        ),
        cost_estimate=pl.CostEstimate(flops=2 * 512 * 512 * 8192, bytes_accessed=3 * 2**19, transcendentals=0),
    )(lengths, activations, out_grads)


def solution(mesh):
    placed = (P("dp", None, "tensor"), P("dp", None, "tensor"), P("dp"))
    return jax.shard_map(
        local, mesh=mesh, in_specs=placed, out_specs=(P("dp", "tensor"), P("dp")), check_vma=False
    )
```

```python
import math

import jax
import jax.numpy as jnp
from jax import lax
from jax.experimental import pallas as pl
from jax.experimental.pallas import tpu as pltpu
from jax.sharding import PartitionSpec as P

D = 8192
K = 8192
SLOT_LEN = 256
SEQS = 32
X, Y, Z = 4, 4, 8
NQ = 4
W = 128
F = 512
BOUND = math.sqrt(K * D * SLOT_LEN / 2.0)
F32 = jnp.float32
BF16 = jnp.bfloat16

FIRST = (
    ("firstL",), ("f1", 1), ("f1", 0), ("f23", 0), ("gram",), ("k", 0, 0), ("f1", 2), ("k", 0, 1), ("gram",),
    ("f1", 3), ("pairs",), ("acts", 3), ("k", 1, 0), ("f23", 1),
)
SOURCE = (
    ("k", 1, 1), ("k", 0, 3), ("k", 2, 0), ("k", 3, 0), ("w23", 0), ("pairw",), ("k", 0, 2), ("ring", 1),
    ("w23", 1), ("k", 1, 2), ("ring", 2), ("f23", 2), ("k", 1, 3), ("k", 2, 1), ("k", 3, 1), ("f23", 3),
    ("ring", 3), ("k", 2, 2), ("k", 3, 2), ("acts", 1), ("ring", 4), ("ringend",), ("k", 2, 3), ("szs",),
    ("ru", 0, 0), ("k", 3, 3), ("ru", 0, 1), ("szw",), ("arel", 0), ("arel", 1), ("ru", 1, 0), ("ru", 1, 1),
    ("syw",), ("aw",), ("ru", 2, 0), ("ru", 2, 1), ("C",), ("C",), ("C",), ("ru", 3, 0), ("ru", 3, 1), ("C",),
    ("ru", 4, 0), ("ru", 4, 1), ("C",), ("ru", 5, 0), ("ru", 5, 1), ("C",), ("C",), ("C",),
)
OTHER = (
    ("w23", 0), ("f23", 2), ("pairw",), ("ring", 1), ("w23", 1), ("f23", 3), ("ring", 2), ("ru", 0, 0),
    ("ru", 0, 1), ("ring", 3), ("ring", 4), ("ringend",), ("szs",), ("ru", 1, 0), ("ru", 1, 1), ("szw",),
    ("acts", 1), ("arel", 0), ("arel", 1), ("ru", 2, 0), ("ru", 2, 1), ("syw",), ("aw",), ("ru", 3, 0),
    ("ru", 3, 1), ("ru", 4, 0), ("ru", 4, 1), ("C",), ("ru", 5, 0), ("ru", 5, 1), ("C",), ("C",), ("C",),
    ("ru", 6, 0), ("ru", 6, 1), ("C",), ("ru", 7, 0), ("ru", 7, 1), ("C",), ("C",), ("C",),
)

def rcopy(src, dst, send, recv, device):
    return pltpu.make_async_remote_copy(
        src_ref=src,
        dst_ref=dst,
        send_sem=send,
        recv_sem=recv,
        device_id=device,
        device_id_type=pl.DeviceIdType.MESH,
    )


def wait_bytes(ref, sem):
    pltpu.make_async_copy(ref, ref, sem).wait()


def kernel(
    len_ref, a_hbm, g_hbm, out_ref, norm_ref,
    a_ref, g_ref, gbuf, at, ats, gpack, gpair, gsum, gup, gdn, sup, sdn, sz, sy,
    hold, own, s1, s2, s3, rl, rr, fl, fr,
    loads, ysend, yrecv, kup, kdn, zsend, zrecv, psend, precv, asend, arecv, afsend,
    gpsend, gprecv, gupsend, guprecv, gdnsend, gdnrecv, szsend, szrecv, sysend, syrecv,
    rsend, rlrecv, rrrecv, fsend, flrecv, frrecv,
):
    dp = lax.axis_index("dp")
    tn = lax.axis_index("tensor")
    x, y = lax.div(dp, Y), lax.rem(dp, Y)
    z, c = lax.div(tn, 2), lax.rem(tn, 2)

    def dev(x_, y_, z_, c_):
        return (x_ * Y + y_, z_ * 2 + c_)

    def xs(k):
        return lax.rem(x + k, X)

    def ys(k):
        return lax.rem(y + k, Y)

    def zs(k):
        return lax.rem(z + k + Z, Z)

    partner = dev(x, y, z, 1 - c)
    z_up, z_dn = dev(x, y, zs(1), c), dev(x, y, zs(-1), c)
    x_up, x_dn = dev(xs(1), y, z, c), dev(xs(3), y, z, c)
    y_up, y_dn = dev(x, ys(1), z, c), dev(x, ys(3), z, c)
    y_others = [(ys(k), c) for k in (1, 2, 3)] + [(ys(k), 1 - c) for k in (0, 1, 2, 3)]

    load_a = pltpu.make_async_copy(a_hbm, a_ref, loads.at[0])
    load_g = pltpu.make_async_copy(g_hbm, g_ref, loads.at[1])
    load_a.start()
    load_g.start()

    barrier = pltpu.get_barrier_semaphore()
    peers = [dev(x, y2, z, c2) for y2, c2 in y_others]
    peers += [dev(x, y, zs(k), c) for k in range(1, Z)] + [x_up, x_dn]
    for peer in peers:
        pl.semaphore_signal(barrier, inc=1, device_id=peer, device_id_type=pl.DeviceIdType.MESH)
    load_a.wait()
    load_g.wait()
    pl.semaphore_wait(barrier, len(peers))

    xb0 = lax.div(z, 2)
    yt = 2 * lax.rem(z, 2) + c
    is_src = lax.rem(z, 2) == lax.div(y, 2)
    steps_y = lax.rem(y - yt + Y, Y)

    def first(q, h):
        return rcopy(
            g_hbm.at[h, :, pl.ds(q * W, W)], gbuf.at[xb0, q, h, steps_y], ysend.at[q, h],
            yrecv.at[q, steps_y], dev(x, yt, z, h),
        )

    def first_stay():
        @pl.when(steps_y == 0)
        def _():
            for q in range(NQ):
                pltpu.make_async_copy(
                    g_hbm.at[c, :, pl.ds(q * W, W)], gbuf.at[xb0, q, c, 0], yrecv.at[q, 0]
                ).start()
                first(q, 1 - c).start()

    def first_near(q):
        @pl.when(steps_y == 1)
        def _():
            first(q, 0).start()
            first(q, 1).start()

    def first_far(q):
        @pl.when(steps_y >= 2)
        def _():
            first(q, 0).start()
            first(q, 1).start()

    def far_left(q):
        @pl.when(steps_y >= 2)
        def _():
            first(q, 0).wait_send()
            first(q, 1).wait_send()

    rows = lax.broadcasted_iota(jnp.int32, (SLOT_LEN, F), 0)
    contract = (((1,), (1,)), ((), ()))
    done = []

    def gram():
        s = len(done)
        done.append(s)
        am = jnp.where(rows < len_ref[s], a_ref[s].astype(F32), 0.0)
        at[y, s] = am.T.astype(BF16)
        am = am.astype(BF16)
        g = g_ref[s]
        for m, v in enumerate((am, g)):
            full = lax.dot_general(v, v, contract, preferred_element_type=F32)
            gpack[s, :, m, 0] = full[:128, :128].reshape(Z, 16, 128)
            gpack[s, :, m, 1] = full[:128, 128:].reshape(Z, 16, 128)
            gpack[s, :, m, 2] = full[128:, 128:].reshape(Z, 16, 128)

    pair = rcopy(gpack.at[1 - c], gpair, gpsend, gprecv, partner)

    def pair_wait():
        pair.wait_recv()
        gsum[...] = gpack[c] + gpair[...]

    def ring_up(i):
        src = gsum.at[zs(4)] if i == 1 else sup.at[i - 2]
        return rcopy(src, gup.at[i - 1], gupsend.at[i - 1], guprecv.at[i - 1], z_up)

    def ring_dn(i):
        src = gsum.at[zs(-3)] if i == 1 else sdn.at[i - 2]
        return rcopy(src, gdn.at[i - 1], gdnsend.at[i - 1], gdnrecv.at[i - 1], z_dn)

    def ring(i):
        if i > 1:
            ring_up(i - 1).wait_recv()
            sup[i - 2] = gsum[zs(5 - i)] + gup[i - 2]
        ring_up(i).start()
        if i <= 3:
            if i > 1:
                ring_dn(i - 1).wait_recv()
                sdn[i - 2] = gsum[zs(i - 4)] + gdn[i - 2]
            ring_dn(i).start()

    def ring_end():
        ring_up(4).wait_recv()
        ring_dn(3).wait_recv()
        total = gsum[z] + gup[3] + gdn[2]
        prod = total[0] * total[1]
        square = jnp.sum(prod[0] + 2.0 * prod[1] + prod[2])
        sz[z] = jnp.full((8, 128), square, F32)

    def squares():
        for k in range(1, Z):
            rcopy(sz.at[z], sz.at[z], szsend, szrecv.at[z], dev(x, y, zs(k), c)).start()

    def squares_wait():
        for k in range(1, Z):
            rcopy(sz.at[zs(k)], sz.at[zs(k)], szsend, szrecv.at[zs(k)], partner).wait_recv()
        tile = sz[0]
        for k in range(1, Z):
            tile = tile + sz[k]
        mine = y * 2 + c
        sy[mine] = tile
        for y2, c2 in y_others:
            rcopy(sy.at[mine], sy.at[mine], sysend, syrecv.at[mine], dev(x, y2, z, c2)).start()

    def norms_wait():
        for y2, c2 in y_others:
            slot = y2 * 2 + c2
            rcopy(sy.at[slot], sy.at[slot], sysend, syrecv.at[slot], partner).wait_recv()

    def acts(side):
        for h in range(2):
            rcopy(at.at[y, h], at.at[y, h], asend.at[side // 2], arecv.at[y, h], y_up if side == 1 else y_dn).start()

    def act_from(y2, h):
        return rcopy(at.at[y2, h], at.at[y2, h], afsend, arecv.at[y2, h], y_dn)

    def act_relay(h):
        act_from(ys(1), h).wait_recv()
        act_from(ys(1), h).start()

    def scale():
        for h in range(2):
            norm_ref[h] = jnp.max(jnp.sqrt(sy[y * 2 + h] + 1e-6))
            act_from(ys(3), h).wait_recv()
            act_from(ys(2), h).wait_recv()
        for h in range(2):
            for k in range(Y):
                factor = jnp.max(jnp.minimum(1.0, BOUND / jnp.sqrt(sy[ys(k) * 2 + h] + 1e-6)))
                scaled = (at[ys(k), h].astype(F32) * factor).astype(BF16)
                ats[:, pl.ds((h * Y + k) * SLOT_LEN, SLOT_LEN)] = scaled

    def unit(xb, q, u, core):
        return gbuf.at[xb, q, core, pl.ds(2 * u, 2)]

    def to_partner(xb, q, u):
        return rcopy(unit(xb, q, u, c), unit(xb, q, u, c), psend, precv.at[xb, q, u], partner)

    def onward(xb, q, u, side):
        return rcopy(
            unit(xb, q, u, c), unit(xb, q, u, c), zsend, zrecv.at[xb, q, u], (z_up, z_dn)[side]
        )

    def own_part(k, q):
        part = gbuf.at[xb0, q, c, k]
        wait_bytes(part, yrecv.at[q, k])
        rcopy(part, part, kup, zrecv.at[xb0, q, k // 2], z_up).start()
        rcopy(part, part, kdn, zrecv.at[xb0, q, k // 2], z_dn).start()
        if k % 2 == 1:
            to_partner(xb0, q, k // 2).start()

    def place(p, src):
        if src:
            if p < 4:
                return p, 0, 0
            return ((p - 4) // 2, 2, p % 2) if p < 12 else (p - 12, 4, p % 2)
        return (p // 2) % 4, 1 + 2 * (p // 8), p % 2

    def receive(i, u, src):
        for p in (4 + 2 * i, 5 + 2 * i) if src else (2 * i, 2 * i + 1):
            q, d, side = place(p, src)
            xb = lax.div(zs(-d if side == 0 else d), 2)
            onward(xb, q, u, 0).wait_recv()
            if d < 3 or (d == 3 and q % 2 == side):
                onward(xb, q, u, side).start()
            to_partner(xb, q, u).start()

    def info(p):
        q_n, d_n = lax.rem(lax.div(p, 2), 4), 1 + 2 * lax.div(p, 8)
        q_s = jnp.where(p < 4, p, jnp.where(p < 12, lax.div(p - 4, 2), p - 12))
        d_s = jnp.where(p < 4, 0, jnp.where(p < 12, 2, 4))
        q = jnp.where(is_src, q_s, q_n)
        d = jnp.where(is_src, d_s, d_n)
        z_from = lax.rem(jnp.where(lax.rem(p, 2) == 0, z + Z - d, z + d), Z)
        return lax.div(z_from, 2), q

    def relay_up(q):
        return rcopy(s2.at[q, pl.ds(0, 256)], rl.at[q], rsend.at[0], rlrecv.at[q], x_up)

    def relay_dn(q):
        return rcopy(s2.at[q, pl.ds(256, 256)], rr.at[q], rsend.at[1], rrrecv.at[q], x_dn)

    def final_up(q):
        return rcopy(s1.at[q], fl.at[q], fsend.at[0], flrecv.at[q], x_up)

    def final_dn(q):
        return rcopy(s3.at[q], fr.at[q], fsend.at[1], frrecv.at[q], x_dn)

    def consume(t):
        pieces = []
        for j in range(2):
            xb, q = info(2 * t + j)
            for u in range(2):
                other = unit(xb, q, u, 1 - c)
                rcopy(other, other, psend, precv.at[xb, q, u], partner).wait_recv()
            pieces.append(gbuf[xb, q].reshape(2 * Y * SLOT_LEN, W))
        both = jnp.concatenate(pieces, axis=1)
        part = jnp.dot(ats[...], both, preferred_element_type=F32) * (1.0 / SEQS)
        for j in range(2):
            xb, q = info(2 * t + j)
            o = lax.rem(xb + X - x, X)
            half = part[:, j * W : (j + 1) * W]

            @pl.when(o == 0)
            def _():
                own[q] = half

            @pl.when(o == 2)
            def _():
                s2[q] = half.astype(BF16)
                relay_up(q).start()
                relay_dn(q).start()

            @pl.when(lax.rem(o, 2) == 1)
            def _():
                hold[lax.rem(t, 2), j] = half

    def finish(t):
        for j in range(2):
            xb, q = info(2 * t + j)
            o = lax.rem(xb + X - x, X)
            s = lax.rem(t, 2)

            @pl.when(o == 1)
            def _():
                relay_up(q).wait_recv()
                s1[q, pl.ds(0, 256)] = (hold[s, j, pl.ds(0, 256)] + rl[q].astype(F32)).astype(BF16)
                s1[q, pl.ds(256, 256)] = hold[s, j, pl.ds(256, 256)].astype(BF16)
                final_up(q).start()

            @pl.when(o == 3)
            def _():
                relay_dn(q).wait_recv()
                s3[q, pl.ds(0, 256)] = hold[s, j, pl.ds(0, 256)].astype(BF16)
                s3[q, pl.ds(256, 256)] = (hold[s, j, pl.ds(256, 256)] + rr[q].astype(F32)).astype(BF16)
                final_dn(q).start()

    calls = {
        "firstL": first_stay, "f1": first_near, "f23": first_far, "w23": far_left, "gram": gram,
        "pairs": pair.start, "pairw": pair_wait, "ring": ring, "ringend": ring_end, "szs": squares,
        "szw": squares_wait, "syw": norms_wait, "aw": scale, "acts": acts, "arel": act_relay,
    }

    def run(plan, src):
        for name, *args in plan:
            if name == "ru":
                receive(*args, src)
            elif name == "k":
                if src is None:
                    pl.when(is_src)(lambda: own_part(*args))
                else:
                    own_part(*args)
            else:
                calls[name](*args)

    rounds = {True: [[]], False: [[]]}
    for src, plan in ((True, SOURCE), (False, OTHER)):
        for item in plan:
            if item == ("C",):
                rounds[src].append([])
            else:
                rounds[src][-1].append(item)

    run(FIRST, None)

    @pl.when(is_src)
    def _():
        run(rounds[True][0], True)

    @pl.when(jnp.logical_not(is_src))
    def _():
        run(rounds[False][0], False)

    def round_of(t, _):
        for src in (True, False):
            for r in range(1, 8):
                if rounds[src][r]:
                    @pl.when(jnp.logical_and(t == r, is_src == src))
                    def _():
                        run(rounds[src][r], src)

        consume(t)

        @pl.when(t > 0)
        def _():
            finish(t - 1)

        return 0

    lax.fori_loop(0, 8, round_of, 0)
    finish(7)

    @pl.when(is_src)
    def _():
        wait_bytes(gbuf.at[0, :, c], kup)
        wait_bytes(gbuf.at[0, :, c], kdn)
        wait_bytes(gbuf.at[pl.ds(0, 2), :, c], zsend)

    @pl.when(jnp.logical_not(is_src))
    def _():
        wait_bytes(gbuf.at[pl.ds(0, 3), :, c], zsend)

    wait_bytes(gbuf.at[:, :, c], psend)

    @pl.when(steps_y == 0)
    def _():
        for q in range(NQ):
            first(q, 1 - c).wait_send()

    @pl.when(steps_y == 1)
    def _():
        for q in range(NQ):
            first(q, 0).wait_send()
            first(q, 1).wait_send()

    far_left(2)
    far_left(3)
    pair.wait_send()
    for i in range(1, 5):
        ring_up(i).wait_send()
    for i in range(1, 4):
        ring_dn(i).wait_send()
    wait_bytes(sz.at[pl.ds(0, 7)], szsend)
    wait_bytes(sy.at[pl.ds(0, 7)], sysend)
    wait_bytes(at.at[y], asend.at[0])
    wait_bytes(at.at[y], asend.at[1])
    wait_bytes(at.at[y], afsend)
    wait_bytes(rl, rsend.at[0])
    wait_bytes(rr, rsend.at[1])

    for q in range(NQ):
        final_up(q).wait_recv()
        final_dn(q).wait_recv()
        block = own[q] + fl[q].astype(F32) + fr[q].astype(F32)
        out_ref[pl.ds(q * W, W), :] = block.T.astype(BF16)
    wait_bytes(s1, fsend.at[0])
    wait_bytes(s3, fsend.at[1])


def local(activations, out_grads, lengths):
    dma, vmem = pltpu.SemaphoreType.DMA, pltpu.VMEM
    grams = (2, 3, 16, 128)
    scratch = [
        vmem((2, SLOT_LEN, F), BF16),
        vmem((2, SLOT_LEN, F), BF16),
        vmem((X, NQ, 2, Y, SLOT_LEN, W), BF16),
        vmem((Y, 2, F, SLOT_LEN), BF16),
        vmem((F, 2 * Y * SLOT_LEN), BF16),
        vmem((2, Z) + grams, F32),
        vmem((Z,) + grams, F32),
        vmem((Z,) + grams, F32),
        vmem((4,) + grams, F32),
        vmem((3,) + grams, F32),
        vmem((3,) + grams, F32),
        vmem((2,) + grams, F32),
        vmem((Z, 8, 128), F32),
        vmem((2 * Y, 8, 128), F32),
        vmem((2, 2, F, W), F32),
        vmem((NQ, F, W), F32),
        vmem((NQ, F, W), BF16),
        vmem((NQ, F, W), BF16),
        vmem((NQ, F, W), BF16),
        vmem((NQ, 256, W), BF16),
        vmem((NQ, 256, W), BF16),
        vmem((NQ, F, W), BF16),
        vmem((NQ, F, W), BF16),
        dma((2,)), dma((NQ, 2)), dma((NQ, Y)), dma, dma, dma, dma((X, NQ, 2)),
        dma, dma((X, NQ, 2)), dma((2,)), dma((Y, 2)), dma,
        dma, dma, dma((4,)), dma((4,)), dma((3,)), dma((3,)), dma, dma((Z,)), dma, dma((2 * Y,)),
        dma((2,)), dma((NQ,)), dma((NQ,)), dma((2,)), dma((NQ,)), dma((NQ,)),
    ]
    return pl.pallas_call(
        kernel,
        out_shape=(
            jax.ShapeDtypeStruct((F, F), BF16),
            jax.ShapeDtypeStruct((2,), F32),
        ),
        in_specs=[
            pl.BlockSpec(memory_space=pltpu.SMEM),
            pl.BlockSpec(memory_space=pl.ANY),
            pl.BlockSpec(memory_space=pl.ANY),
        ],
        out_specs=(
            pl.BlockSpec(memory_space=pltpu.VMEM),
            pl.BlockSpec(memory_space=pltpu.SMEM),
        ),
        scratch_shapes=scratch,
        compiler_params=pltpu.CompilerParams(
            collective_id=0, has_side_effects=True, vmem_limit_bytes=63 * 1024 * 1024 + 768 * 1024
        ),
        cost_estimate=pl.CostEstimate(flops=2 * 512 * 512 * 8192, bytes_accessed=3 * 2**19, transcendentals=0),
    )(lengths, activations, out_grads)


def solution(mesh):
    placed = (P("dp", None, "tensor"), P("dp", None, "tensor"), P("dp"))
    return jax.shard_map(
        local, mesh=mesh, in_specs=placed, out_specs=(P("dp", "tensor"), P("dp")), check_vma=False
    )
```

```python
import math

import jax
import jax.numpy as jnp
from jax import lax
from jax.experimental import pallas as pl
from jax.experimental.pallas import tpu as pltpu
from jax.sharding import PartitionSpec as P

D = 8192
K = 8192
SLOT_LEN = 256
SEQS = 32
X, Y, Z = 4, 4, 8
NQ = 2
W = 256
F = 512
BOUND = math.sqrt(K * D * SLOT_LEN / 2.0)
F32 = jnp.float32
BF16 = jnp.bfloat16

FIRST = (
    ("yf", 0), ("pairs",), ("yl",),
)
SOURCE = (
    ("o", 0), ("pairw",), ("o", 1), ("ring", 1), ("ring", 2), ("acts", 3), ("ring", 3), ("yf", 1), ("o", 2),
    ("ol", 0), ("ol", 1), ("ring", 4), ("o", 3), ("arel", 0), ("ringend",), ("szs",), ("r", 1, 2, 0),
    ("acts", 1), ("r", 0, 2, 0), ("szw",), ("syw",), ("arel", 1), ("r", 1, 2, 2), ("r", 0, 2, 1),
    ("r", 1, 2, 1), ("aw",), ("r", 0, 2, 2), ("C",), ("C",), ("r", 0, 2, 3), ("r", 1, 2, 3), ("C",), ("C",),
    ("r", 0, 4, 0), ("r", 1, 4, 1), ("r", 0, 4, 2), ("C",), ("C",), ("r", 1, 4, 3), ("C",), ("C",),
)
OTHER = (
    ("r", 0, 1, 0), ("r", 1, 1, 0), ("acts", 3), ("yf", 1), ("pairw",), ("ring", 1), ("ring", 2), ("ring", 3),
    ("r", 0, 1, 1), ("r", 1, 1, 1), ("acts", 1), ("ring", 4), ("ringend",), ("szs",), ("r", 1, 1, 2),
    ("arel", 0), ("szw",), ("r", 0, 1, 2), ("r", 1, 3, 0), ("r", 0, 1, 3), ("arel", 1), ("syw",),
    ("r", 1, 1, 3), ("r", 0, 3, 0), ("aw",), ("C",), ("r", 0, 3, 1), ("C",), ("r", 1, 3, 2), ("r", 1, 3, 1),
    ("r", 0, 3, 2), ("C",), ("C",), ("r", 0, 3, 3), ("r", 1, 3, 3), ("C",), ("C",), ("C",), ("C",),
)

def rcopy(src, dst, send, recv, device):
    return pltpu.make_async_remote_copy(
        src_ref=src,
        dst_ref=dst,
        send_sem=send,
        recv_sem=recv,
        device_id=device,
        device_id_type=pl.DeviceIdType.MESH,
    )


def wait_bytes(ref, sem):
    pltpu.make_async_copy(ref, ref, sem).wait()


def kernel(
    len_ref, a_hbm, g_hbm, out_ref, norm_ref,
    a_ref, g_ref, gbuf, at, ats, gpack, gpair, gsum, gup, gdn, sup, sdn, sz, sy,
    hold, own, s1, s2, s3, rl, rr, fl, fr,
    loads, ysend, yrecv, kup, kdn, zsend, zrecv, psend, precv, asend, a_up, a_dn, a_far, afsend,
    gpsend, gprecv, gupsend, guprecv, gdnsend, gdnrecv, szsend, szrecv, sysend, syrecv,
    rsend, rlrecv, rrrecv, fsend, flrecv, frrecv,
):
    dp = lax.axis_index("dp")
    tn = lax.axis_index("tensor")
    x, y = lax.div(dp, Y), lax.rem(dp, Y)
    z, c = lax.div(tn, 2), lax.rem(tn, 2)

    def dev(x_, y_, z_, c_):
        return (x_ * Y + y_, z_ * 2 + c_)

    def xs(k):
        return lax.rem(x + k, X)

    def ys(k):
        return lax.rem(y + k, Y)

    def zs(k):
        return lax.rem(z + k + Z, Z)

    partner = dev(x, y, z, 1 - c)
    z_up, z_dn = dev(x, y, zs(1), c), dev(x, y, zs(-1), c)
    x_up, x_dn = dev(xs(1), y, z, c), dev(xs(3), y, z, c)
    y_up, y_dn = dev(x, ys(1), z, c), dev(x, ys(3), z, c)
    y_others = [(ys(k), c) for k in (1, 2, 3)] + [(ys(k), 1 - c) for k in (0, 1, 2, 3)]

    load_a = pltpu.make_async_copy(a_hbm, a_ref, loads.at[0])
    load_g = pltpu.make_async_copy(g_hbm, g_ref, loads.at[1])
    load_a.start()
    load_g.start()

    barrier = pltpu.get_barrier_semaphore()
    peers = [dev(x, y2, z, c2) for y2, c2 in y_others]
    peers += [dev(x, y, zs(k), c) for k in range(1, Z)] + [x_up, x_dn]
    for peer in peers:
        pl.semaphore_signal(barrier, inc=1, device_id=peer, device_id_type=pl.DeviceIdType.MESH)
    rows = lax.broadcasted_iota(jnp.int32, (SLOT_LEN, F), 0)
    contract = (((1,), (1,)), ((), ()))
    load_a.wait()
    load_g.wait()
    for s in range(2):
        am = jnp.where(rows < len_ref[s], a_ref[s].astype(F32), 0.0)
        at[y, s] = am.T.astype(BF16)
        am = am.astype(BF16)
        g = g_ref[s]
        for m, v in enumerate((am, g)):
            full = lax.dot_general(v, v, contract, preferred_element_type=F32)
            gpack[s, :, m, 0] = full[:128, :128].reshape(Z, 16, 128)
            gpack[s, :, m, 1] = full[:128, 128:].reshape(Z, 16, 128)
            gpack[s, :, m, 2] = full[128:, 128:].reshape(Z, 16, 128)
    pl.semaphore_wait(barrier, len(peers))

    xb0 = lax.div(z, 2)
    yt = 2 * lax.rem(z, 2) + c
    is_src = lax.rem(z, 2) == lax.div(y, 2)
    steps_y = lax.rem(y - yt + Y, Y)

    def first(q, h):
        return rcopy(
            g_hbm.at[h, :, pl.ds(q * W, W)], gbuf.at[xb0, q, h, steps_y], ysend.at[q, h],
            yrecv.at[q, steps_y], dev(x, yt, z, h),
        )

    def first_steps():
        @pl.when(steps_y == 0)
        def _():
            for q in range(NQ):
                pltpu.make_async_copy(
                    g_hbm.at[c, :, pl.ds(q * W, W)], gbuf.at[xb0, q, c, 0], yrecv.at[q, 0]
                ).start()
                first(q, 1 - c).start()

        @pl.when(steps_y == 1)
        def _():
            for q in range(NQ):
                first(q, 0).start()
                first(q, 1).start()

    def first_far(q):
        @pl.when(steps_y >= 2)
        def _():
            first(q, 0).start()
            first(q, 1).start()

    pair = rcopy(gpack.at[1 - c], gpair, gpsend, gprecv, partner)

    def pair_wait():
        pair.wait_recv()
        gsum[...] = gpack[c] + gpair[...]

    def ring_up(i):
        src = gsum.at[zs(4)] if i == 1 else sup.at[i - 2]
        return rcopy(src, gup.at[i - 1], gupsend.at[i - 1], guprecv.at[i - 1], z_up)

    def ring_dn(i):
        src = gsum.at[zs(-3)] if i == 1 else sdn.at[i - 2]
        return rcopy(src, gdn.at[i - 1], gdnsend.at[i - 1], gdnrecv.at[i - 1], z_dn)

    def ring(i):
        if i > 1:
            ring_up(i - 1).wait_recv()
            sup[i - 2] = gsum[zs(5 - i)] + gup[i - 2]
        ring_up(i).start()
        if i <= 3:
            if i > 1:
                ring_dn(i - 1).wait_recv()
                sdn[i - 2] = gsum[zs(i - 4)] + gdn[i - 2]
            ring_dn(i).start()

    def ring_end():
        ring_up(4).wait_recv()
        ring_dn(3).wait_recv()
        total = gsum[z] + gup[3] + gdn[2]
        prod = total[0] * total[1]
        square = jnp.sum(prod[0] + 2.0 * prod[1] + prod[2])
        sz[z] = jnp.full((8, 128), square, F32)

    def squares():
        for k in range(1, Z):
            rcopy(sz.at[z], sz.at[z], szsend, szrecv, dev(x, y, zs(k), c)).start()

    def squares_wait():
        wait_bytes(sz.at[pl.ds(0, 7)], szrecv)
        tile = sz[0]
        for k in range(1, Z):
            tile = tile + sz[k]
        mine = y * 2 + c
        sy[mine] = tile
        for y2, c2 in y_others:
            rcopy(sy.at[mine], sy.at[mine], sysend, syrecv, dev(x, y2, z, c2)).start()

    def norms_wait():
        wait_bytes(sy.at[pl.ds(0, 7)], syrecv)

    def acts(side):
        if side == 1:
            rcopy(at.at[y], at.at[y], asend.at[0], a_dn, y_up).start()
        else:
            for h in range(2):
                rcopy(at.at[y, h], at.at[y, h], asend.at[1], a_up.at[h], y_dn).start()

    def act_relay(h):
        part = at.at[ys(1), h]
        wait_bytes(part, a_up.at[h])
        rcopy(part, part, afsend, a_far, y_dn).start()

    def scale():
        wait_bytes(at.at[ys(3)], a_dn)
        wait_bytes(at.at[ys(2)], a_far)
        for h in range(2):
            norm_ref[h] = jnp.max(jnp.sqrt(sy[y * 2 + h] + 1e-6))
        for h in range(2):
            for k in range(Y):
                factor = jnp.max(jnp.minimum(1.0, BOUND / jnp.sqrt(sy[ys(k) * 2 + h] + 1e-6)))
                scaled = (at[ys(k), h].astype(F32) * factor).astype(BF16)
                ats[:, pl.ds((h * Y + k) * SLOT_LEN, SLOT_LEN)] = scaled

    def chunk(xb, j):
        return gbuf.at[xb, :, c, j] if j < 2 else gbuf.at[xb, j - 2, c, pl.ds(2, 2)]

    def to_partner(xb, j):
        part = gbuf.at[xb, :, c, pl.ds(0, 2)] if j == 1 else chunk(xb, j)
        return rcopy(part, part, psend, precv.at[xb, j - 1], partner)

    def own_chunk(j):
        part = chunk(xb0, j)
        if j < 2:
            for q in range(NQ):
                wait_bytes(gbuf.at[xb0, q, c, j], yrecv.at[q, j])
        else:
            for k in (2, 3):
                wait_bytes(gbuf.at[xb0, j - 2, c, k], yrecv.at[j - 2, k])
        rcopy(part, part, kup.at[j], zrecv.at[xb0, j], z_up).start()
        rcopy(part, part, kdn.at[j], zrecv.at[xb0, j], z_dn).start()
        if j > 0:
            to_partner(xb0, j).start()

    def own_left(j):
        wait_bytes(chunk(xb0, j), kup.at[j])
        wait_bytes(chunk(xb0, j), kdn.at[j])

    def receive(side, d, j):
        xb = lax.div(zs(-d if side == 0 else d), 2)
        part = chunk(xb, j)
        wait_bytes(part, zrecv.at[xb, j])
        if d < 3 or (d == 3 and j % 2 == side):
            rcopy(part, part, zsend, zrecv.at[xb, j], (z_up, z_dn)[side]).start()
        if j > 0:
            to_partner(xb, j).start()

    def info(t):
        q_s = jnp.where(t < 2, t, jnp.where(t < 6, lax.div(t - 2, 2), t - 6))
        d_s = jnp.where(t < 2, 0, jnp.where(t < 6, 2, 4))
        q = jnp.where(is_src, q_s, lax.rem(lax.div(t, 2), 2))
        d = jnp.where(is_src, d_s, jnp.where(t < 4, 1, 3))
        z_from = lax.rem(jnp.where(lax.rem(t, 2) == 0, z + Z - d, z + d), Z)
        return lax.div(z_from, 2), q

    def relay_up(q):
        return rcopy(s2.at[q, pl.ds(0, 256)], rl.at[q], rsend.at[0], rlrecv.at[q], x_up)

    def relay_dn(q):
        return rcopy(s2.at[q, pl.ds(256, 256)], rr.at[q], rsend.at[1], rrrecv.at[q], x_dn)

    def final_up(q):
        return rcopy(s1.at[q], fl.at[q], fsend.at[0], flrecv.at[q], x_up)

    def final_dn(q):
        return rcopy(s3.at[q], fr.at[q], fsend.at[1], frrecv.at[q], x_dn)

    def consume(t):
        xb, q = info(t)

        @pl.when(q == 0)
        def _():
            wait_bytes(gbuf.at[xb, :, 1 - c, pl.ds(0, 2)], precv.at[xb, 0])

        wait_bytes(gbuf.at[xb, q, 1 - c, pl.ds(2, 2)], precv.at[xb, 1 + q])
        both = gbuf[xb, q].reshape(2 * Y * SLOT_LEN, W)
        part = jnp.dot(ats[...], both, preferred_element_type=F32) * (1.0 / SEQS)
        o = lax.rem(xb + X - x, X)

        @pl.when(o == 0)
        def _():
            own[q] = part

        @pl.when(o == 2)
        def _():
            s2[q] = part.astype(BF16)
            relay_up(q).start()
            relay_dn(q).start()

        @pl.when(lax.rem(o, 2) == 1)
        def _():
            hold[lax.rem(t, 2)] = part

    def finish(t):
        xb, q = info(t)
        o = lax.rem(xb + X - x, X)
        s = lax.rem(t, 2)

        @pl.when(o == 1)
        def _():
            relay_up(q).wait_recv()
            s1[q, pl.ds(0, 256)] = (hold[s, pl.ds(0, 256)] + rl[q].astype(F32)).astype(BF16)
            s1[q, pl.ds(256, 256)] = hold[s, pl.ds(256, 256)].astype(BF16)
            final_up(q).start()

        @pl.when(o == 3)
        def _():
            relay_dn(q).wait_recv()
            s3[q, pl.ds(0, 256)] = hold[s, pl.ds(0, 256)].astype(BF16)
            s3[q, pl.ds(256, 256)] = (hold[s, pl.ds(256, 256)] + rr[q].astype(F32)).astype(BF16)
            final_dn(q).start()

    calls = {
        "yl": first_steps, "yf": first_far, "o": own_chunk, "ol": own_left,
        "pairs": pair.start, "pairw": pair_wait, "ring": ring, "ringend": ring_end, "szs": squares,
        "szw": squares_wait, "syw": norms_wait, "aw": scale, "acts": acts, "arel": act_relay,
    }

    def run(plan):
        for name, *args in plan:
            if name == "r":
                receive(*args)
            else:
                calls[name](*args)

    rounds = {True: [[]], False: [[]]}
    for src, plan in ((True, SOURCE), (False, OTHER)):
        for item in plan:
            if item == ("C",):
                rounds[src].append([])
            else:
                rounds[src][-1].append(item)

    run(FIRST)

    @pl.when(is_src)
    def _():
        run(rounds[True][0])

    @pl.when(jnp.logical_not(is_src))
    def _():
        run(rounds[False][0])

    def round_of(t, _):
        for src in (True, False):
            for r in range(1, 8):
                if rounds[src][r]:
                    @pl.when(jnp.logical_and(t == r, is_src == src))
                    def _():
                        run(rounds[src][r])

        consume(t)

        @pl.when(t > 0)
        def _():
            finish(t - 1)

        return 0

    lax.fori_loop(0, 8, round_of, 0)
    finish(7)

    @pl.when(is_src)
    def _():
        for j in range(4):
            if ("ol", j) not in SOURCE:
                own_left(j)
        wait_bytes(gbuf.at[pl.ds(0, 2), :, c], zsend)

    @pl.when(jnp.logical_not(is_src))
    def _():
        wait_bytes(gbuf.at[pl.ds(0, 3), :, c], zsend)

    wait_bytes(gbuf.at[:, :, c], psend)

    @pl.when(steps_y == 0)
    def _():
        for q in range(NQ):
            first(q, 1 - c).wait_send()

    @pl.when(steps_y >= 1)
    def _():
        for q in range(NQ):
            first(q, 0).wait_send()
            first(q, 1).wait_send()

    pair.wait_send()
    for i in range(1, 5):
        ring_up(i).wait_send()
    for i in range(1, 4):
        ring_dn(i).wait_send()
    wait_bytes(sz.at[pl.ds(0, 7)], szsend)
    wait_bytes(sy.at[pl.ds(0, 7)], sysend)
    wait_bytes(at.at[y], asend.at[0])
    wait_bytes(at.at[y], asend.at[1])
    wait_bytes(at.at[y], afsend)
    wait_bytes(rl, rsend.at[0])
    wait_bytes(rr, rsend.at[1])

    for q in range(NQ):
        final_up(q).wait_recv()
        final_dn(q).wait_recv()
        block = own[q] + fl[q].astype(F32) + fr[q].astype(F32)
        out_ref[pl.ds(q * W, W), :] = block.T.astype(BF16)
    wait_bytes(s1, fsend.at[0])
    wait_bytes(s3, fsend.at[1])


def local(activations, out_grads, lengths):
    dma, vmem = pltpu.SemaphoreType.DMA, pltpu.VMEM
    grams = (2, 3, 16, 128)
    scratch = [
        vmem((2, SLOT_LEN, F), BF16),
        vmem((2, SLOT_LEN, F), BF16),
        vmem((X, NQ, 2, Y, SLOT_LEN, W), BF16),
        vmem((Y, 2, F, SLOT_LEN), BF16),
        vmem((F, 2 * Y * SLOT_LEN), BF16),
        vmem((2, Z) + grams, F32),
        vmem((Z,) + grams, F32),
        vmem((Z,) + grams, F32),
        vmem((4,) + grams, F32),
        vmem((3,) + grams, F32),
        vmem((3,) + grams, F32),
        vmem((2,) + grams, F32),
        vmem((Z, 8, 128), F32),
        vmem((2 * Y, 8, 128), F32),
        vmem((2, F, W), F32),
        vmem((NQ, F, W), F32),
        vmem((NQ, F, W), BF16),
        vmem((NQ, F, W), BF16),
        vmem((NQ, F, W), BF16),
        vmem((NQ, 256, W), BF16),
        vmem((NQ, 256, W), BF16),
        vmem((NQ, F, W), BF16),
        vmem((NQ, F, W), BF16),
        dma((2,)), dma((NQ, 2)), dma((NQ, Y)), dma((4,)), dma((4,)), dma, dma((X, 4)),
        dma, dma((X, 3)), dma((2,)), dma((2,)), dma, dma, dma,
        dma, dma, dma((4,)), dma((4,)), dma((3,)), dma((3,)), dma, dma, dma, dma,
        dma((2,)), dma((NQ,)), dma((NQ,)), dma((2,)), dma((NQ,)), dma((NQ,)),
    ]
    return pl.pallas_call(
        kernel,
        out_shape=(
            jax.ShapeDtypeStruct((F, F), BF16),
            jax.ShapeDtypeStruct((2,), F32),
        ),
        in_specs=[
            pl.BlockSpec(memory_space=pltpu.SMEM),
            pl.BlockSpec(memory_space=pl.ANY),
            pl.BlockSpec(memory_space=pl.ANY),
        ],
        out_specs=(
            pl.BlockSpec(memory_space=pltpu.VMEM),
            pl.BlockSpec(memory_space=pltpu.SMEM),
        ),
        scratch_shapes=scratch,
        compiler_params=pltpu.CompilerParams(
            collective_id=0, has_side_effects=True, vmem_limit_bytes=63 * 1024 * 1024 + 768 * 1024
        ),
        cost_estimate=pl.CostEstimate(flops=2 * 512 * 512 * 8192, bytes_accessed=3 * 2**19, transcendentals=0),
    )(lengths, activations, out_grads)


def solution(mesh):
    placed = (P("dp", None, "tensor"), P("dp", None, "tensor"), P("dp"))
    return jax.shard_map(
        local, mesh=mesh, in_specs=placed, out_specs=(P("dp", "tensor"), P("dp")), check_vma=False
    )
```

```python
import math

import jax
import jax.numpy as jnp
from jax import lax
from jax.experimental import pallas as pl
from jax.experimental.pallas import tpu as pltpu
from jax.sharding import PartitionSpec as P

D = 8192
K = 8192
SLOT_LEN = 256
SEQS = 32
X, Y, Z = 4, 4, 8
NQ = 2
W = 256
F = 512
BOUND = math.sqrt(K * D * SLOT_LEN / 2.0)
F32 = jnp.float32
BF16 = jnp.bfloat16

FIRST = (
    ("pairs",), ("yl",), ("yf", 0),
)
SOURCE = (
    ("o", 0), ("pairw",), ("ring", 1), ("yf", 1), ("ring", 2), ("o", 1), ("ring", 3), ("acts", 3),
    ("acts", 1), ("ring", 4), ("o", 2), ("ringend",), ("szs",), ("o", 3), ("r", 1, 2, 0), ("r", 0, 2, 0),
    ("arel", 0), ("arel", 1), ("szw",), ("r", 0, 2, 1), ("r", 1, 2, 1), ("syw",), ("aw",), ("r", 1, 2, 2),
    ("C",), ("r", 0, 2, 2), ("C",), ("r", 1, 2, 3), ("C",), ("r", 0, 2, 3), ("C",), ("C",), ("C",),
    ("r", 0, 4, 0), ("r", 1, 4, 1), ("r", 0, 4, 2), ("C",), ("r", 1, 4, 3), ("C",),
)
OTHER = (
    ("pairw",), ("ring", 1), ("yf", 1), ("ring", 2), ("ring", 3), ("acts", 3), ("r", 0, 1, 0), ("r", 1, 1, 0),
    ("acts", 1), ("ring", 4), ("ringend",), ("szs",), ("r", 1, 1, 1), ("r", 0, 1, 1), ("arel", 0),
    ("arel", 1), ("szw",), ("r", 1, 1, 2), ("r", 0, 1, 2), ("r", 1, 1, 3), ("r", 0, 1, 3), ("syw",), ("aw",),
    ("C",), ("r", 1, 3, 0), ("C",), ("r", 0, 3, 0), ("C",), ("C",), ("r", 1, 3, 1), ("r", 0, 3, 1),
    ("r", 1, 3, 2), ("r", 0, 3, 2), ("C",), ("r", 1, 3, 3), ("r", 0, 3, 3), ("C",), ("C",), ("C",),
)

def rcopy(src, dst, send, recv, device):
    return pltpu.make_async_remote_copy(
        src_ref=src,
        dst_ref=dst,
        send_sem=send,
        recv_sem=recv,
        device_id=device,
        device_id_type=pl.DeviceIdType.MESH,
    )


def wait_bytes(ref, sem):
    pltpu.make_async_copy(ref, ref, sem).wait()


def kernel(
    len_ref, a_hbm, g_hbm, out_ref, norm_ref,
    a_ref, g_ref, gbuf, at, ats, gpack, gpair, gsum, gup, gdn, sup, sdn, sz, sy,
    hold, own, s1, s2, s3, rl, rr, fl, fr,
    loads, ysend, yrecv, kup, kdn, zsend, zrecv, psend, precv, asend, a_up, a_dn, a_far, afsend,
    gpsend, gprecv, gupsend, guprecv, gdnsend, gdnrecv, szsend, szrecv, sysend, syrecv,
    rsend, rlrecv, rrrecv, fsend, flrecv, frrecv,
):
    dp = lax.axis_index("dp")
    tn = lax.axis_index("tensor")
    x, y = lax.div(dp, Y), lax.rem(dp, Y)
    z, c = lax.div(tn, 2), lax.rem(tn, 2)

    def dev(x_, y_, z_, c_):
        return (x_ * Y + y_, z_ * 2 + c_)

    def xs(k):
        return lax.rem(x + k, X)

    def ys(k):
        return lax.rem(y + k, Y)

    def zs(k):
        return lax.rem(z + k + Z, Z)

    partner = dev(x, y, z, 1 - c)
    z_up, z_dn = dev(x, y, zs(1), c), dev(x, y, zs(-1), c)
    x_up, x_dn = dev(xs(1), y, z, c), dev(xs(3), y, z, c)
    y_up, y_dn = dev(x, ys(1), z, c), dev(x, ys(3), z, c)
    y_others = [(ys(k), c) for k in (1, 2, 3)] + [(ys(k), 1 - c) for k in (0, 1, 2, 3)]

    load_a = pltpu.make_async_copy(a_hbm, a_ref, loads.at[0])
    load_g = pltpu.make_async_copy(g_hbm, g_ref, loads.at[1])
    load_a.start()
    load_g.start()

    barrier = pltpu.get_barrier_semaphore()
    peers = [dev(x, y2, z, c2) for y2, c2 in y_others]
    peers += [dev(x, y, zs(k), c) for k in range(1, Z)] + [x_up, x_dn]
    for peer in peers:
        pl.semaphore_signal(barrier, inc=1, device_id=peer, device_id_type=pl.DeviceIdType.MESH)
    rows = lax.broadcasted_iota(jnp.int32, (SLOT_LEN, F), 0)
    contract = (((1,), (1,)), ((), ()))
    load_a.wait()
    load_g.wait()
    for s in range(2):
        am = jnp.where(rows < len_ref[s], a_ref[s].astype(F32), 0.0)
        at[y, s] = am.T.astype(BF16)
        am = am.astype(BF16)
        g = g_ref[s]
        for m, v in enumerate((am, g)):
            full = lax.dot_general(v, v, contract, preferred_element_type=F32)
            gpack[s, :, m, 0] = full[:128, :128].reshape(Z, 16, 128)
            gpack[s, :, m, 1] = full[:128, 128:].reshape(Z, 16, 128)
            gpack[s, :, m, 2] = full[128:, 128:].reshape(Z, 16, 128)
    pl.semaphore_wait(barrier, len(peers))

    xb0 = lax.div(z, 2)
    yt = 2 * lax.rem(z, 2) + c
    is_src = lax.rem(z, 2) == lax.div(y, 2)
    steps_y = lax.rem(y - yt + Y, Y)

    def first(q, h):
        return rcopy(
            g_hbm.at[h, :, pl.ds(q * W, W)], gbuf.at[xb0, q, h, steps_y], ysend.at[q, h],
            yrecv.at[q, steps_y], dev(x, yt, z, h),
        )

    def first_steps():
        @pl.when(steps_y == 0)
        def _():
            for q in range(NQ):
                pltpu.make_async_copy(
                    g_hbm.at[c, :, pl.ds(q * W, W)], gbuf.at[xb0, q, c, 0], yrecv.at[q, 0]
                ).start()
                first(q, 1 - c).start()

        @pl.when(steps_y == 1)
        def _():
            for q in range(NQ):
                first(q, 0).start()
                first(q, 1).start()

    def first_far(q):
        @pl.when(steps_y >= 2)
        def _():
            first(q, 0).start()
            first(q, 1).start()

    pair = rcopy(gpack.at[1 - c], gpair, gpsend, gprecv, partner)

    def pair_wait():
        pair.wait_recv()
        gsum[...] = gpack[c] + gpair[...]

    def ring_up(i):
        src = gsum.at[zs(4)] if i == 1 else sup.at[i - 2]
        return rcopy(src, gup.at[i - 1], gupsend.at[i - 1], guprecv.at[i - 1], z_up)

    def ring_dn(i):
        src = gsum.at[zs(-3)] if i == 1 else sdn.at[i - 2]
        return rcopy(src, gdn.at[i - 1], gdnsend.at[i - 1], gdnrecv.at[i - 1], z_dn)

    def ring(i):
        if i > 1:
            ring_up(i - 1).wait_recv()
            sup[i - 2] = gsum[zs(5 - i)] + gup[i - 2]
        ring_up(i).start()
        if i <= 3:
            if i > 1:
                ring_dn(i - 1).wait_recv()
                sdn[i - 2] = gsum[zs(i - 4)] + gdn[i - 2]
            ring_dn(i).start()

    def ring_end():
        ring_up(4).wait_recv()
        ring_dn(3).wait_recv()
        total = gsum[z] + gup[3] + gdn[2]
        prod = total[0] * total[1]
        square = jnp.sum(prod[0] + 2.0 * prod[1] + prod[2])
        sz[z] = jnp.full((8, 128), square, F32)

    def squares():
        for k in range(1, Z):
            rcopy(sz.at[z], sz.at[z], szsend, szrecv, dev(x, y, zs(k), c)).start()

    def squares_wait():
        wait_bytes(sz.at[pl.ds(0, 7)], szrecv)
        tile = sz[0]
        for k in range(1, Z):
            tile = tile + sz[k]
        mine = y * 2 + c
        sy[mine] = tile
        for y2, c2 in y_others:
            rcopy(sy.at[mine], sy.at[mine], sysend, syrecv, dev(x, y2, z, c2)).start()

    def norms_wait():
        wait_bytes(sy.at[pl.ds(0, 7)], syrecv)

    def acts(side):
        if side == 1:
            rcopy(at.at[y], at.at[y], asend.at[0], a_dn, y_up).start()
        else:
            for h in range(2):
                rcopy(at.at[y, h], at.at[y, h], asend.at[1], a_up.at[h], y_dn).start()

    def act_relay(h):
        part = at.at[ys(1), h]
        wait_bytes(part, a_up.at[h])
        rcopy(part, part, afsend, a_far, y_dn).start()

    def scale():
        wait_bytes(at.at[ys(3)], a_dn)
        wait_bytes(at.at[ys(2)], a_far)
        for h in range(2):
            norm_ref[h] = jnp.max(jnp.sqrt(sy[y * 2 + h] + 1e-6))
        for h in range(2):
            for k in range(Y):
                factor = jnp.max(jnp.minimum(1.0, BOUND / jnp.sqrt(sy[ys(k) * 2 + h] + 1e-6)))
                scaled = (at[ys(k), h].astype(F32) * factor).astype(BF16)
                ats[:, pl.ds((h * Y + k) * SLOT_LEN, SLOT_LEN)] = scaled

    def chunk(xb, j):
        return gbuf.at[xb, :, c, j] if j < 2 else gbuf.at[xb, j - 2, c, pl.ds(2, 2)]

    def to_partner(xb, j):
        part = gbuf.at[xb, :, c, pl.ds(0, 2)] if j == 1 else chunk(xb, j)
        return rcopy(part, part, psend, precv.at[xb, j - 1], partner)

    def own_chunk(j):
        part = chunk(xb0, j)
        if j < 2:
            for q in range(NQ):
                wait_bytes(gbuf.at[xb0, q, c, j], yrecv.at[q, j])
        else:
            for k in (2, 3):
                wait_bytes(gbuf.at[xb0, j - 2, c, k], yrecv.at[j - 2, k])
        rcopy(part, part, kup.at[j], zrecv.at[xb0, j], z_up).start()
        rcopy(part, part, kdn.at[j], zrecv.at[xb0, j], z_dn).start()
        if j > 0:
            to_partner(xb0, j).start()

    def own_left(j):
        wait_bytes(chunk(xb0, j), kup.at[j])
        wait_bytes(chunk(xb0, j), kdn.at[j])

    def receive(side, d, j):
        xb = lax.div(zs(-d if side == 0 else d), 2)
        part = chunk(xb, j)
        wait_bytes(part, zrecv.at[xb, j])
        if d < 3 or (d == 3 and j % 2 == side):
            rcopy(part, part, zsend, zrecv.at[xb, j], (z_up, z_dn)[side]).start()
        if j > 0:
            to_partner(xb, j).start()

    def info(t):
        q_s = jnp.where(t < 2, t, jnp.where(t < 6, lax.div(t - 2, 2), t - 6))
        d_s = jnp.where(t < 2, 0, jnp.where(t < 6, 2, 4))
        q = jnp.where(is_src, q_s, lax.rem(lax.div(t, 2), 2))
        d = jnp.where(is_src, d_s, jnp.where(t < 4, 1, 3))
        z_from = lax.rem(jnp.where(lax.rem(t, 2) == 0, z + Z - d, z + d), Z)
        return lax.div(z_from, 2), q

    def relay_up(q):
        return rcopy(s2.at[q, pl.ds(0, 256)], rl.at[q], rsend.at[0], rlrecv.at[q], x_up)

    def relay_dn(q):
        return rcopy(s2.at[q, pl.ds(256, 256)], rr.at[q], rsend.at[1], rrrecv.at[q], x_dn)

    def final_up(q):
        return rcopy(s1.at[q], fl.at[q], fsend.at[0], flrecv.at[q], x_up)

    def final_dn(q):
        return rcopy(s3.at[q], fr.at[q], fsend.at[1], frrecv.at[q], x_dn)

    def consume(t):
        xb, q = info(t)

        @pl.when(q == 0)
        def _():
            wait_bytes(gbuf.at[xb, :, 1 - c, pl.ds(0, 2)], precv.at[xb, 0])

        wait_bytes(gbuf.at[xb, q, 1 - c, pl.ds(2, 2)], precv.at[xb, 1 + q])
        both = gbuf[xb, q].reshape(2 * Y * SLOT_LEN, W)
        part = jnp.dot(ats[...], both, preferred_element_type=F32) * (1.0 / SEQS)
        o = lax.rem(xb + X - x, X)

        @pl.when(o == 0)
        def _():
            own[q] = part

        @pl.when(o == 2)
        def _():
            s2[q] = part.astype(BF16)
            relay_up(q).start()
            relay_dn(q).start()

        @pl.when(lax.rem(o, 2) == 1)
        def _():
            hold[lax.rem(t, 2)] = part

    def finish(t):
        xb, q = info(t)
        o = lax.rem(xb + X - x, X)
        s = lax.rem(t, 2)

        @pl.when(o == 1)
        def _():
            relay_up(q).wait_recv()
            s1[q, pl.ds(0, 256)] = (hold[s, pl.ds(0, 256)] + rl[q].astype(F32)).astype(BF16)
            s1[q, pl.ds(256, 256)] = hold[s, pl.ds(256, 256)].astype(BF16)
            final_up(q).start()

        @pl.when(o == 3)
        def _():
            relay_dn(q).wait_recv()
            s3[q, pl.ds(0, 256)] = hold[s, pl.ds(0, 256)].astype(BF16)
            s3[q, pl.ds(256, 256)] = (hold[s, pl.ds(256, 256)] + rr[q].astype(F32)).astype(BF16)
            final_dn(q).start()

    calls = {
        "yl": first_steps, "yf": first_far, "o": own_chunk, "ol": own_left,
        "pairs": pair.start, "pairw": pair_wait, "ring": ring, "ringend": ring_end, "szs": squares,
        "szw": squares_wait, "syw": norms_wait, "aw": scale, "acts": acts, "arel": act_relay,
    }

    def run(plan):
        for name, *args in plan:
            if name == "r":
                receive(*args)
            else:
                calls[name](*args)

    rounds = {True: [[]], False: [[]]}
    for src, plan in ((True, SOURCE), (False, OTHER)):
        for item in plan:
            if item == ("C",):
                rounds[src].append([])
            else:
                rounds[src][-1].append(item)

    run(FIRST)

    @pl.when(is_src)
    def _():
        run(rounds[True][0])

    @pl.when(jnp.logical_not(is_src))
    def _():
        run(rounds[False][0])

    def round_of(t, _):
        for src in (True, False):
            for r in range(1, 8):
                if rounds[src][r]:
                    @pl.when(jnp.logical_and(t == r, is_src == src))
                    def _():
                        run(rounds[src][r])

        consume(t)

        @pl.when(t > 0)
        def _():
            finish(t - 1)

        return 0

    lax.fori_loop(0, 8, round_of, 0)
    finish(7)

    @pl.when(is_src)
    def _():
        for j in range(4):
            if ("ol", j) not in SOURCE:
                own_left(j)
        wait_bytes(gbuf.at[pl.ds(0, 2), :, c], zsend)

    @pl.when(jnp.logical_not(is_src))
    def _():
        wait_bytes(gbuf.at[pl.ds(0, 3), :, c], zsend)

    wait_bytes(gbuf.at[:, :, c], psend)

    @pl.when(steps_y == 0)
    def _():
        for q in range(NQ):
            first(q, 1 - c).wait_send()

    @pl.when(steps_y >= 1)
    def _():
        for q in range(NQ):
            first(q, 0).wait_send()
            first(q, 1).wait_send()

    pair.wait_send()
    for i in range(1, 5):
        ring_up(i).wait_send()
    for i in range(1, 4):
        ring_dn(i).wait_send()
    wait_bytes(sz.at[pl.ds(0, 7)], szsend)
    wait_bytes(sy.at[pl.ds(0, 7)], sysend)
    wait_bytes(at.at[y], asend.at[0])
    wait_bytes(at.at[y], asend.at[1])
    wait_bytes(at.at[y], afsend)
    wait_bytes(rl, rsend.at[0])
    wait_bytes(rr, rsend.at[1])

    for q in range(NQ):
        final_up(q).wait_recv()
        final_dn(q).wait_recv()
        block = own[q] + fl[q].astype(F32) + fr[q].astype(F32)
        out_ref[pl.ds(q * W, W), :] = block.T.astype(BF16)
    wait_bytes(s1, fsend.at[0])
    wait_bytes(s3, fsend.at[1])


def local(activations, out_grads, lengths):
    dma, vmem = pltpu.SemaphoreType.DMA, pltpu.VMEM
    grams = (2, 3, 16, 128)
    scratch = [
        vmem((2, SLOT_LEN, F), BF16),
        vmem((2, SLOT_LEN, F), BF16),
        vmem((X, NQ, 2, Y, SLOT_LEN, W), BF16),
        vmem((Y, 2, F, SLOT_LEN), BF16),
        vmem((F, 2 * Y * SLOT_LEN), BF16),
        vmem((2, Z) + grams, F32),
        vmem((Z,) + grams, F32),
        vmem((Z,) + grams, F32),
        vmem((4,) + grams, F32),
        vmem((3,) + grams, F32),
        vmem((3,) + grams, F32),
        vmem((2,) + grams, F32),
        vmem((Z, 8, 128), F32),
        vmem((2 * Y, 8, 128), F32),
        vmem((2, F, W), F32),
        vmem((NQ, F, W), F32),
        vmem((NQ, F, W), BF16),
        vmem((NQ, F, W), BF16),
        vmem((NQ, F, W), BF16),
        vmem((NQ, 256, W), BF16),
        vmem((NQ, 256, W), BF16),
        vmem((NQ, F, W), BF16),
        vmem((NQ, F, W), BF16),
        dma((2,)), dma((NQ, 2)), dma((NQ, Y)), dma((4,)), dma((4,)), dma, dma((X, 4)),
        dma, dma((X, 3)), dma((2,)), dma((2,)), dma, dma, dma,
        dma, dma, dma((4,)), dma((4,)), dma((3,)), dma((3,)), dma, dma, dma, dma,
        dma((2,)), dma((NQ,)), dma((NQ,)), dma((2,)), dma((NQ,)), dma((NQ,)),
    ]
    return pl.pallas_call(
        kernel,
        out_shape=(
            jax.ShapeDtypeStruct((F, F), BF16),
            jax.ShapeDtypeStruct((2,), F32),
        ),
        in_specs=[
            pl.BlockSpec(memory_space=pltpu.SMEM),
            pl.BlockSpec(memory_space=pl.ANY),
            pl.BlockSpec(memory_space=pl.ANY),
        ],
        out_specs=(
            pl.BlockSpec(memory_space=pltpu.VMEM),
            pl.BlockSpec(memory_space=pltpu.SMEM),
        ),
        scratch_shapes=scratch,
        compiler_params=pltpu.CompilerParams(
            collective_id=0, has_side_effects=True, vmem_limit_bytes=63 * 1024 * 1024 + 768 * 1024
        ),
        cost_estimate=pl.CostEstimate(flops=2 * 512 * 512 * 8192, bytes_accessed=3 * 2**19, transcendentals=0),
    )(lengths, activations, out_grads)


def solution(mesh):
    placed = (P("dp", None, "tensor"), P("dp", None, "tensor"), P("dp"))
    return jax.shard_map(
        local, mesh=mesh, in_specs=placed, out_specs=(P("dp", "tensor"), P("dp")), check_vma=False
    )
```

```python
import math

import jax
import jax.numpy as jnp
from jax import lax
from jax.experimental import pallas as pl
from jax.experimental.pallas import tpu as pltpu
from jax.sharding import PartitionSpec as P

D = 8192
K = 8192
SLOT_LEN = 256
SEQS = 32
X, Y, Z = 4, 4, 8
NQ = 2
W = 256
F = 512
BOUND = math.sqrt(K * D * SLOT_LEN / 2.0)
F32 = jnp.float32
BF16 = jnp.bfloat16

FIRST = (
    ("pairs",), ("yl",), ("yf", 0),
)
SOURCE = (
    ("o", 0), ("pairw",), ("ring", 1), ("yf", 1), ("ring", 2), ("o", 1), ("ring", 3), ("acts", 3),
    ("acts", 1), ("ring", 4), ("o", 2), ("ringend",), ("szs",), ("o", 3), ("r", 1, 2, 0), ("r", 0, 2, 0),
    ("arel", 0), ("arel", 1), ("szw",), ("r", 0, 2, 1), ("r", 1, 2, 1), ("syw",), ("aw",), ("r", 1, 2, 2),
    ("C",), ("r", 0, 2, 2), ("C",), ("r", 1, 2, 3), ("C",), ("r", 0, 2, 3), ("C",), ("C",), ("C",),
    ("r", 0, 4, 0), ("r", 1, 4, 1), ("r", 0, 4, 2), ("C",), ("r", 1, 4, 3), ("C",),
)
OTHER = (
    ("pairw",), ("ring", 1), ("yf", 1), ("ring", 2), ("ring", 3), ("acts", 3), ("r", 0, 1, 0), ("r", 1, 1, 0),
    ("acts", 1), ("ring", 4), ("ringend",), ("szs",), ("r", 1, 1, 1), ("r", 0, 1, 1), ("arel", 0),
    ("arel", 1), ("szw",), ("r", 1, 1, 2), ("r", 0, 1, 2), ("r", 1, 1, 3), ("r", 0, 1, 3), ("syw",), ("aw",),
    ("C",), ("r", 1, 3, 0), ("C",), ("r", 0, 3, 0), ("C",), ("C",), ("r", 1, 3, 1), ("r", 0, 3, 1),
    ("r", 1, 3, 2), ("r", 0, 3, 2), ("C",), ("r", 1, 3, 3), ("r", 0, 3, 3), ("C",), ("C",), ("C",),
)

def rcopy(src, dst, send, recv, device):
    return pltpu.make_async_remote_copy(
        src_ref=src,
        dst_ref=dst,
        send_sem=send,
        recv_sem=recv,
        device_id=device,
        device_id_type=pl.DeviceIdType.MESH,
    )


def wait_bytes(ref, sem):
    pltpu.make_async_copy(ref, ref, sem).wait()


def kernel(
    len_ref, a_hbm, g_hbm, out_ref, norm_ref,
    a_ref, g_ref, gbuf, at, ats, gpack, gpair, gsum, gup, gdn, sup, sdn, sz, sy,
    hold, own, s1, s2, s3, rl, rr, fl, fr,
    loads, ysend, yrecv, kup, kdn, zsend, zrecv, psend, precv, asend, a_up, a_dn, a_far, afsend,
    gpsend, gprecv, gupsend, guprecv, gdnsend, gdnrecv, szsend, szrecv, sysend, syrecv,
    rsend, rlrecv, rrrecv, fsend, flrecv, frrecv,
):
    dp = lax.axis_index("dp")
    tn = lax.axis_index("tensor")
    x, y = lax.div(dp, Y), lax.rem(dp, Y)
    z, c = lax.div(tn, 2), lax.rem(tn, 2)

    def dev(x_, y_, z_, c_):
        return (x_ * Y + y_, z_ * 2 + c_)

    def xs(k):
        return lax.rem(x + k, X)

    def ys(k):
        return lax.rem(y + k, Y)

    def zs(k):
        return lax.rem(z + k + Z, Z)

    partner = dev(x, y, z, 1 - c)
    z_up, z_dn = dev(x, y, zs(1), c), dev(x, y, zs(-1), c)
    x_up, x_dn = dev(xs(1), y, z, c), dev(xs(3), y, z, c)
    y_up, y_dn = dev(x, ys(1), z, c), dev(x, ys(3), z, c)
    y_others = [(ys(k), c) for k in (1, 2, 3)] + [(ys(k), 1 - c) for k in (0, 1, 2, 3)]

    load_a = pltpu.make_async_copy(a_hbm, a_ref, loads.at[0])
    load_g = pltpu.make_async_copy(g_hbm, g_ref, loads.at[1])
    load_a.start()
    load_g.start()

    barrier = pltpu.get_barrier_semaphore()
    peers = [dev(x, y2, z, c2) for y2, c2 in y_others]
    peers += [dev(x, y, zs(k), c) for k in range(1, Z)] + [x_up, x_dn]
    for peer in peers:
        pl.semaphore_signal(barrier, inc=1, device_id=peer, device_id_type=pl.DeviceIdType.MESH)
    rows = lax.broadcasted_iota(jnp.int32, (SLOT_LEN, F), 0)
    contract = (((1,), (1,)), ((), ()))
    load_a.wait()
    load_g.wait()
    for s in range(2):
        am = jnp.where(rows < len_ref[s], a_ref[s].astype(F32), 0.0)
        at[y, s] = am.T.astype(BF16)
        am = am.astype(BF16)
        g = g_ref[s]
        for m, v in enumerate((am, g)):
            full = lax.dot_general(v, v, contract, preferred_element_type=F32)
            gpack[s, :, m, 0] = full[:128, :128].reshape(Z, 16, 128)
            gpack[s, :, m, 1] = full[:128, 128:].reshape(Z, 16, 128)
            gpack[s, :, m, 2] = full[128:, 128:].reshape(Z, 16, 128)
    pl.semaphore_wait(barrier, len(peers))

    xb0 = lax.div(z, 2)
    yt = 2 * lax.rem(z, 2) + c
    is_src = lax.rem(z, 2) == lax.div(y, 2)
    steps_y = lax.rem(y - yt + Y, Y)

    def first(q, h):
        return rcopy(
            g_hbm.at[h, :, pl.ds(q * W, W)], gbuf.at[xb0, q, h, steps_y], ysend.at[q, h],
            yrecv.at[q, steps_y], dev(x, yt, z, h),
        )

    def first_steps():
        @pl.when(steps_y == 0)
        def _():
            for q in range(NQ):
                pltpu.make_async_copy(
                    g_hbm.at[c, :, pl.ds(q * W, W)], gbuf.at[xb0, q, c, 0], yrecv.at[q, 0]
                ).start()
                first(q, 1 - c).start()

        @pl.when(steps_y == 1)
        def _():
            for q in range(NQ):
                first(q, 0).start()
                first(q, 1).start()

    def first_far(q):
        @pl.when(steps_y >= 2)
        def _():
            first(q, 0).start()
            first(q, 1).start()

    pair = rcopy(gpack.at[1 - c], gpair, gpsend, gprecv, partner)

    def pair_wait():
        pair.wait_recv()
        gsum[...] = gpack[c] + gpair[...]

    def ring_up(i):
        src = gsum.at[zs(4)] if i == 1 else sup.at[i - 2]
        return rcopy(src, gup.at[i - 1], gupsend.at[i - 1], guprecv.at[i - 1], z_up)

    def ring_dn(i):
        src = gsum.at[zs(-3)] if i == 1 else sdn.at[i - 2]
        return rcopy(src, gdn.at[i - 1], gdnsend.at[i - 1], gdnrecv.at[i - 1], z_dn)

    def ring(i):
        if i > 1:
            ring_up(i - 1).wait_recv()
            sup[i - 2] = gsum[zs(5 - i)] + gup[i - 2]
        ring_up(i).start()
        if i <= 3:
            if i > 1:
                ring_dn(i - 1).wait_recv()
                sdn[i - 2] = gsum[zs(i - 4)] + gdn[i - 2]
            ring_dn(i).start()

    def ring_end():
        ring_up(4).wait_recv()
        ring_dn(3).wait_recv()
        total = gsum[z] + gup[3] + gdn[2]
        prod = total[0] * total[1]
        square = jnp.sum(prod[0] + 2.0 * prod[1] + prod[2])
        sz[z] = jnp.full((8, 128), square, F32)

    def squares():
        for k in range(1, Z):
            rcopy(sz.at[z], sz.at[z], szsend, szrecv, dev(x, y, zs(k), c)).start()

    def squares_wait():
        wait_bytes(sz.at[pl.ds(0, 7)], szrecv)
        tile = sz[0]
        for k in range(1, Z):
            tile = tile + sz[k]
        mine = y * 2 + c
        sy[mine] = tile
        for y2, c2 in y_others:
            rcopy(sy.at[mine], sy.at[mine], sysend, syrecv, dev(x, y2, z, c2)).start()

    def norms_wait():
        wait_bytes(sy.at[pl.ds(0, 7)], syrecv)

    def acts(side):
        if side == 1:
            rcopy(at.at[y], at.at[y], asend.at[0], a_dn, y_up).start()
        else:
            for h in range(2):
                rcopy(at.at[y, h], at.at[y, h], asend.at[1], a_up.at[h], y_dn).start()

    def act_relay(h):
        part = at.at[ys(1), h]
        wait_bytes(part, a_up.at[h])
        rcopy(part, part, afsend, a_far, y_dn).start()

    def scale():
        wait_bytes(at.at[ys(3)], a_dn)
        wait_bytes(at.at[ys(2)], a_far)
        for h in range(2):
            norm_ref[h] = jnp.max(jnp.sqrt(sy[y * 2 + h] + 1e-6))
        for h in range(2):
            for k in range(Y):
                factor = jnp.max(jnp.minimum(1.0, BOUND / jnp.sqrt(sy[ys(k) * 2 + h] + 1e-6)))
                scaled = (at[ys(k), h].astype(F32) * factor).astype(BF16)
                ats[:, pl.ds((h * Y + k) * SLOT_LEN, SLOT_LEN)] = scaled

    def chunk(xb, j):
        return gbuf.at[xb, :, c, j] if j < 2 else gbuf.at[xb, j - 2, c, pl.ds(2, 2)]

    def to_partner(xb, j):
        part = gbuf.at[xb, :, c, pl.ds(0, 2)] if j == 1 else chunk(xb, j)
        return rcopy(part, part, psend, precv.at[xb, j - 1], partner)

    def own_chunk(j):
        part = chunk(xb0, j)
        if j < 2:
            for q in range(NQ):
                wait_bytes(gbuf.at[xb0, q, c, j], yrecv.at[q, j])
        else:
            for k in (2, 3):
                wait_bytes(gbuf.at[xb0, j - 2, c, k], yrecv.at[j - 2, k])
        rcopy(part, part, kup.at[j], zrecv.at[xb0, j], z_up).start()
        rcopy(part, part, kdn.at[j], zrecv.at[xb0, j], z_dn).start()
        if j > 0:
            to_partner(xb0, j).start()

    def own_left(j):
        wait_bytes(chunk(xb0, j), kup.at[j])
        wait_bytes(chunk(xb0, j), kdn.at[j])

    def receive(side, d, j):
        xb = lax.div(zs(-d if side == 0 else d), 2)
        part = chunk(xb, j)
        wait_bytes(part, zrecv.at[xb, j])
        if d < 3 or (d == 3 and j % 2 == side):
            rcopy(part, part, zsend, zrecv.at[xb, j], (z_up, z_dn)[side]).start()
        if j > 0:
            to_partner(xb, j).start()

    def info(t):
        q_s = jnp.where(t < 2, t, jnp.where(t < 6, lax.div(t - 2, 2), t - 6))
        d_s = jnp.where(t < 2, 0, jnp.where(t < 6, 2, 4))
        q = jnp.where(is_src, q_s, lax.rem(lax.div(t, 2), 2))
        d = jnp.where(is_src, d_s, jnp.where(t < 4, 1, 3))
        z_from = lax.rem(jnp.where(lax.rem(t, 2) == 0, z + Z - d, z + d), Z)
        return lax.div(z_from, 2), q

    def relay_up(q):
        return rcopy(s2.at[q, pl.ds(0, 256)], rl.at[q], rsend.at[0], rlrecv.at[q], x_up)

    def relay_dn(q):
        return rcopy(s2.at[q, pl.ds(256, 256)], rr.at[q], rsend.at[1], rrrecv.at[q], x_dn)

    def final_up(q):
        return rcopy(s1.at[q], fl.at[q], fsend.at[0], flrecv.at[q], x_up)

    def final_dn(q):
        return rcopy(s3.at[q], fr.at[q], fsend.at[1], frrecv.at[q], x_dn)

    def consume(t):
        xb, q = info(t)

        @pl.when(q == 0)
        def _():
            wait_bytes(gbuf.at[xb, :, 1 - c, pl.ds(0, 2)], precv.at[xb, 0])

        wait_bytes(gbuf.at[xb, q, 1 - c, pl.ds(2, 2)], precv.at[xb, 1 + q])
        both = gbuf[xb, q].reshape(2 * Y * SLOT_LEN, W)
        part = jnp.dot(ats[...], both, preferred_element_type=F32) * (1.0 / SEQS)
        o = lax.rem(xb + X - x, X)

        @pl.when(o == 0)
        def _():
            own[q] = part

        @pl.when(o == 2)
        def _():
            s2[q] = part.astype(BF16)
            relay_up(q).start()
            relay_dn(q).start()

        @pl.when(lax.rem(o, 2) == 1)
        def _():
            hold[lax.rem(t, 3)] = part

    def finish(t):
        xb, q = info(t)
        o = lax.rem(xb + X - x, X)
        s = lax.rem(t, 3)

        @pl.when(o == 1)
        def _():
            relay_up(q).wait_recv()
            s1[q, pl.ds(0, 256)] = (hold[s, pl.ds(0, 256)] + rl[q].astype(F32)).astype(BF16)
            s1[q, pl.ds(256, 256)] = hold[s, pl.ds(256, 256)].astype(BF16)
            final_up(q).start()

        @pl.when(o == 3)
        def _():
            relay_dn(q).wait_recv()
            s3[q, pl.ds(0, 256)] = hold[s, pl.ds(0, 256)].astype(BF16)
            s3[q, pl.ds(256, 256)] = (hold[s, pl.ds(256, 256)] + rr[q].astype(F32)).astype(BF16)
            final_dn(q).start()

    calls = {
        "yl": first_steps, "yf": first_far, "o": own_chunk, "ol": own_left,
        "pairs": pair.start, "pairw": pair_wait, "ring": ring, "ringend": ring_end, "szs": squares,
        "szw": squares_wait, "syw": norms_wait, "aw": scale, "acts": acts, "arel": act_relay,
    }

    def run(plan):
        for name, *args in plan:
            if name == "r":
                receive(*args)
            else:
                calls[name](*args)

    rounds = {True: [[]], False: [[]]}
    for src, plan in ((True, SOURCE), (False, OTHER)):
        for item in plan:
            if item == ("C",):
                rounds[src].append([])
            else:
                rounds[src][-1].append(item)

    run(FIRST)

    @pl.when(is_src)
    def _():
        run(rounds[True][0])

    @pl.when(jnp.logical_not(is_src))
    def _():
        run(rounds[False][0])

    def round_of(t, _):
        for src in (True, False):
            for r in range(1, 8):
                if rounds[src][r]:
                    @pl.when(jnp.logical_and(t == r, is_src == src))
                    def _():
                        run(rounds[src][r])

        consume(t)

        @pl.when(t > 1)
        def _():
            finish(t - 2)

        return 0

    lax.fori_loop(0, 8, round_of, 0)
    finish(6)
    finish(7)

    @pl.when(is_src)
    def _():
        for j in range(4):
            if ("ol", j) not in SOURCE:
                own_left(j)
        wait_bytes(gbuf.at[pl.ds(0, 2), :, c], zsend)

    @pl.when(jnp.logical_not(is_src))
    def _():
        wait_bytes(gbuf.at[pl.ds(0, 3), :, c], zsend)

    wait_bytes(gbuf.at[:, :, c], psend)

    @pl.when(steps_y == 0)
    def _():
        for q in range(NQ):
            first(q, 1 - c).wait_send()

    @pl.when(steps_y >= 1)
    def _():
        for q in range(NQ):
            first(q, 0).wait_send()
            first(q, 1).wait_send()

    pair.wait_send()
    for i in range(1, 5):
        ring_up(i).wait_send()
    for i in range(1, 4):
        ring_dn(i).wait_send()
    wait_bytes(sz.at[pl.ds(0, 7)], szsend)
    wait_bytes(sy.at[pl.ds(0, 7)], sysend)
    wait_bytes(at.at[y], asend.at[0])
    wait_bytes(at.at[y], asend.at[1])
    wait_bytes(at.at[y], afsend)
    wait_bytes(rl, rsend.at[0])
    wait_bytes(rr, rsend.at[1])

    for q in range(NQ):
        final_up(q).wait_recv()
        final_dn(q).wait_recv()
        block = own[q] + fl[q].astype(F32) + fr[q].astype(F32)
        out_ref[pl.ds(q * W, W), :] = block.T.astype(BF16)
    wait_bytes(s1, fsend.at[0])
    wait_bytes(s3, fsend.at[1])


def local(activations, out_grads, lengths):
    dma, vmem = pltpu.SemaphoreType.DMA, pltpu.VMEM
    grams = (2, 3, 16, 128)
    scratch = [
        vmem((2, SLOT_LEN, F), BF16),
        vmem((2, SLOT_LEN, F), BF16),
        vmem((X, NQ, 2, Y, SLOT_LEN, W), BF16),
        vmem((Y, 2, F, SLOT_LEN), BF16),
        vmem((F, 2 * Y * SLOT_LEN), BF16),
        vmem((2, Z) + grams, F32),
        vmem((Z,) + grams, F32),
        vmem((Z,) + grams, F32),
        vmem((4,) + grams, F32),
        vmem((3,) + grams, F32),
        vmem((3,) + grams, F32),
        vmem((2,) + grams, F32),
        vmem((Z, 8, 128), F32),
        vmem((2 * Y, 8, 128), F32),
        vmem((3, F, W), F32),
        vmem((NQ, F, W), F32),
        vmem((NQ, F, W), BF16),
        vmem((NQ, F, W), BF16),
        vmem((NQ, F, W), BF16),
        vmem((NQ, 256, W), BF16),
        vmem((NQ, 256, W), BF16),
        vmem((NQ, F, W), BF16),
        vmem((NQ, F, W), BF16),
        dma((2,)), dma((NQ, 2)), dma((NQ, Y)), dma((4,)), dma((4,)), dma, dma((X, 4)),
        dma, dma((X, 3)), dma((2,)), dma((2,)), dma, dma, dma,
        dma, dma, dma((4,)), dma((4,)), dma((3,)), dma((3,)), dma, dma, dma, dma,
        dma((2,)), dma((NQ,)), dma((NQ,)), dma((2,)), dma((NQ,)), dma((NQ,)),
    ]
    return pl.pallas_call(
        kernel,
        out_shape=(
            jax.ShapeDtypeStruct((F, F), BF16),
            jax.ShapeDtypeStruct((2,), F32),
        ),
        in_specs=[
            pl.BlockSpec(memory_space=pltpu.SMEM),
            pl.BlockSpec(memory_space=pl.ANY),
            pl.BlockSpec(memory_space=pl.ANY),
        ],
        out_specs=(
            pl.BlockSpec(memory_space=pltpu.VMEM),
            pl.BlockSpec(memory_space=pltpu.SMEM),
        ),
        scratch_shapes=scratch,
        compiler_params=pltpu.CompilerParams(
            collective_id=0, has_side_effects=True, vmem_limit_bytes=40 * 1024 * 1024
        ),
        cost_estimate=pl.CostEstimate(flops=2 * 512 * 512 * 8192, bytes_accessed=3 * 2**19, transcendentals=0),
    )(*(pltpu.with_memory_space_constraint(v, pltpu.HBM) for v in (lengths, activations, out_grads)))


def solution(mesh):
    placed = (P("dp", None, "tensor"), P("dp", None, "tensor"), P("dp"))
    return jax.shard_map(
        local, mesh=mesh, in_specs=placed, out_specs=(P("dp", "tensor"), P("dp")), check_vma=False
    )
```

```python
import math

import jax
import jax.numpy as jnp
from jax import lax
from jax.experimental import pallas as pl
from jax.experimental.pallas import tpu as pltpu
from jax.sharding import PartitionSpec as P

D = 8192
K = 8192
SLOT_LEN = 256
SEQS = 32
X, Y, Z = 4, 4, 8
NQ = 2
W = 256
F = 512
BOUND = math.sqrt(K * D * SLOT_LEN / 2.0)
F32 = jnp.float32
BF16 = jnp.bfloat16

FIRST = (
    ("yl",), ("gram",), ("yf", 0), ("pairs",),
)
SOURCE = (
    ("o", 0), ("yf", 1), ("pairw",), ("ring", 1), ("ring", 2), ("o", 1), ("acts", 3), ("ring", 3),
    ("ring", 4), ("o", 2), ("acts", 1), ("ringend",), ("szs",), ("o", 3), ("r", 1, 2, 0), ("r", 0, 2, 0),
    ("arel", 0), ("arel", 1), ("szw",), ("r", 1, 2, 1), ("r", 0, 2, 1), ("syw",), ("aw",), ("C",),
    ("r", 1, 2, 2), ("r", 0, 2, 2), ("C",), ("C",), ("r", 1, 2, 3), ("C",), ("r", 0, 2, 3), ("C",), ("C",),
    ("r", 0, 4, 0), ("r", 1, 4, 1), ("r", 0, 4, 2), ("C",), ("r", 1, 4, 3), ("C",),
)
OTHER = (
    ("pairw",), ("yf", 1), ("ring", 1), ("ring", 2), ("acts", 3), ("ring", 3), ("r", 0, 1, 0), ("r", 1, 1, 0),
    ("ring", 4), ("acts", 1), ("ringend",), ("szs",), ("r", 1, 1, 1), ("r", 0, 1, 1), ("arel", 0),
    ("arel", 1), ("szw",), ("r", 0, 1, 2), ("r", 1, 1, 2), ("r", 1, 1, 3), ("syw",), ("r", 0, 1, 3), ("aw",),
    ("C",), ("C",), ("r", 1, 3, 0), ("r", 0, 3, 0), ("C",), ("C",), ("r", 1, 3, 1), ("r", 0, 3, 1),
    ("r", 0, 3, 2), ("r", 1, 3, 2), ("C",), ("r", 1, 3, 3), ("C",), ("r", 0, 3, 3), ("C",), ("C",),
)

def rcopy(src, dst, send, recv, device):
    return pltpu.make_async_remote_copy(
        src_ref=src,
        dst_ref=dst,
        send_sem=send,
        recv_sem=recv,
        device_id=device,
        device_id_type=pl.DeviceIdType.MESH,
    )


def wait_bytes(ref, sem):
    pltpu.make_async_copy(ref, ref, sem).wait()


def kernel(
    len_ref, a_hbm, g_hbm, out_ref, norm_ref,
    a_ref, g_ref, gbuf, at, ats, gpack, gpair, gsum, gup, gdn, sup, sdn, sz, sy,
    hold, own, s1, s2, s3, rl, rr, fl, fr,
    loads, ysend, yrecv, kup, kdn, zsend, zrecv, psend, precv, asend, a_up, a_dn, a_far, afsend,
    gpsend, gprecv, gupsend, guprecv, gdnsend, gdnrecv, szsend, szrecv, sysend, syrecv,
    rsend, rlrecv, rrrecv, fsend, flrecv, frrecv,
):
    dp = lax.axis_index("dp")
    tn = lax.axis_index("tensor")
    x, y = lax.div(dp, Y), lax.rem(dp, Y)
    z, c = lax.div(tn, 2), lax.rem(tn, 2)

    def dev(x_, y_, z_, c_):
        return (x_ * Y + y_, z_ * 2 + c_)

    def xs(k):
        return lax.rem(x + k, X)

    def ys(k):
        return lax.rem(y + k, Y)

    def zs(k):
        return lax.rem(z + k + Z, Z)

    partner = dev(x, y, z, 1 - c)
    z_up, z_dn = dev(x, y, zs(1), c), dev(x, y, zs(-1), c)
    x_up, x_dn = dev(xs(1), y, z, c), dev(xs(3), y, z, c)
    y_up, y_dn = dev(x, ys(1), z, c), dev(x, ys(3), z, c)
    y_others = [(ys(k), c) for k in (1, 2, 3)] + [(ys(k), 1 - c) for k in (0, 1, 2, 3)]

    load_a = pltpu.make_async_copy(a_hbm, a_ref, loads.at[0])
    load_g = pltpu.make_async_copy(g_hbm, g_ref, loads.at[1])
    load_a.start()
    load_g.start()

    barrier = pltpu.get_barrier_semaphore()
    peers = [dev(x, y2, z, c2) for y2, c2 in y_others]
    peers += [dev(x, y, zs(k), c) for k in range(1, Z)] + [x_up, x_dn]
    for peer in peers:
        pl.semaphore_signal(barrier, inc=1, device_id=peer, device_id_type=pl.DeviceIdType.MESH)
    rows = lax.broadcasted_iota(jnp.int32, (SLOT_LEN, F), 0)
    contract = (((1,), (1,)), ((), ()))
    load_a.wait()
    load_g.wait()

    def gram(s):
        am = jnp.where(rows < len_ref[s], a_ref[s].astype(F32), 0.0)
        at[y, s] = am.T.astype(BF16)
        am = am.astype(BF16)
        g = g_ref[s]
        for m, v in enumerate((am, g)):
            full = lax.dot_general(v, v, contract, preferred_element_type=F32)
            gpack[s, :, m, 0] = full[:128, :128].reshape(Z, 16, 128)
            gpack[s, :, m, 1] = full[:128, 128:].reshape(Z, 16, 128)
            gpack[s, :, m, 2] = full[128:, 128:].reshape(Z, 16, 128)
    gram(0)
    pl.semaphore_wait(barrier, len(peers))

    xb0 = lax.div(z, 2)
    yt = 2 * lax.rem(z, 2) + c
    is_src = lax.rem(z, 2) == lax.div(y, 2)
    steps_y = lax.rem(y - yt + Y, Y)

    def first(q, h):
        return rcopy(
            g_hbm.at[h, :, pl.ds(q * W, W)], gbuf.at[xb0, q, h, steps_y], ysend.at[q, h],
            yrecv.at[q, steps_y], dev(x, yt, z, h),
        )

    def first_steps():
        @pl.when(steps_y == 0)
        def _():
            for q in range(NQ):
                pltpu.make_async_copy(
                    g_hbm.at[c, :, pl.ds(q * W, W)], gbuf.at[xb0, q, c, 0], yrecv.at[q, 0]
                ).start()
                first(q, 1 - c).start()

        @pl.when(steps_y == 1)
        def _():
            for q in range(NQ):
                first(q, 0).start()
                first(q, 1).start()

    def first_far(q):
        @pl.when(steps_y >= 2)
        def _():
            first(q, 0).start()
            first(q, 1).start()

    pair = rcopy(gpack.at[1 - c], gpair, gpsend, gprecv, partner)

    def pair_wait():
        pair.wait_recv()
        gsum[...] = gpack[c] + gpair[...]

    def ring_up(i):
        src = gsum.at[zs(4)] if i == 1 else sup.at[i - 2]
        return rcopy(src, gup.at[i - 1], gupsend.at[i - 1], guprecv.at[i - 1], z_up)

    def ring_dn(i):
        src = gsum.at[zs(-3)] if i == 1 else sdn.at[i - 2]
        return rcopy(src, gdn.at[i - 1], gdnsend.at[i - 1], gdnrecv.at[i - 1], z_dn)

    def ring(i):
        if i > 1:
            ring_up(i - 1).wait_recv()
            sup[i - 2] = gsum[zs(5 - i)] + gup[i - 2]
        ring_up(i).start()
        if i <= 3:
            if i > 1:
                ring_dn(i - 1).wait_recv()
                sdn[i - 2] = gsum[zs(i - 4)] + gdn[i - 2]
            ring_dn(i).start()

    def ring_end():
        ring_up(4).wait_recv()
        ring_dn(3).wait_recv()
        total = gsum[z] + gup[3] + gdn[2]
        prod = total[0] * total[1]
        square = jnp.sum(prod[0] + 2.0 * prod[1] + prod[2])
        sz[z] = jnp.full((8, 128), square, F32)

    def squares():
        for k in range(1, Z):
            rcopy(sz.at[z], sz.at[z], szsend, szrecv, dev(x, y, zs(k), c)).start()

    def squares_wait():
        wait_bytes(sz.at[pl.ds(0, 7)], szrecv)
        tile = sz[0]
        for k in range(1, Z):
            tile = tile + sz[k]
        mine = y * 2 + c
        sy[mine] = tile
        for y2, c2 in y_others:
            rcopy(sy.at[mine], sy.at[mine], sysend, syrecv, dev(x, y2, z, c2)).start()

    def norms_wait():
        wait_bytes(sy.at[pl.ds(0, 7)], syrecv)

    def acts(side):
        if side == 1:
            rcopy(at.at[y], at.at[y], asend.at[0], a_dn, y_up).start()
        else:
            for h in range(2):
                rcopy(at.at[y, h], at.at[y, h], asend.at[1], a_up.at[h], y_dn).start()

    def act_relay(h):
        part = at.at[ys(1), h]
        wait_bytes(part, a_up.at[h])
        rcopy(part, part, afsend, a_far, y_dn).start()

    def scale():
        wait_bytes(at.at[ys(3)], a_dn)
        wait_bytes(at.at[ys(2)], a_far)
        for h in range(2):
            norm_ref[h] = jnp.max(jnp.sqrt(sy[y * 2 + h] + 1e-6))
        for h in range(2):
            for k in range(Y):
                factor = jnp.max(jnp.minimum(1.0, BOUND / jnp.sqrt(sy[ys(k) * 2 + h] + 1e-6)))
                scaled = (at[ys(k), h].astype(F32) * factor).astype(BF16)
                ats[:, pl.ds((h * Y + k) * SLOT_LEN, SLOT_LEN)] = scaled

    def chunk(xb, j):
        return gbuf.at[xb, :, c, j] if j < 2 else gbuf.at[xb, j - 2, c, pl.ds(2, 2)]

    def to_partner(xb, j):
        part = gbuf.at[xb, :, c, pl.ds(0, 2)] if j == 1 else chunk(xb, j)
        return rcopy(part, part, psend, precv.at[xb, j - 1], partner)

    def own_chunk(j):
        part = chunk(xb0, j)
        if j < 2:
            for q in range(NQ):
                wait_bytes(gbuf.at[xb0, q, c, j], yrecv.at[q, j])
        else:
            for k in (2, 3):
                wait_bytes(gbuf.at[xb0, j - 2, c, k], yrecv.at[j - 2, k])
        rcopy(part, part, kup.at[j], zrecv.at[xb0, j], z_up).start()
        rcopy(part, part, kdn.at[j], zrecv.at[xb0, j], z_dn).start()
        if j > 0:
            to_partner(xb0, j).start()

    def own_left(j):
        wait_bytes(chunk(xb0, j), kup.at[j])
        wait_bytes(chunk(xb0, j), kdn.at[j])

    def receive(side, d, j):
        xb = lax.div(zs(-d if side == 0 else d), 2)
        part = chunk(xb, j)
        wait_bytes(part, zrecv.at[xb, j])
        if d < 3 or (d == 3 and j % 2 == side):
            rcopy(part, part, zsend, zrecv.at[xb, j], (z_up, z_dn)[side]).start()
        if j > 0:
            to_partner(xb, j).start()

    def info(t):
        q_s = jnp.where(t < 2, t, jnp.where(t < 6, lax.div(t - 2, 2), t - 6))
        d_s = jnp.where(t < 2, 0, jnp.where(t < 6, 2, 4))
        q = jnp.where(is_src, q_s, lax.rem(lax.div(t, 2), 2))
        d = jnp.where(is_src, d_s, jnp.where(t < 4, 1, 3))
        z_from = lax.rem(jnp.where(lax.rem(t, 2) == 0, z + Z - d, z + d), Z)
        return lax.div(z_from, 2), q

    def relay_up(q, first, rows, slot):
        part = pl.ds(first, rows)
        return rcopy(s2.at[q, part], rl.at[q, part], rsend.at[0], rlrecv.at[q, slot], x_up)

    def relay_dn(q, first, rows, slot):
        return rcopy(
            s2.at[q, pl.ds(256 + first, rows)], rr.at[q, pl.ds(first, rows)], rsend.at[1],
            rrrecv.at[q, slot], x_dn,
        )

    def final_up(q, first, rows):
        part = pl.ds(first, rows)
        rcopy(s1.at[q, part], fl.at[q, part], fsend.at[0], flrecv.at[q], x_up).start()

    def final_dn(q, first, rows):
        part = pl.ds(first, rows)
        rcopy(s3.at[q, part], fr.at[q, part], fsend.at[1], frrecv.at[q], x_dn).start()

    def parts_of(t, run_part):
        @pl.when(t < 6)
        def _():
            run_part(0, 256, 0)

        @pl.when(t >= 6)
        def _():
            run_part(0, 128, 0)
            run_part(128, 128, 1)

    def consume(t):
        xb, q = info(t)

        @pl.when(q == 0)
        def _():
            wait_bytes(gbuf.at[xb, :, 1 - c, pl.ds(0, 2)], precv.at[xb, 0])

        wait_bytes(gbuf.at[xb, q, 1 - c, pl.ds(2, 2)], precv.at[xb, 1 + q])
        both = gbuf[xb, q].reshape(2 * Y * SLOT_LEN, W)
        part = jnp.dot(ats[...], both, preferred_element_type=F32) * (1.0 / SEQS)
        o = lax.rem(xb + X - x, X)

        @pl.when(o == 0)
        def _():
            own[q] = part

        @pl.when(o == 2)
        def _():
            s2[q] = part.astype(BF16)

            def send(first, rows, slot):
                relay_up(q, first, rows, slot).start()
                relay_dn(q, first, rows, slot).start()

            parts_of(t, send)

        @pl.when(o == 1)
        def _():
            s1[q, pl.ds(256, 256)] = part[256:].astype(BF16)
            final_up(q, 256, 256)
            hold[lax.rem(t, 3)] = part[:256]

        @pl.when(o == 3)
        def _():
            s3[q, pl.ds(0, 256)] = part[:256].astype(BF16)
            final_dn(q, 0, 256)
            hold[lax.rem(t, 3)] = part[256:]

    def finish(t):
        xb, q = info(t)
        o = lax.rem(xb + X - x, X)
        s = lax.rem(t, 3)

        @pl.when(o == 1)
        def _():
            def add(first, rows, slot):
                part = pl.ds(first, rows)
                relay_up(q, first, rows, slot).wait_recv()
                s1[q, part] = (hold[s, part] + rl[q, part].astype(F32)).astype(BF16)
                final_up(q, first, rows)

            parts_of(t, add)

        @pl.when(o == 3)
        def _():
            def add(first, rows, slot):
                part = pl.ds(first, rows)
                relay_dn(q, first, rows, slot).wait_recv()
                s3[q, pl.ds(256 + first, rows)] = (hold[s, part] + rr[q, part].astype(F32)).astype(BF16)
                final_dn(q, 256 + first, rows)

            parts_of(t, add)

    calls = {
        "gram": lambda: gram(1), "yl": first_steps, "yf": first_far, "o": own_chunk, "ol": own_left,
        "pairs": pair.start, "pairw": pair_wait, "ring": ring, "ringend": ring_end, "szs": squares,
        "szw": squares_wait, "syw": norms_wait, "aw": scale, "acts": acts, "arel": act_relay,
    }

    def run(plan):
        for name, *args in plan:
            if name == "r":
                receive(*args)
            else:
                calls[name](*args)

    rounds = {True: [[]], False: [[]]}
    for src, plan in ((True, SOURCE), (False, OTHER)):
        for item in plan:
            if item == ("C",):
                rounds[src].append([])
            else:
                rounds[src][-1].append(item)

    run(FIRST)

    @pl.when(is_src)
    def _():
        run(rounds[True][0])

    @pl.when(jnp.logical_not(is_src))
    def _():
        run(rounds[False][0])

    def round_of(t, _):
        for src in (True, False):
            for r in range(1, 8):
                if rounds[src][r]:
                    @pl.when(jnp.logical_and(t == r, is_src == src))
                    def _():
                        run(rounds[src][r])

        consume(t)

        @pl.when(t > 1)
        def _():
            finish(t - 2)

        return 0

    lax.fori_loop(0, 8, round_of, 0)
    finish(6)
    finish(7)

    @pl.when(is_src)
    def _():
        for j in range(4):
            if ("ol", j) not in SOURCE:
                own_left(j)
        wait_bytes(gbuf.at[pl.ds(0, 2), :, c], zsend)

    @pl.when(jnp.logical_not(is_src))
    def _():
        wait_bytes(gbuf.at[pl.ds(0, 3), :, c], zsend)

    wait_bytes(gbuf.at[:, :, c], psend)

    @pl.when(steps_y == 0)
    def _():
        for q in range(NQ):
            first(q, 1 - c).wait_send()

    @pl.when(steps_y >= 1)
    def _():
        for q in range(NQ):
            first(q, 0).wait_send()
            first(q, 1).wait_send()

    pair.wait_send()
    for i in range(1, 5):
        ring_up(i).wait_send()
    for i in range(1, 4):
        ring_dn(i).wait_send()
    wait_bytes(sz.at[pl.ds(0, 7)], szsend)
    wait_bytes(sy.at[pl.ds(0, 7)], sysend)
    wait_bytes(at.at[y], asend.at[0])
    wait_bytes(at.at[y], asend.at[1])
    wait_bytes(at.at[y], afsend)
    wait_bytes(rl, rsend.at[0])
    wait_bytes(rr, rsend.at[1])

    for q in range(NQ):
        wait_bytes(fl.at[q], flrecv.at[q])
        wait_bytes(fr.at[q], frrecv.at[q])
        block = own[q] + fl[q].astype(F32) + fr[q].astype(F32)
        out_ref[pl.ds(q * W, W), :] = block.T.astype(BF16)
    wait_bytes(s1, fsend.at[0])
    wait_bytes(s3, fsend.at[1])


def local(activations, out_grads, lengths):
    dma, vmem = pltpu.SemaphoreType.DMA, pltpu.VMEM
    grams = (2, 3, 16, 128)
    scratch = [
        vmem((2, SLOT_LEN, F), BF16),
        vmem((2, SLOT_LEN, F), BF16),
        vmem((X, NQ, 2, Y, SLOT_LEN, W), BF16),
        vmem((Y, 2, F, SLOT_LEN), BF16),
        vmem((F, 2 * Y * SLOT_LEN), BF16),
        vmem((2, Z) + grams, F32),
        vmem((Z,) + grams, F32),
        vmem((Z,) + grams, F32),
        vmem((4,) + grams, F32),
        vmem((3,) + grams, F32),
        vmem((3,) + grams, F32),
        vmem((2,) + grams, F32),
        vmem((Z, 8, 128), F32),
        vmem((2 * Y, 8, 128), F32),
        vmem((3, 256, W), F32),
        vmem((NQ, F, W), F32),
        vmem((NQ, F, W), BF16),
        vmem((NQ, F, W), BF16),
        vmem((NQ, F, W), BF16),
        vmem((NQ, 256, W), BF16),
        vmem((NQ, 256, W), BF16),
        vmem((NQ, F, W), BF16),
        vmem((NQ, F, W), BF16),
        dma((2,)), dma((NQ, 2)), dma((NQ, Y)), dma((4,)), dma((4,)), dma, dma((X, 4)),
        dma, dma((X, 3)), dma((2,)), dma((2,)), dma, dma, dma,
        dma, dma, dma((4,)), dma((4,)), dma((3,)), dma((3,)), dma, dma, dma, dma,
        dma((2,)), dma((NQ, 2)), dma((NQ, 2)), dma((2,)), dma((NQ,)), dma((NQ,)),
    ]
    return pl.pallas_call(
        kernel,
        out_shape=(
            jax.ShapeDtypeStruct((F, F), BF16),
            jax.ShapeDtypeStruct((2,), F32),
        ),
        in_specs=[
            pl.BlockSpec(memory_space=pltpu.SMEM),
            pl.BlockSpec(memory_space=pl.ANY),
            pl.BlockSpec(memory_space=pl.ANY),
        ],
        out_specs=(
            pl.BlockSpec(memory_space=pltpu.VMEM),
            pl.BlockSpec(memory_space=pltpu.SMEM),
        ),
        scratch_shapes=scratch,
        compiler_params=pltpu.CompilerParams(
            collective_id=0, has_side_effects=True, vmem_limit_bytes=40 * 1024 * 1024
        ),
        cost_estimate=pl.CostEstimate(flops=2 * 512 * 512 * 8192, bytes_accessed=3 * 2**19, transcendentals=0),
    )(*(pltpu.with_memory_space_constraint(v, pltpu.HBM) for v in (lengths, activations, out_grads)))


def solution(mesh):
    placed = (P("dp", None, "tensor"), P("dp", None, "tensor"), P("dp"))
    return jax.shard_map(
        local, mesh=mesh, in_specs=placed, out_specs=(P("dp", "tensor"), P("dp")), check_vma=False
    )
```

```python
import math

import jax
import jax.numpy as jnp
from jax import lax
from jax.experimental import pallas as pl
from jax.experimental.pallas import tpu as pltpu
from jax.sharding import PartitionSpec as P

D = 8192
K = 8192
SLOT_LEN = 256
SEQS = 32
X, Y, Z = 4, 4, 8
NQ = 2
W = 256
F = 512
BOUND = math.sqrt(K * D * SLOT_LEN / 2.0)
F32 = jnp.float32
BF16 = jnp.bfloat16

FIRST = (
    ("yl",),
)
SOURCE = (
    ("gram",), ("o", 0), ("pairs",), ("yf", 0), ("pairw",), ("ring", 1), ("yg", 0), ("ring", 2), ("yg", 1),
    ("yf", 1), ("acts", 3), ("o", 1), ("ring", 3), ("ring", 4), ("o", 2), ("ringend",), ("szs",), ("acts", 1),
    ("o", 3), ("r", 0, 2, 0), ("r", 1, 2, 0), ("arel", 0), ("szw",), ("arel", 1), ("r", 1, 2, 1),
    ("r", 0, 2, 1), ("syw",), ("r", 1, 2, 2), ("aw",), ("C",), ("r", 0, 2, 2), ("C",), ("C",), ("C",),
    ("r", 1, 2, 3), ("r", 0, 2, 3), ("C",), ("r", 0, 4, 0), ("C",), ("r", 1, 4, 1), ("r", 0, 4, 2), ("C",),
    ("r", 1, 4, 3), ("C",),
)
OTHER = (
    ("yf", 0), ("gram",), ("pairs",), ("pairw",), ("ring", 1), ("yg", 0), ("yg", 1), ("yf", 1), ("ring", 2),
    ("acts", 3), ("ring", 3), ("r", 1, 1, 0), ("r", 0, 1, 0), ("ring", 4), ("ringend",), ("szs",),
    ("acts", 1), ("r", 1, 1, 1), ("r", 0, 1, 1), ("arel", 0), ("szw",), ("arel", 1), ("r", 1, 1, 2),
    ("r", 0, 1, 2), ("syw",), ("r", 0, 1, 3), ("r", 1, 1, 3), ("aw",), ("r", 1, 3, 0), ("C",), ("r", 0, 3, 0),
    ("C",), ("C",), ("C",), ("r", 0, 3, 1), ("r", 1, 3, 1), ("r", 0, 3, 2), ("r", 1, 3, 2), ("C",), ("C",),
    ("r", 1, 3, 3), ("r", 0, 3, 3), ("C",), ("C",),
)

def rcopy(src, dst, send, recv, device):
    return pltpu.make_async_remote_copy(
        src_ref=src,
        dst_ref=dst,
        send_sem=send,
        recv_sem=recv,
        device_id=device,
        device_id_type=pl.DeviceIdType.MESH,
    )


def wait_bytes(ref, sem):
    pltpu.make_async_copy(ref, ref, sem).wait()


def kernel(
    len_ref, a_hbm, g_hbm, out_ref, norm_ref,
    a_ref, g_ref, gbuf, at, ats, gpack, gpair, gsum, gup, gdn, sup, sdn, sz, sy,
    hold, own, s1, s2, s3, rl, rr, fl, fr,
    loads, ysend, yrecv, kup, kdn, zsend, zrecv, psend, precv, asend, a_up, a_dn, a_far, afsend,
    gpsend, gprecv, gupsend, guprecv, gdnsend, gdnrecv, szsend, szrecv, sysend, syrecv,
    rsend, rlrecv, rrrecv, fsend, flrecv, frrecv,
):
    dp = lax.axis_index("dp")
    tn = lax.axis_index("tensor")
    x, y = lax.div(dp, Y), lax.rem(dp, Y)
    z, c = lax.div(tn, 2), lax.rem(tn, 2)

    def dev(x_, y_, z_, c_):
        return (x_ * Y + y_, z_ * 2 + c_)

    def xs(k):
        return lax.rem(x + k, X)

    def ys(k):
        return lax.rem(y + k, Y)

    def zs(k):
        return lax.rem(z + k + Z, Z)

    partner = dev(x, y, z, 1 - c)
    z_up, z_dn = dev(x, y, zs(1), c), dev(x, y, zs(-1), c)
    x_up, x_dn = dev(xs(1), y, z, c), dev(xs(3), y, z, c)
    y_up, y_dn = dev(x, ys(1), z, c), dev(x, ys(3), z, c)
    y_others = [(ys(k), c) for k in (1, 2, 3)] + [(ys(k), 1 - c) for k in (0, 1, 2, 3)]

    load_a = pltpu.make_async_copy(a_hbm, a_ref, loads.at[0])
    load_g = pltpu.make_async_copy(g_hbm, g_ref, loads.at[1])
    load_a.start()
    load_g.start()

    barrier = pltpu.get_barrier_semaphore()
    peers = [dev(x, y2, z, c2) for y2, c2 in y_others]
    peers += [dev(x, y, zs(k), c) for k in range(1, Z)] + [x_up, x_dn]
    for peer in peers:
        pl.semaphore_signal(barrier, inc=1, device_id=peer, device_id_type=pl.DeviceIdType.MESH)
    rows = lax.broadcasted_iota(jnp.int32, (SLOT_LEN, F), 0)
    contract = (((1,), (1,)), ((), ()))
    load_a.wait()
    load_g.wait()

    def gram(s):
        am = jnp.where(rows < len_ref[s], a_ref[s].astype(F32), 0.0)
        at[y, s] = am.T.astype(BF16)
        am = am.astype(BF16)
        g = g_ref[s]
        for m, v in enumerate((am, g)):
            full = lax.dot_general(v, v, contract, preferred_element_type=F32)
            gpack[s, :, m, 0] = full[:128, :128].reshape(Z, 16, 128)
            gpack[s, :, m, 1] = full[:128, 128:].reshape(Z, 16, 128)
            gpack[s, :, m, 2] = full[128:, 128:].reshape(Z, 16, 128)
    gram(0)
    pl.semaphore_wait(barrier, len(peers))

    xb0 = lax.div(z, 2)
    yt = 2 * lax.rem(z, 2) + c
    is_src = lax.rem(z, 2) == lax.div(y, 2)
    steps_y = lax.rem(y - yt + Y, Y)

    def first(q, h):
        return rcopy(
            g_hbm.at[h, :, pl.ds(q * W, W)], gbuf.at[xb0, q, h, steps_y], ysend.at[q, h],
            yrecv.at[q, steps_y], dev(x, yt, z, h),
        )

    def first_steps():
        @pl.when(steps_y == 0)
        def _():
            for q in range(NQ):
                pltpu.make_async_copy(
                    g_hbm.at[c, :, pl.ds(q * W, W)], gbuf.at[xb0, q, c, 0], yrecv.at[q, 0]
                ).start()
                first(q, 1 - c).start()

        @pl.when(steps_y == 1)
        def _():
            for q in range(NQ):
                first(q, 0).start()
                first(q, 1).start()

    def first_far(steps, q):
        @pl.when(steps_y == steps)
        def _():
            first(q, 0).start()
            first(q, 1).start()

    pair = rcopy(gpack.at[1 - c], gpair, gpsend, gprecv, partner)

    def pair_wait():
        pair.wait_recv()
        gsum[...] = gpack[c] + gpair[...]

    def ring_up(i):
        src = gsum.at[zs(4)] if i == 1 else sup.at[i - 2]
        return rcopy(src, gup.at[i - 1], gupsend.at[i - 1], guprecv.at[i - 1], z_up)

    def ring_dn(i):
        src = gsum.at[zs(-3)] if i == 1 else sdn.at[i - 2]
        return rcopy(src, gdn.at[i - 1], gdnsend.at[i - 1], gdnrecv.at[i - 1], z_dn)

    def ring(i):
        if i > 1:
            ring_up(i - 1).wait_recv()
            sup[i - 2] = gsum[zs(5 - i)] + gup[i - 2]
        ring_up(i).start()
        if i <= 3:
            if i > 1:
                ring_dn(i - 1).wait_recv()
                sdn[i - 2] = gsum[zs(i - 4)] + gdn[i - 2]
            ring_dn(i).start()

    def ring_end():
        ring_up(4).wait_recv()
        ring_dn(3).wait_recv()
        total = gsum[z] + gup[3] + gdn[2]
        prod = total[0] * total[1]
        square = jnp.sum(prod[0] + 2.0 * prod[1] + prod[2])
        sz[z] = jnp.full((8, 128), square, F32)

    def squares():
        for k in range(1, Z):
            rcopy(sz.at[z], sz.at[z], szsend, szrecv, dev(x, y, zs(k), c)).start()

    def squares_wait():
        wait_bytes(sz.at[pl.ds(0, 7)], szrecv)
        tile = sz[0]
        for k in range(1, Z):
            tile = tile + sz[k]
        mine = y * 2 + c
        sy[mine] = tile
        for y2, c2 in y_others:
            rcopy(sy.at[mine], sy.at[mine], sysend, syrecv, dev(x, y2, z, c2)).start()

    def norms_wait():
        wait_bytes(sy.at[pl.ds(0, 7)], syrecv)

    def acts(side):
        if side == 1:
            rcopy(at.at[y], at.at[y], asend.at[0], a_dn, y_dn).start()
        else:
            for h in range(2):
                rcopy(at.at[y, h], at.at[y, h], asend.at[1], a_up.at[h], y_up).start()

    def act_relay(h):
        part = at.at[ys(3), h]
        wait_bytes(part, a_up.at[h])
        rcopy(part, part, afsend, a_far, y_up).start()

    def scale():
        wait_bytes(at.at[ys(1)], a_dn)
        wait_bytes(at.at[ys(2)], a_far)
        for h in range(2):
            norm_ref[h] = jnp.max(jnp.sqrt(sy[y * 2 + h] + 1e-6))
        for h in range(2):
            for k in range(Y):
                factor = jnp.max(jnp.minimum(1.0, BOUND / jnp.sqrt(sy[ys(k) * 2 + h] + 1e-6)))
                scaled = (at[ys(k), h].astype(F32) * factor).astype(BF16)
                ats[:, pl.ds((h * Y + k) * SLOT_LEN, SLOT_LEN)] = scaled

    def chunk(xb, j):
        return gbuf.at[xb, :, c, j] if j < 2 else gbuf.at[xb, j - 2, c, pl.ds(2, 2)]

    def to_partner(xb, j):
        part = gbuf.at[xb, :, c, pl.ds(0, 2)] if j == 1 else chunk(xb, j)
        return rcopy(part, part, psend, precv.at[xb, j - 1], partner)

    def own_chunk(j):
        part = chunk(xb0, j)
        if j < 2:
            for q in range(NQ):
                wait_bytes(gbuf.at[xb0, q, c, j], yrecv.at[q, j])
        else:
            for k in (2, 3):
                wait_bytes(gbuf.at[xb0, j - 2, c, k], yrecv.at[j - 2, k])
        rcopy(part, part, kup.at[j], zrecv.at[xb0, j], z_up).start()
        rcopy(part, part, kdn.at[j], zrecv.at[xb0, j], z_dn).start()
        if j > 0:
            to_partner(xb0, j).start()

    def own_left(j):
        wait_bytes(chunk(xb0, j), kup.at[j])
        wait_bytes(chunk(xb0, j), kdn.at[j])

    def receive(side, d, j):
        xb = lax.div(zs(-d if side == 0 else d), 2)
        part = chunk(xb, j)
        wait_bytes(part, zrecv.at[xb, j])
        if d < 3 or (d == 3 and j % 2 == side):
            rcopy(part, part, zsend, zrecv.at[xb, j], (z_up, z_dn)[side]).start()
        if j > 0:
            to_partner(xb, j).start()

    def info(t):
        q_s = jnp.where(t < 2, t, jnp.where(t < 6, lax.div(t - 2, 2), t - 6))
        d_s = jnp.where(t < 2, 0, jnp.where(t < 6, 2, 4))
        q = jnp.where(is_src, q_s, lax.rem(lax.div(t, 2), 2))
        d = jnp.where(is_src, d_s, jnp.where(t < 4, 1, 3))
        z_from = lax.rem(jnp.where(lax.rem(t, 2) == 0, z + Z - d, z + d), Z)
        return lax.div(z_from, 2), q

    def relay_up(q, first, rows, slot):
        part = pl.ds(first, rows)
        return rcopy(s2.at[q, part], rl.at[q, part], rsend.at[0], rlrecv.at[q, slot], x_up)

    def relay_dn(q, first, rows, slot):
        return rcopy(
            s2.at[q, pl.ds(256 + first, rows)], rr.at[q, pl.ds(first, rows)], rsend.at[1],
            rrrecv.at[q, slot], x_dn,
        )

    def final_up(q, first, rows):
        part = pl.ds(first, rows)
        rcopy(s1.at[q, part], fl.at[q, part], fsend.at[0], flrecv.at[q], x_up).start()

    def final_dn(q, first, rows):
        part = pl.ds(first, rows)
        rcopy(s3.at[q, part], fr.at[q, part], fsend.at[1], frrecv.at[q], x_dn).start()

    def parts_of(t, run_part):
        @pl.when(t < 6)
        def _():
            run_part(0, 256, 0)

        @pl.when(t >= 6)
        def _():
            run_part(0, 128, 0)
            run_part(128, 128, 1)

    def consume(t):
        xb, q = info(t)

        @pl.when(q == 0)
        def _():
            wait_bytes(gbuf.at[xb, :, 1 - c, pl.ds(0, 2)], precv.at[xb, 0])

        wait_bytes(gbuf.at[xb, q, 1 - c, pl.ds(2, 2)], precv.at[xb, 1 + q])
        both = gbuf[xb, q].reshape(2 * Y * SLOT_LEN, W)
        part = jnp.dot(ats[...], both, preferred_element_type=F32) * (1.0 / SEQS)
        o = lax.rem(xb + X - x, X)

        @pl.when(o == 0)
        def _():
            own[q] = part

        @pl.when(o == 2)
        def _():
            s2[q] = part.astype(BF16)

            def send(first, rows, slot):
                relay_up(q, first, rows, slot).start()
                relay_dn(q, first, rows, slot).start()

            parts_of(t, send)

        @pl.when(o == 1)
        def _():
            s1[q, pl.ds(256, 256)] = part[256:].astype(BF16)
            final_up(q, 256, 256)
            hold[lax.rem(t, 3)] = part[:256]

        @pl.when(o == 3)
        def _():
            s3[q, pl.ds(0, 256)] = part[:256].astype(BF16)
            final_dn(q, 0, 256)
            hold[lax.rem(t, 3)] = part[256:]

    def finish(t):
        xb, q = info(t)
        o = lax.rem(xb + X - x, X)
        s = lax.rem(t, 3)

        @pl.when(o == 1)
        def _():
            def add(first, rows, slot):
                part = pl.ds(first, rows)
                relay_up(q, first, rows, slot).wait_recv()
                s1[q, part] = (hold[s, part] + rl[q, part].astype(F32)).astype(BF16)
                final_up(q, first, rows)

            parts_of(t, add)

        @pl.when(o == 3)
        def _():
            def add(first, rows, slot):
                part = pl.ds(first, rows)
                relay_dn(q, first, rows, slot).wait_recv()
                s3[q, pl.ds(256 + first, rows)] = (hold[s, part] + rr[q, part].astype(F32)).astype(BF16)
                final_dn(q, 256 + first, rows)

            parts_of(t, add)

    calls = {
        "gram": lambda: gram(1), "yl": first_steps, "yf": lambda q: first_far(3, q), "yg": lambda q: first_far(2, q), "o": own_chunk, "ol": own_left,
        "pairs": pair.start, "pairw": pair_wait, "ring": ring, "ringend": ring_end, "szs": squares,
        "szw": squares_wait, "syw": norms_wait, "aw": scale, "acts": acts, "arel": act_relay,
    }

    def run(plan):
        for name, *args in plan:
            if name == "r":
                receive(*args)
            else:
                calls[name](*args)

    rounds = {True: [[]], False: [[]]}
    for src, plan in ((True, SOURCE), (False, OTHER)):
        for item in plan:
            if item == ("C",):
                rounds[src].append([])
            else:
                rounds[src][-1].append(item)

    run(FIRST)

    @pl.when(is_src)
    def _():
        run(rounds[True][0])

    @pl.when(jnp.logical_not(is_src))
    def _():
        run(rounds[False][0])

    def round_of(t, _):
        for src in (True, False):
            for r in range(1, 8):
                if rounds[src][r]:
                    @pl.when(jnp.logical_and(t == r, is_src == src))
                    def _():
                        run(rounds[src][r])

        consume(t)

        @pl.when(t > 1)
        def _():
            finish(t - 2)

        return 0

    lax.fori_loop(0, 8, round_of, 0)
    finish(6)
    finish(7)

    @pl.when(is_src)
    def _():
        for j in range(4):
            if ("ol", j) not in SOURCE:
                own_left(j)
        wait_bytes(gbuf.at[pl.ds(0, 2), :, c], zsend)

    @pl.when(jnp.logical_not(is_src))
    def _():
        wait_bytes(gbuf.at[pl.ds(0, 3), :, c], zsend)

    wait_bytes(gbuf.at[:, :, c], psend)

    @pl.when(steps_y == 0)
    def _():
        for q in range(NQ):
            first(q, 1 - c).wait_send()

    @pl.when(steps_y >= 1)
    def _():
        for q in range(NQ):
            first(q, 0).wait_send()
            first(q, 1).wait_send()

    pair.wait_send()
    for i in range(1, 5):
        ring_up(i).wait_send()
    for i in range(1, 4):
        ring_dn(i).wait_send()
    wait_bytes(sz.at[pl.ds(0, 7)], szsend)
    wait_bytes(sy.at[pl.ds(0, 7)], sysend)
    wait_bytes(at.at[y], asend.at[0])
    wait_bytes(at.at[y], asend.at[1])
    wait_bytes(at.at[y], afsend)
    wait_bytes(rl, rsend.at[0])
    wait_bytes(rr, rsend.at[1])

    for q in range(NQ):
        wait_bytes(fl.at[q], flrecv.at[q])
        wait_bytes(fr.at[q], frrecv.at[q])
        block = own[q] + fl[q].astype(F32) + fr[q].astype(F32)
        out_ref[pl.ds(q * W, W), :] = block.T.astype(BF16)
    wait_bytes(s1, fsend.at[0])
    wait_bytes(s3, fsend.at[1])


def local(activations, out_grads, lengths):
    dma, vmem = pltpu.SemaphoreType.DMA, pltpu.VMEM
    grams = (2, 3, 16, 128)
    scratch = [
        vmem((2, SLOT_LEN, F), BF16),
        vmem((2, SLOT_LEN, F), BF16),
        vmem((X, NQ, 2, Y, SLOT_LEN, W), BF16),
        vmem((Y, 2, F, SLOT_LEN), BF16),
        vmem((F, 2 * Y * SLOT_LEN), BF16),
        vmem((2, Z) + grams, F32),
        vmem((Z,) + grams, F32),
        vmem((Z,) + grams, F32),
        vmem((4,) + grams, F32),
        vmem((3,) + grams, F32),
        vmem((3,) + grams, F32),
        vmem((2,) + grams, F32),
        vmem((Z, 8, 128), F32),
        vmem((2 * Y, 8, 128), F32),
        vmem((3, 256, W), F32),
        vmem((NQ, F, W), F32),
        vmem((NQ, F, W), BF16),
        vmem((NQ, F, W), BF16),
        vmem((NQ, F, W), BF16),
        vmem((NQ, 256, W), BF16),
        vmem((NQ, 256, W), BF16),
        vmem((NQ, F, W), BF16),
        vmem((NQ, F, W), BF16),
        dma((2,)), dma((NQ, 2)), dma((NQ, Y)), dma((4,)), dma((4,)), dma, dma((X, 4)),
        dma, dma((X, 3)), dma((2,)), dma((2,)), dma, dma, dma,
        dma, dma, dma((4,)), dma((4,)), dma((3,)), dma((3,)), dma, dma, dma, dma,
        dma((2,)), dma((NQ, 2)), dma((NQ, 2)), dma((2,)), dma((NQ,)), dma((NQ,)),
    ]
    return pl.pallas_call(
        kernel,
        out_shape=(
            jax.ShapeDtypeStruct((F, F), BF16),
            jax.ShapeDtypeStruct((2,), F32),
        ),
        in_specs=[
            pl.BlockSpec(memory_space=pltpu.SMEM),
            pl.BlockSpec(memory_space=pl.ANY),
            pl.BlockSpec(memory_space=pl.ANY),
        ],
        out_specs=(
            pl.BlockSpec(memory_space=pltpu.VMEM),
            pl.BlockSpec(memory_space=pltpu.SMEM),
        ),
        scratch_shapes=scratch,
        compiler_params=pltpu.CompilerParams(
            collective_id=0, has_side_effects=True, vmem_limit_bytes=40 * 1024 * 1024
        ),
        cost_estimate=pl.CostEstimate(flops=2 * 512 * 512 * 8192, bytes_accessed=3 * 2**19, transcendentals=0),
    )(*(pltpu.with_memory_space_constraint(v, pltpu.HBM) for v in (lengths, activations, out_grads)))


def solution(mesh):
    placed = (P("dp", None, "tensor"), P("dp", None, "tensor"), P("dp"))
    return jax.shard_map(
        local, mesh=mesh, in_specs=placed, out_specs=(P("dp", "tensor"), P("dp")), check_vma=False
    )
```

```python
import math

import jax
import jax.numpy as jnp
from jax import lax
from jax.experimental import pallas as pl
from jax.experimental.pallas import tpu as pltpu
from jax.sharding import PartitionSpec as P

D = 8192
K = 8192
SLOT_LEN = 256
SEQS = 32
X, Y, Z = 4, 4, 8
NQ = 2
W = 256
F = 512
BOUND = math.sqrt(K * D * SLOT_LEN / 2.0)
F32 = jnp.float32
BF16 = jnp.bfloat16

FIRST = (
    ("yl",),
)
SOURCE = (
    ("yf", 0), ("gram",), ("pairs",), ("o", 0), ("pairw",), ("yf", 1), ("ring", 1), ("yg", 0), ("ring", 2),
    ("yg", 1), ("o", 1), ("acts", 3), ("ring", 3), ("acts", 1), ("o", 2), ("ring", 4), ("ringend",), ("szs",),
    ("r", 1, 2, 0), ("o", 3), ("r", 0, 2, 0), ("arel", 0), ("arel", 1), ("szw",), ("r", 1, 2, 1), ("syw",),
    ("r", 0, 2, 1), ("aw",), ("C",), ("r", 1, 2, 2), ("r", 0, 2, 2), ("C",), ("C",), ("C",), ("r", 1, 2, 3),
    ("r", 0, 2, 3), ("r", 0, 4, 0), ("C",), ("C",), ("r", 1, 4, 1), ("r", 0, 4, 2), ("C",), ("r", 1, 4, 3),
    ("C",),
)
OTHER = (
    ("yf", 0), ("gram",), ("pairs",), ("pairw",), ("ring", 1), ("yf", 1), ("yg", 0), ("ring", 2), ("acts", 3),
    ("r", 0, 1, 0), ("yg", 1), ("ring", 3), ("r", 1, 1, 0), ("acts", 1), ("ring", 4), ("r", 1, 1, 1),
    ("r", 0, 1, 1), ("arel", 0), ("ringend",), ("szs",), ("arel", 1), ("r", 1, 1, 2), ("r", 0, 1, 2),
    ("szw",), ("syw",), ("aw",), ("r", 1, 3, 0), ("C",), ("r", 1, 1, 3), ("r", 0, 1, 3), ("C",),
    ("r", 0, 3, 0), ("C",), ("C",), ("r", 1, 3, 1), ("r", 0, 3, 1), ("r", 1, 3, 2), ("r", 0, 3, 2), ("C",),
    ("r", 1, 3, 3), ("C",), ("r", 0, 3, 3), ("C",), ("C",),
)

def rcopy(src, dst, send, recv, device):
    return pltpu.make_async_remote_copy(
        src_ref=src,
        dst_ref=dst,
        send_sem=send,
        recv_sem=recv,
        device_id=device,
        device_id_type=pl.DeviceIdType.MESH,
    )


def wait_bytes(ref, sem):
    pltpu.make_async_copy(ref, ref, sem).wait()


def kernel(
    len_ref, a_hbm, g_hbm, out_ref, norm_ref,
    a_ref, g_ref, gbuf, at, ats, gpack, gpair, gsum, gup, gdn, sup, sdn, sz, sy,
    hold, own, s1, s2, s3, rl, rr, fl, fr,
    loads, ysend, yrecv, kup, kdn, zsend, zrecv, psend, precv, asend, a_near, a_other, a_far, afsend,
    gpsend, gprecv, gupsend, guprecv, gdnsend, gdnrecv, szsend, szrecv, sysend, syrecv,
    rsend, rlrecv, rrrecv, fsend, flrecv, frrecv,
):
    dp = lax.axis_index("dp")
    tn = lax.axis_index("tensor")
    x, y = lax.div(dp, Y), lax.rem(dp, Y)
    z, c = lax.div(tn, 2), lax.rem(tn, 2)

    def dev(x_, y_, z_, c_):
        return (x_ * Y + y_, z_ * 2 + c_)

    def xs(k):
        return lax.rem(x + k, X)

    def ys(k):
        return lax.rem(y + k, Y)

    def zs(k):
        return lax.rem(z + k + Z, Z)

    partner = dev(x, y, z, 1 - c)
    z_up, z_dn = dev(x, y, zs(1), c), dev(x, y, zs(-1), c)
    x_up, x_dn = dev(xs(1), y, z, c), dev(xs(3), y, z, c)
    y_up, y_dn = dev(x, ys(1), z, c), dev(x, ys(3), z, c)
    y_others = [(ys(k), c) for k in (1, 2, 3)] + [(ys(k), 1 - c) for k in (0, 1, 2, 3)]

    load_a = pltpu.make_async_copy(a_hbm, a_ref, loads.at[0])
    load_g = pltpu.make_async_copy(g_hbm, g_ref, loads.at[1])
    load_a.start()
    load_g.start()

    barrier = pltpu.get_barrier_semaphore()
    peers = [dev(x, y2, z, c2) for y2, c2 in y_others]
    peers += [dev(x, y, zs(k), c) for k in range(1, Z)] + [x_up, x_dn]
    for peer in peers:
        pl.semaphore_signal(barrier, inc=1, device_id=peer, device_id_type=pl.DeviceIdType.MESH)
    rows = lax.broadcasted_iota(jnp.int32, (SLOT_LEN, F), 0)
    contract = (((1,), (1,)), ((), ()))
    load_a.wait()
    load_g.wait()

    def gram(s):
        am = jnp.where(rows < len_ref[s], a_ref[s].astype(F32), 0.0)
        at[y, s] = am.T.astype(BF16)
        am = am.astype(BF16)
        g = g_ref[s]
        for m, v in enumerate((am, g)):
            full = lax.dot_general(v, v, contract, preferred_element_type=F32)
            gpack[s, :, m, 0] = full[:128, :128].reshape(Z, 16, 128)
            gpack[s, :, m, 1] = full[:128, 128:].reshape(Z, 16, 128)
            gpack[s, :, m, 2] = full[128:, 128:].reshape(Z, 16, 128)
    gram(0)
    pl.semaphore_wait(barrier, len(peers))

    xb0 = lax.div(z, 2)
    yt = 2 * lax.rem(z, 2) + c
    is_src = lax.rem(z, 2) == lax.div(y, 2)
    steps_y = lax.rem(y - yt + Y, Y)

    def first(q, h):
        return rcopy(
            g_hbm.at[h, :, pl.ds(q * W, W)], gbuf.at[xb0, q, h, steps_y], ysend.at[q, h],
            yrecv.at[q, steps_y], dev(x, yt, z, h),
        )

    def first_steps():
        @pl.when(steps_y == 0)
        def _():
            for q in range(NQ):
                pltpu.make_async_copy(
                    g_hbm.at[c, :, pl.ds(q * W, W)], gbuf.at[xb0, q, c, 0], yrecv.at[q, 0]
                ).start()
                first(q, 1 - c).start()

        @pl.when(steps_y == 1)
        def _():
            for q in range(NQ):
                first(q, 0).start()
                first(q, 1).start()

    def first_far(steps, q):
        @pl.when(steps_y == steps)
        def _():
            first(q, 0).start()
            first(q, 1).start()

    pair = rcopy(gpack.at[1 - c], gpair, gpsend, gprecv, partner)

    def pair_wait():
        pair.wait_recv()
        gsum[...] = gpack[c] + gpair[...]

    def ring_up(i):
        src = gsum.at[zs(4)] if i == 1 else sup.at[i - 2]
        return rcopy(src, gup.at[i - 1], gupsend.at[i - 1], guprecv.at[i - 1], z_up)

    def ring_dn(i):
        src = gsum.at[zs(-3)] if i == 1 else sdn.at[i - 2]
        return rcopy(src, gdn.at[i - 1], gdnsend.at[i - 1], gdnrecv.at[i - 1], z_dn)

    def ring(i):
        if i > 1:
            ring_up(i - 1).wait_recv()
            sup[i - 2] = gsum[zs(5 - i)] + gup[i - 2]
        ring_up(i).start()
        if i <= 3:
            if i > 1:
                ring_dn(i - 1).wait_recv()
                sdn[i - 2] = gsum[zs(i - 4)] + gdn[i - 2]
            ring_dn(i).start()

    def ring_end():
        ring_up(4).wait_recv()
        ring_dn(3).wait_recv()
        total = gsum[z] + gup[3] + gdn[2]
        prod = total[0] * total[1]
        square = jnp.sum(prod[0] + 2.0 * prod[1] + prod[2])
        sz[z] = jnp.full((8, 128), square, F32)

    def squares():
        for k in range(1, Z):
            rcopy(sz.at[z], sz.at[z], szsend, szrecv, dev(x, y, zs(k), c)).start()

    def squares_wait():
        wait_bytes(sz.at[pl.ds(0, 7)], szrecv)
        tile = sz[0]
        for k in range(1, Z):
            tile = tile + sz[k]
        mine = y * 2 + c
        sy[mine] = tile
        for y2, c2 in y_others:
            rcopy(sy.at[mine], sy.at[mine], sysend, syrecv, dev(x, y2, z, c2)).start()

    def norms_wait():
        wait_bytes(sy.at[pl.ds(0, 7)], syrecv)

    def act(h, way):
        sem = a_near.at[h] if h == way else a_other.at[h]
        rcopy(at.at[y, h], at.at[y, h], asend.at[way], sem, (y_up, y_dn)[way]).start()

    def acts(which):
        for way in range(2):
            act(way if which == 3 else 1 - way, way)

    def act_relay(h):
        part = at.at[ys(3 - 2 * h), h]
        wait_bytes(part, a_near.at[h])
        rcopy(part, part, afsend.at[h], a_far.at[h], (y_up, y_dn)[h]).start()

    def scale():
        for h in range(2):
            wait_bytes(at.at[ys(1 + 2 * h), h], a_other.at[h])
            wait_bytes(at.at[ys(2), h], a_far.at[h])
        for h in range(2):
            norm_ref[h] = jnp.max(jnp.sqrt(sy[y * 2 + h] + 1e-6))
        for h in range(2):
            for k in range(Y):
                factor = jnp.max(jnp.minimum(1.0, BOUND / jnp.sqrt(sy[ys(k) * 2 + h] + 1e-6)))
                scaled = (at[ys(k), h].astype(F32) * factor).astype(BF16)
                ats[:, pl.ds((h * Y + k) * SLOT_LEN, SLOT_LEN)] = scaled

    def chunk(xb, j):
        return gbuf.at[xb, :, c, j] if j < 2 else gbuf.at[xb, j - 2, c, pl.ds(2, 2)]

    def to_partner(xb, j):
        part = gbuf.at[xb, :, c, pl.ds(0, 2)] if j == 1 else chunk(xb, j)
        return rcopy(part, part, psend, precv.at[xb, j - 1], partner)

    def own_chunk(j):
        part = chunk(xb0, j)
        if j < 2:
            for q in range(NQ):
                wait_bytes(gbuf.at[xb0, q, c, j], yrecv.at[q, j])
        else:
            for k in (2, 3):
                wait_bytes(gbuf.at[xb0, j - 2, c, k], yrecv.at[j - 2, k])
        rcopy(part, part, kup.at[j], zrecv.at[xb0, j], z_up).start()
        rcopy(part, part, kdn.at[j], zrecv.at[xb0, j], z_dn).start()
        if j > 0:
            to_partner(xb0, j).start()

    def own_left(j):
        wait_bytes(chunk(xb0, j), kup.at[j])
        wait_bytes(chunk(xb0, j), kdn.at[j])

    def receive(side, d, j):
        xb = lax.div(zs(-d if side == 0 else d), 2)
        part = chunk(xb, j)
        wait_bytes(part, zrecv.at[xb, j])
        if d < 3 or (d == 3 and j % 2 == side):
            rcopy(part, part, zsend, zrecv.at[xb, j], (z_up, z_dn)[side]).start()
        if j > 0:
            to_partner(xb, j).start()

    def info(t):
        q_s = jnp.where(t < 2, t, jnp.where(t < 6, lax.div(t - 2, 2), t - 6))
        d_s = jnp.where(t < 2, 0, jnp.where(t < 6, 2, 4))
        q = jnp.where(is_src, q_s, lax.rem(lax.div(t, 2), 2))
        d = jnp.where(is_src, d_s, jnp.where(t < 4, 1, 3))
        z_from = lax.rem(jnp.where(lax.rem(t, 2) == 0, z + Z - d, z + d), Z)
        return lax.div(z_from, 2), q

    def relay_up(q, first, rows, slot):
        part = pl.ds(first, rows)
        return rcopy(s2.at[q, part], rl.at[q, part], rsend.at[0], rlrecv.at[q, slot], x_up)

    def relay_dn(q, first, rows, slot):
        return rcopy(
            s2.at[q, pl.ds(256 + first, rows)], rr.at[q, pl.ds(first, rows)], rsend.at[1],
            rrrecv.at[q, slot], x_dn,
        )

    def final_up(q, first, rows):
        part = pl.ds(first, rows)
        rcopy(s1.at[q, part], fl.at[q, part], fsend.at[0], flrecv.at[q], x_up).start()

    def final_dn(q, first, rows):
        part = pl.ds(first, rows)
        rcopy(s3.at[q, part], fr.at[q, part], fsend.at[1], frrecv.at[q], x_dn).start()

    def parts_of(t, run_part):
        @pl.when(t < 6)
        def _():
            run_part(0, 256, 0)

        @pl.when(t >= 6)
        def _():
            run_part(0, 128, 0)
            run_part(128, 128, 1)

    def consume(t):
        xb, q = info(t)

        @pl.when(q == 0)
        def _():
            wait_bytes(gbuf.at[xb, :, 1 - c, pl.ds(0, 2)], precv.at[xb, 0])

        wait_bytes(gbuf.at[xb, q, 1 - c, pl.ds(2, 2)], precv.at[xb, 1 + q])
        both = gbuf[xb, q].reshape(2 * Y * SLOT_LEN, W)
        part = jnp.dot(ats[...], both, preferred_element_type=F32) * (1.0 / SEQS)
        o = lax.rem(xb + X - x, X)

        @pl.when(o == 0)
        def _():
            own[q] = part

        @pl.when(o == 2)
        def _():
            s2[q] = part.astype(BF16)

            def send(first, rows, slot):
                relay_up(q, first, rows, slot).start()
                relay_dn(q, first, rows, slot).start()

            parts_of(t, send)

        @pl.when(o == 1)
        def _():
            s1[q, pl.ds(256, 256)] = part[256:].astype(BF16)
            final_up(q, 256, 256)
            hold[lax.rem(t, 3)] = part[:256]

        @pl.when(o == 3)
        def _():
            s3[q, pl.ds(0, 256)] = part[:256].astype(BF16)
            final_dn(q, 0, 256)
            hold[lax.rem(t, 3)] = part[256:]

    def finish(t):
        xb, q = info(t)
        o = lax.rem(xb + X - x, X)
        s = lax.rem(t, 3)

        @pl.when(o == 1)
        def _():
            def add(first, rows, slot):
                part = pl.ds(first, rows)
                relay_up(q, first, rows, slot).wait_recv()
                s1[q, part] = (hold[s, part] + rl[q, part].astype(F32)).astype(BF16)
                final_up(q, first, rows)

            parts_of(t, add)

        @pl.when(o == 3)
        def _():
            def add(first, rows, slot):
                part = pl.ds(first, rows)
                relay_dn(q, first, rows, slot).wait_recv()
                s3[q, pl.ds(256 + first, rows)] = (hold[s, part] + rr[q, part].astype(F32)).astype(BF16)
                final_dn(q, 256 + first, rows)

            parts_of(t, add)

    calls = {
        "gram": lambda: gram(1), "yl": first_steps, "yf": lambda q: first_far(3, q), "yg": lambda q: first_far(2, q), "o": own_chunk, "ol": own_left,
        "pairs": pair.start, "pairw": pair_wait, "ring": ring, "ringend": ring_end, "szs": squares,
        "szw": squares_wait, "syw": norms_wait, "aw": scale, "acts": acts, "arel": act_relay,
    }

    def run(plan):
        for name, *args in plan:
            if name == "r":
                receive(*args)
            else:
                calls[name](*args)

    rounds = {True: [[]], False: [[]]}
    for src, plan in ((True, SOURCE), (False, OTHER)):
        for item in plan:
            if item == ("C",):
                rounds[src].append([])
            else:
                rounds[src][-1].append(item)

    run(FIRST)

    @pl.when(is_src)
    def _():
        run(rounds[True][0])

    @pl.when(jnp.logical_not(is_src))
    def _():
        run(rounds[False][0])

    def round_of(t, _):
        for src in (True, False):
            for r in range(1, 8):
                if rounds[src][r]:
                    @pl.when(jnp.logical_and(t == r, is_src == src))
                    def _():
                        run(rounds[src][r])

        consume(t)

        @pl.when(t > 1)
        def _():
            finish(t - 2)

        return 0

    lax.fori_loop(0, 8, round_of, 0)
    finish(6)
    finish(7)

    @pl.when(is_src)
    def _():
        for j in range(4):
            if ("ol", j) not in SOURCE:
                own_left(j)
        wait_bytes(gbuf.at[pl.ds(0, 2), :, c], zsend)

    @pl.when(jnp.logical_not(is_src))
    def _():
        wait_bytes(gbuf.at[pl.ds(0, 3), :, c], zsend)

    wait_bytes(gbuf.at[:, :, c], psend)

    @pl.when(steps_y == 0)
    def _():
        for q in range(NQ):
            first(q, 1 - c).wait_send()

    @pl.when(steps_y >= 1)
    def _():
        for q in range(NQ):
            first(q, 0).wait_send()
            first(q, 1).wait_send()

    pair.wait_send()
    for i in range(1, 5):
        ring_up(i).wait_send()
    for i in range(1, 4):
        ring_dn(i).wait_send()
    wait_bytes(sz.at[pl.ds(0, 7)], szsend)
    wait_bytes(sy.at[pl.ds(0, 7)], sysend)
    wait_bytes(at.at[y], asend.at[0])
    wait_bytes(at.at[y], asend.at[1])
    for h in range(2):
        wait_bytes(at.at[y, h], afsend.at[h])
    wait_bytes(rl, rsend.at[0])
    wait_bytes(rr, rsend.at[1])

    for q in range(NQ):
        wait_bytes(fl.at[q], flrecv.at[q])
        wait_bytes(fr.at[q], frrecv.at[q])
        block = own[q] + fl[q].astype(F32) + fr[q].astype(F32)
        out_ref[pl.ds(q * W, W), :] = block.T.astype(BF16)
    wait_bytes(s1, fsend.at[0])
    wait_bytes(s3, fsend.at[1])


def local(activations, out_grads, lengths):
    dma, vmem = pltpu.SemaphoreType.DMA, pltpu.VMEM
    grams = (2, 3, 16, 128)
    scratch = [
        vmem((2, SLOT_LEN, F), BF16),
        vmem((2, SLOT_LEN, F), BF16),
        vmem((X, NQ, 2, Y, SLOT_LEN, W), BF16),
        vmem((Y, 2, F, SLOT_LEN), BF16),
        vmem((F, 2 * Y * SLOT_LEN), BF16),
        vmem((2, Z) + grams, F32),
        vmem((Z,) + grams, F32),
        vmem((Z,) + grams, F32),
        vmem((4,) + grams, F32),
        vmem((3,) + grams, F32),
        vmem((3,) + grams, F32),
        vmem((2,) + grams, F32),
        vmem((Z, 8, 128), F32),
        vmem((2 * Y, 8, 128), F32),
        vmem((3, 256, W), F32),
        vmem((NQ, F, W), F32),
        vmem((NQ, F, W), BF16),
        vmem((NQ, F, W), BF16),
        vmem((NQ, F, W), BF16),
        vmem((NQ, 256, W), BF16),
        vmem((NQ, 256, W), BF16),
        vmem((NQ, F, W), BF16),
        vmem((NQ, F, W), BF16),
        dma((2,)), dma((NQ, 2)), dma((NQ, Y)), dma((4,)), dma((4,)), dma, dma((X, 4)),
        dma, dma((X, 3)), dma((2,)), dma((2,)), dma((2,)), dma((2,)), dma((2,)),
        dma, dma, dma((4,)), dma((4,)), dma((3,)), dma((3,)), dma, dma, dma, dma,
        dma((2,)), dma((NQ, 2)), dma((NQ, 2)), dma((2,)), dma((NQ,)), dma((NQ,)),
    ]
    return pl.pallas_call(
        kernel,
        out_shape=(
            jax.ShapeDtypeStruct((F, F), BF16),
            jax.ShapeDtypeStruct((2,), F32),
        ),
        in_specs=[
            pl.BlockSpec(memory_space=pltpu.SMEM),
            pl.BlockSpec(memory_space=pl.ANY),
            pl.BlockSpec(memory_space=pl.ANY),
        ],
        out_specs=(
            pl.BlockSpec(memory_space=pltpu.VMEM),
            pl.BlockSpec(memory_space=pltpu.SMEM),
        ),
        scratch_shapes=scratch,
        compiler_params=pltpu.CompilerParams(
            collective_id=0, has_side_effects=True, vmem_limit_bytes=40 * 1024 * 1024
        ),
        cost_estimate=pl.CostEstimate(flops=2 * 512 * 512 * 8192, bytes_accessed=3 * 2**19, transcendentals=0),
    )(*(pltpu.with_memory_space_constraint(v, pltpu.HBM) for v in (lengths, activations, out_grads)))


def solution(mesh):
    placed = (P("dp", None, "tensor"), P("dp", None, "tensor"), P("dp"))
    return jax.shard_map(
        local, mesh=mesh, in_specs=placed, out_specs=(P("dp", "tensor"), P("dp")), check_vma=False
    )
```

```python
import math

import jax
import jax.numpy as jnp
from jax import lax
from jax.experimental import pallas as pl
from jax.experimental.pallas import tpu as pltpu
from jax.sharding import PartitionSpec as P

D = 8192
K = 8192
SLOT_LEN = 256
SEQS = 32
X, Y, Z = 4, 4, 8
NQ = 2
W = 256
F = 512
BOUND = math.sqrt(K * D * SLOT_LEN / 2.0)
F32 = jnp.float32
BF16 = jnp.bfloat16

FIRST = (
    ("yl",),
)
SOURCE = (
    ("gram",), ("pairs",), ("o", 0), ("yf", 0), ("pairw",), ("yf", 1), ("yg", 0), ("ring", 1), ("acts", 1),
    ("acts", 3), ("ring", 2), ("o", 1), ("ring", 3), ("o", 2), ("ring", 4), ("yg", 1), ("ringend",), ("szs",),
    ("r", 1, 2, 0), ("r", 0, 2, 0), ("o", 3), ("arel", 0), ("arel", 1), ("szw",), ("r", 1, 2, 1), ("syw",),
    ("aw",), ("r", 0, 2, 1), ("C",), ("r", 1, 2, 2), ("r", 0, 2, 2), ("C",), ("C",), ("C",), ("r", 1, 2, 3),
    ("r", 0, 2, 3), ("r", 0, 4, 0), ("C",), ("C",), ("r", 1, 4, 1), ("r", 0, 4, 2), ("E", 6), ("C",),
    ("E", 7), ("r", 1, 4, 3), ("C",),
)
OTHER = (
    ("yf", 0), ("gram",), ("pairs",), ("pairw",), ("ring", 1), ("yg", 0), ("ring", 2), ("acts", 3), ("yf", 1),
    ("r", 0, 1, 0), ("yg", 1), ("ring", 3), ("r", 1, 1, 0), ("acts", 1), ("ring", 4), ("r", 1, 1, 1),
    ("r", 0, 1, 1), ("ringend",), ("arel", 0), ("arel", 1), ("szs",), ("r", 1, 1, 2), ("r", 0, 1, 2),
    ("szw",), ("syw",), ("aw",), ("C",), ("r", 1, 3, 0), ("r", 1, 1, 3), ("r", 0, 1, 3), ("C",),
    ("r", 0, 3, 0), ("C",), ("C",), ("r", 0, 3, 1), ("r", 1, 3, 1), ("r", 1, 3, 2), ("r", 0, 3, 2), ("C",),
    ("r", 1, 3, 3), ("C",), ("r", 0, 3, 3), ("E", 6), ("E", 7), ("C",), ("C",),
)

def rcopy(src, dst, send, recv, device):
    return pltpu.make_async_remote_copy(
        src_ref=src,
        dst_ref=dst,
        send_sem=send,
        recv_sem=recv,
        device_id=device,
        device_id_type=pl.DeviceIdType.MESH,
    )


def wait_bytes(ref, sem):
    pltpu.make_async_copy(ref, ref, sem).wait()


def kernel(
    len_hbm, a_hbm, g_hbm, out_ref, norm_ref,
    len_ref, a_ref, g_ref, gbuf, at, ats, gpack, gpair, gsum, gup, gdn, sup, sdn, sz, sy,
    hold, total, pre, own, s1, s2, s3, rl, rr, fl, fr,
    loads, ysend, yrecv, kup, kdn, zsend, zrecv, psend, precv, asend, a_near, a_other, a_far, afsend,
    gpsend, gprecv, gupsend, guprecv, gdnsend, gdnrecv, szsend, szrecv, sysend, syrecv,
    rsend, rlrecv, rrrecv, fsend, flrecv, frrecv,
):
    dp = lax.axis_index("dp")
    tn = lax.axis_index("tensor")
    x, y = lax.div(dp, Y), lax.rem(dp, Y)
    z, c = lax.div(tn, 2), lax.rem(tn, 2)

    def dev(x_, y_, z_, c_):
        return (x_ * Y + y_, z_ * 2 + c_)

    def xs(k):
        return lax.rem(x + k, X)

    def ys(k):
        return lax.rem(y + k, Y)

    def zs(k):
        return lax.rem(z + k + Z, Z)

    partner = dev(x, y, z, 1 - c)
    z_up, z_dn = dev(x, y, zs(1), c), dev(x, y, zs(-1), c)
    x_up, x_dn = dev(xs(1), y, z, c), dev(xs(3), y, z, c)
    y_up, y_dn = dev(x, ys(1), z, c), dev(x, ys(3), z, c)
    y_others = [(ys(k), c) for k in (1, 2, 3)] + [(ys(k), 1 - c) for k in (0, 1, 2, 3)]

    load_a = pltpu.make_async_copy(a_hbm, a_ref, loads.at[0])
    load_g = pltpu.make_async_copy(g_hbm, g_ref, loads.at[1])
    load_len = pltpu.make_async_copy(len_hbm, len_ref, loads.at[2])
    load_len.start()
    load_a.start()
    load_g.start()

    barrier = pltpu.get_barrier_semaphore()
    peers = [dev(x, y2, z, c2) for y2, c2 in y_others]
    peers += [dev(x, y, zs(k), c) for k in range(1, Z)] + [x_up, x_dn]
    for peer in peers:
        pl.semaphore_signal(barrier, inc=1, device_id=peer, device_id_type=pl.DeviceIdType.MESH)
    rows = lax.broadcasted_iota(jnp.int32, (SLOT_LEN, F), 0)
    contract = (((1,), (1,)), ((), ()))
    load_len.wait()
    load_a.wait()
    load_g.wait()

    def gram(s):
        am = jnp.where(rows < len_ref[s], a_ref[s].astype(F32), 0.0)
        at[y, s] = am.T.astype(BF16)
        am = am.astype(BF16)
        g = g_ref[s]
        for m, v in enumerate((am, g)):
            full = lax.dot_general(v, v, contract, preferred_element_type=F32)
            gpack[s, :, m, 0] = full[:128, :128].reshape(Z, 16, 128)
            gpack[s, :, m, 1] = full[:128, 128:].reshape(Z, 16, 128)
            gpack[s, :, m, 2] = full[128:, 128:].reshape(Z, 16, 128)
    gram(0)
    pl.semaphore_wait(barrier, len(peers))

    xb0 = lax.div(z, 2)
    yt = 2 * lax.rem(z, 2) + c
    is_src = lax.rem(z, 2) == lax.div(y, 2)
    steps_y = lax.rem(y - yt + Y, Y)

    def first(q, h):
        return rcopy(
            g_hbm.at[h, :, pl.ds(q * W, W)], gbuf.at[xb0, q, h, steps_y], ysend.at[q, h],
            yrecv.at[q, steps_y], dev(x, yt, z, h),
        )

    def first_steps():
        @pl.when(steps_y == 0)
        def _():
            for q in range(NQ):
                pltpu.make_async_copy(
                    g_hbm.at[c, :, pl.ds(q * W, W)], gbuf.at[xb0, q, c, 0], yrecv.at[q, 0]
                ).start()
                first(q, 1 - c).start()

        @pl.when(steps_y == 1)
        def _():
            for q in range(NQ):
                first(q, 0).start()
                first(q, 1).start()

    def first_far(steps, q):
        @pl.when(steps_y == steps)
        def _():
            first(q, 0).start()
            first(q, 1).start()

    pair = rcopy(gpack.at[1 - c], gpair, gpsend, gprecv, partner)

    def pair_wait():
        pair.wait_recv()
        gsum[...] = gpack[c] + gpair[...]

    def ring_up(i):
        src = gsum.at[zs(4)] if i == 1 else sup.at[i - 2]
        return rcopy(src, gup.at[i - 1], gupsend.at[i - 1], guprecv.at[i - 1], z_up)

    def ring_dn(i):
        src = gsum.at[zs(-3)] if i == 1 else sdn.at[i - 2]
        return rcopy(src, gdn.at[i - 1], gdnsend.at[i - 1], gdnrecv.at[i - 1], z_dn)

    def ring(i):
        if i > 1:
            ring_up(i - 1).wait_recv()
            sup[i - 2] = gsum[zs(5 - i)] + gup[i - 2]
        ring_up(i).start()
        if i <= 3:
            if i > 1:
                ring_dn(i - 1).wait_recv()
                sdn[i - 2] = gsum[zs(i - 4)] + gdn[i - 2]
            ring_dn(i).start()

    def ring_end():
        ring_up(4).wait_recv()
        ring_dn(3).wait_recv()
        total = gsum[z] + gup[3] + gdn[2]
        prod = total[0] * total[1]
        square = jnp.sum(prod[0] + 2.0 * prod[1] + prod[2])
        sz[z] = jnp.full((8, 128), square, F32)

    def squares():
        for k in range(1, Z):
            rcopy(sz.at[z], sz.at[z], szsend, szrecv, dev(x, y, zs(k), c)).start()

    def squares_wait():
        wait_bytes(sz.at[pl.ds(0, 7)], szrecv)
        tile = sz[0]
        for k in range(1, Z):
            tile = tile + sz[k]
        mine = y * 2 + c
        sy[mine] = tile
        for y2, c2 in y_others:
            rcopy(sy.at[mine], sy.at[mine], sysend, syrecv, dev(x, y2, z, c2)).start()

    def norms_wait():
        wait_bytes(sy.at[pl.ds(0, 7)], syrecv)

    def act(h, way):
        sem = a_near.at[h] if h == way else a_other.at[h]
        rcopy(at.at[y, h], at.at[y, h], asend.at[way], sem, (y_up, y_dn)[way]).start()

    def acts(which):
        for way in range(2):
            act(way if which == 3 else 1 - way, way)

    def act_relay(h):
        part = at.at[ys(3 - 2 * h), h]
        wait_bytes(part, a_near.at[h])
        rcopy(part, part, afsend.at[h], a_far.at[h], (y_up, y_dn)[h]).start()

    def scale():
        for h in range(2):
            wait_bytes(at.at[ys(1 + 2 * h), h], a_other.at[h])
            wait_bytes(at.at[ys(2), h], a_far.at[h])
        for h in range(2):
            norm_ref[h] = jnp.max(jnp.sqrt(sy[y * 2 + h] + 1e-6))
        for h in range(2):
            for k in range(Y):
                factor = jnp.max(jnp.minimum(1.0, BOUND / jnp.sqrt(sy[ys(k) * 2 + h] + 1e-6)))
                scaled = (at[ys(k), h].astype(F32) * factor).astype(BF16)
                ats[h, :, pl.ds(k * SLOT_LEN, SLOT_LEN)] = scaled

    def chunk(xb, j):
        return gbuf.at[xb, :, c, j] if j < 2 else gbuf.at[xb, j - 2, c, pl.ds(2, 2)]

    def to_partner(xb, j):
        part = gbuf.at[xb, :, c, pl.ds(0, 2)] if j == 1 else chunk(xb, j)
        return rcopy(part, part, psend, precv.at[xb, j - 1], partner)

    def own_chunk(j):
        part = chunk(xb0, j)
        if j < 2:
            for q in range(NQ):
                wait_bytes(gbuf.at[xb0, q, c, j], yrecv.at[q, j])
        else:
            for k in (2, 3):
                wait_bytes(gbuf.at[xb0, j - 2, c, k], yrecv.at[j - 2, k])
        rcopy(part, part, kup.at[j], zrecv.at[xb0, j], z_up).start()
        rcopy(part, part, kdn.at[j], zrecv.at[xb0, j], z_dn).start()
        if j > 0:
            to_partner(xb0, j).start()

    def own_left(j):
        wait_bytes(chunk(xb0, j), kup.at[j])
        wait_bytes(chunk(xb0, j), kdn.at[j])

    def receive(side, d, j):
        xb = lax.div(zs(-d if side == 0 else d), 2)
        part = chunk(xb, j)
        wait_bytes(part, zrecv.at[xb, j])
        if d < 3 or (d == 3 and j % 2 == side):
            rcopy(part, part, zsend, zrecv.at[xb, j], (z_up, z_dn)[side]).start()
        if j > 0:
            to_partner(xb, j).start()

    def info(t):
        q_s = jnp.where(t < 2, t, jnp.where(t < 6, lax.div(t - 2, 2), t - 6))
        d_s = jnp.where(t < 2, 0, jnp.where(t < 6, 2, 4))
        q = jnp.where(is_src, q_s, lax.rem(lax.div(t, 2), 2))
        d = jnp.where(is_src, d_s, jnp.where(t < 4, 1, 3))
        z_from = lax.rem(jnp.where(lax.rem(t, 2) == 0, z + Z - d, z + d), Z)
        return lax.div(z_from, 2), q

    def relay_up(q, first, rows, slot):
        part = pl.ds(first, rows)
        return rcopy(s2.at[q, part], rl.at[q, part], rsend.at[0], rlrecv.at[q, slot], x_up)

    def relay_dn(q, first, rows, slot):
        return rcopy(
            s2.at[q, pl.ds(256 + first, rows)], rr.at[q, pl.ds(first, rows)], rsend.at[1],
            rrrecv.at[q, slot], x_dn,
        )

    def final_up(q, first, rows):
        part = pl.ds(first, rows)
        rcopy(s1.at[q, part], fl.at[q, part], fsend.at[0], flrecv.at[q], x_up).start()

    def final_dn(q, first, rows):
        part = pl.ds(first, rows)
        rcopy(s3.at[q, part], fr.at[q, part], fsend.at[1], frrecv.at[q], x_dn).start()

    def parts_of(t, run_part):
        @pl.when(t < 6)
        def _():
            run_part(0, 256, 0)

        @pl.when(t >= 6)
        def _():
            run_part(0, 128, 0)
            run_part(128, 128, 1)

    def product(xb, q, core, slot, slots):
        rows = gbuf[xb, q, core, pl.ds(slot, slots)].reshape(slots * SLOT_LEN, W)
        cols = ats[core, :, pl.ds(slot * SLOT_LEN, slots * SLOT_LEN)]
        return jnp.dot(cols, rows, preferred_element_type=F32)

    def others(xb, j):
        part = gbuf.at[xb, :, 1 - c, pl.ds(0, 2)] if j == 0 else gbuf.at[xb, j - 1, 1 - c, pl.ds(2, 2)]
        wait_bytes(part, precv.at[xb, j])

    def others_last(xb, q):
        wait_bytes(gbuf.at[xb, q, 1 - c, pl.ds(2, 2)], precv.at[xb, 1 + q])

    def ahead(t):
        xb, q = info(t)
        if t == 6:
            @pl.when(is_src)
            def _():
                others(xb, 0)

        pre[t - 6] = product(xb, q, c, 0, 2) + product(xb, q, 1 - c, 0, 2)

    def consume(t):
        xb, q = info(t)

        @pl.when(t < 6)
        def _():
            total[...] = product(xb, q, c, 0, 4)

            @pl.when(q == 0)
            def _():
                others(xb, 0)

            others_last(xb, q)
            total[...] = (total[...] + product(xb, q, 1 - c, 0, 4)) * (1.0 / SEQS)

        @pl.when(t >= 6)
        def _():
            late = lax.max(t - 6, 0)
            total[...] = pre[late] + product(xb, q, c, 2, 2)
            others_last(xb, q)
            total[...] = (total[...] + product(xb, q, 1 - c, 2, 2)) * (1.0 / SEQS)

        o = lax.rem(xb + X - x, X)

        @pl.when(o == 0)
        def _():
            own[q] = total[...]

        @pl.when(o == 2)
        def _():
            s2[q] = total[...].astype(BF16)

            def send(first, rows, slot):
                relay_up(q, first, rows, slot).start()
                relay_dn(q, first, rows, slot).start()

            parts_of(t, send)

        @pl.when(o == 1)
        def _():
            s1[q, pl.ds(256, 256)] = total[pl.ds(256, 256)].astype(BF16)
            final_up(q, 256, 256)
            hold[lax.rem(t, 3)] = total[pl.ds(0, 256)]

        @pl.when(o == 3)
        def _():
            s3[q, pl.ds(0, 256)] = total[pl.ds(0, 256)].astype(BF16)
            final_dn(q, 0, 256)
            hold[lax.rem(t, 3)] = total[pl.ds(256, 256)]

    def finish(t):
        xb, q = info(t)
        o = lax.rem(xb + X - x, X)
        s = lax.rem(t, 3)

        @pl.when(o == 1)
        def _():
            def add(first, rows, slot):
                part = pl.ds(first, rows)
                relay_up(q, first, rows, slot).wait_recv()
                s1[q, part] = (hold[s, part] + rl[q, part].astype(F32)).astype(BF16)
                final_up(q, first, rows)

            parts_of(t, add)

        @pl.when(o == 3)
        def _():
            def add(first, rows, slot):
                part = pl.ds(first, rows)
                relay_dn(q, first, rows, slot).wait_recv()
                s3[q, pl.ds(256 + first, rows)] = (hold[s, part] + rr[q, part].astype(F32)).astype(BF16)
                final_dn(q, 256 + first, rows)

            parts_of(t, add)

    calls = {
        "gram": lambda: gram(1), "E": ahead, "yl": first_steps, "yf": lambda q: first_far(3, q), "yg": lambda q: first_far(2, q), "o": own_chunk, "ol": own_left,
        "pairs": pair.start, "pairw": pair_wait, "ring": ring, "ringend": ring_end, "szs": squares,
        "szw": squares_wait, "syw": norms_wait, "aw": scale, "acts": acts, "arel": act_relay,
    }

    def run(plan):
        for name, *args in plan:
            if name == "r":
                receive(*args)
            else:
                calls[name](*args)

    rounds = {True: [[]], False: [[]]}
    for src, plan in ((True, SOURCE), (False, OTHER)):
        for item in plan:
            if item == ("C",):
                rounds[src].append([])
            else:
                rounds[src][-1].append(item)

    run(FIRST)

    @pl.when(is_src)
    def _():
        run(rounds[True][0])

    @pl.when(jnp.logical_not(is_src))
    def _():
        run(rounds[False][0])

    def round_of(t, _):
        for src in (True, False):
            for r in range(1, 8):
                if rounds[src][r]:
                    @pl.when(jnp.logical_and(t == r, is_src == src))
                    def _():
                        run(rounds[src][r])

        consume(t)

        @pl.when(t > 1)
        def _():
            finish(t - 2)

        return 0

    lax.fori_loop(0, 8, round_of, 0)
    finish(6)
    finish(7)

    @pl.when(is_src)
    def _():
        for j in range(4):
            if ("ol", j) not in SOURCE:
                own_left(j)
        wait_bytes(gbuf.at[pl.ds(0, 2), :, c], zsend)

    @pl.when(jnp.logical_not(is_src))
    def _():
        wait_bytes(gbuf.at[pl.ds(0, 3), :, c], zsend)

    wait_bytes(gbuf.at[:, :, c], psend)

    @pl.when(steps_y == 0)
    def _():
        for q in range(NQ):
            first(q, 1 - c).wait_send()

    @pl.when(steps_y >= 1)
    def _():
        for q in range(NQ):
            first(q, 0).wait_send()
            first(q, 1).wait_send()

    pair.wait_send()
    for i in range(1, 5):
        ring_up(i).wait_send()
    for i in range(1, 4):
        ring_dn(i).wait_send()
    wait_bytes(sz.at[pl.ds(0, 7)], szsend)
    wait_bytes(sy.at[pl.ds(0, 7)], sysend)
    wait_bytes(at.at[y], asend.at[0])
    wait_bytes(at.at[y], asend.at[1])
    for h in range(2):
        wait_bytes(at.at[y, h], afsend.at[h])
    wait_bytes(rl, rsend.at[0])
    wait_bytes(rr, rsend.at[1])

    for q in range(NQ):
        wait_bytes(fl.at[q], flrecv.at[q])
        wait_bytes(fr.at[q], frrecv.at[q])
        block = own[q] + fl[q].astype(F32) + fr[q].astype(F32)
        out_ref[pl.ds(q * W, W), :] = block.T.astype(BF16)
    wait_bytes(s1, fsend.at[0])
    wait_bytes(s3, fsend.at[1])


def local(activations, out_grads, lengths):
    dma, vmem = pltpu.SemaphoreType.DMA, pltpu.VMEM
    grams = (2, 3, 16, 128)
    scratch = [
        pltpu.SMEM((2,), jnp.int32),
        vmem((2, SLOT_LEN, F), BF16),
        vmem((2, SLOT_LEN, F), BF16),
        vmem((X, NQ, 2, Y, SLOT_LEN, W), BF16),
        vmem((Y, 2, F, SLOT_LEN), BF16),
        vmem((2, F, Y * SLOT_LEN), BF16),
        vmem((2, Z) + grams, F32),
        vmem((Z,) + grams, F32),
        vmem((Z,) + grams, F32),
        vmem((4,) + grams, F32),
        vmem((3,) + grams, F32),
        vmem((3,) + grams, F32),
        vmem((2,) + grams, F32),
        vmem((Z, 8, 128), F32),
        vmem((2 * Y, 8, 128), F32),
        vmem((3, 256, W), F32),
        vmem((F, W), F32),
        vmem((2, F, W), F32),
        vmem((NQ, F, W), F32),
        vmem((NQ, F, W), BF16),
        vmem((NQ, F, W), BF16),
        vmem((NQ, F, W), BF16),
        vmem((NQ, 256, W), BF16),
        vmem((NQ, 256, W), BF16),
        vmem((NQ, F, W), BF16),
        vmem((NQ, F, W), BF16),
        dma((3,)), dma((NQ, 2)), dma((NQ, Y)), dma((4,)), dma((4,)), dma, dma((X, 4)),
        dma, dma((X, 3)), dma((2,)), dma((2,)), dma((2,)), dma((2,)), dma((2,)),
        dma, dma, dma((4,)), dma((4,)), dma((3,)), dma((3,)), dma, dma, dma, dma,
        dma((2,)), dma((NQ, 2)), dma((NQ, 2)), dma((2,)), dma((NQ,)), dma((NQ,)),
    ]
    return pl.pallas_call(
        kernel,
        out_shape=(
            jax.ShapeDtypeStruct((F, F), BF16),
            jax.ShapeDtypeStruct((2,), F32),
        ),
        in_specs=[
            pl.BlockSpec(memory_space=pl.ANY),
            pl.BlockSpec(memory_space=pl.ANY),
            pl.BlockSpec(memory_space=pl.ANY),
        ],
        out_specs=(
            pl.BlockSpec(memory_space=pltpu.VMEM),
            pl.BlockSpec(memory_space=pltpu.SMEM),
        ),
        scratch_shapes=scratch,
        compiler_params=pltpu.CompilerParams(
            collective_id=0, has_side_effects=True, vmem_limit_bytes=40 * 1024 * 1024
        ),
        cost_estimate=pl.CostEstimate(flops=2 * 512 * 512 * 8192, bytes_accessed=3 * 2**19, transcendentals=0),
    )(*(pltpu.with_memory_space_constraint(v, pltpu.HBM) for v in (lengths, activations, out_grads)))


def solution(mesh):
    placed = (P("dp", None, "tensor"), P("dp", None, "tensor"), P("dp"))
    return jax.shard_map(
        local, mesh=mesh, in_specs=placed, out_specs=(P("dp", "tensor"), P("dp")), check_vma=False
    )
```

```python
import math

import jax
import jax.numpy as jnp
from jax import lax
from jax.experimental import pallas as pl
from jax.experimental.pallas import tpu as pltpu
from jax.sharding import PartitionSpec as P

D = 8192
K = 8192
SLOT_LEN = 256
SEQS = 32
X, Y, Z = 4, 4, 8
NQ = 2
W = 256
F = 512
BOUND = math.sqrt(K * D * SLOT_LEN / 2.0)
F32 = jnp.float32
BF16 = jnp.bfloat16

FIRST = (
    ("yl",),
)
SOURCE = (
    ("yf", 0), ("gram",), ("pairs",), ("o", 0), ("pairw",), ("yf", 1), ("ring", 1), ("yg", 0), ("ring", 2),
    ("o", 1), ("yg", 1), ("acts", 3), ("ring", 3), ("o", 2), ("ring", 4), ("acts", 1), ("ringend",),
    ("arel", 1), ("szs",), ("r", 1, 2, 0), ("o", 3), ("arel", 0), ("r", 0, 2, 0), ("szw",), ("r", 1, 2, 1),
    ("syw",), ("aw",), ("r", 0, 2, 1), ("r", 1, 2, 2), ("r", 0, 2, 2), ("C",), ("C",), ("C",), ("r", 1, 2, 3),
    ("C",), ("r", 0, 2, 3), ("r", 0, 4, 0), ("C",), ("r", 1, 4, 1), ("C",), ("r", 0, 4, 2), ("E", 6),
    ("E", 7), ("C",), ("r", 1, 4, 3), ("C",),
)
OTHER = (
    ("yf", 0), ("gram",), ("pairs",), ("pairw",), ("ring", 1), ("yf", 1), ("yg", 0), ("ring", 2), ("acts", 3),
    ("r", 0, 1, 0), ("yg", 1), ("ring", 3), ("r", 1, 1, 0), ("acts", 1), ("ring", 4), ("r", 1, 1, 1),
    ("r", 0, 1, 1), ("arel", 0), ("ringend",), ("szs",), ("arel", 1), ("r", 1, 1, 2), ("r", 0, 1, 2),
    ("szw",), ("syw",), ("aw",), ("C",), ("r", 1, 1, 3), ("r", 0, 1, 3), ("r", 0, 3, 0), ("r", 1, 3, 0),
    ("C",), ("C",), ("C",), ("r", 1, 3, 1), ("r", 0, 3, 1), ("r", 1, 3, 2), ("r", 0, 3, 2), ("C",),
    ("r", 1, 3, 3), ("C",), ("E", 6), ("r", 0, 3, 3), ("E", 7), ("C",), ("C",),
)

def rcopy(src, dst, send, recv, device):
    return pltpu.make_async_remote_copy(
        src_ref=src,
        dst_ref=dst,
        send_sem=send,
        recv_sem=recv,
        device_id=device,
        device_id_type=pl.DeviceIdType.MESH,
    )


def wait_bytes(ref, sem):
    pltpu.make_async_copy(ref, ref, sem).wait()


def kernel(
    len_hbm, a_hbm, g_hbm, out_ref, norm_ref,
    len_ref, a_ref, g_ref, gbuf, at, ats, gpack, gpair, gsum, gup, gdn, sup, sdn, sz, sy,
    hold, total, pre, own, s1, s2, s3, rl, rr, fl, fr,
    loads, ysend, yrecv, kup, kdn, zsend, zrecv, psend, precv, asend, a_near, a_other, a_far, afsend,
    gpsend, gprecv, gupsend, guprecv, gdnsend, gdnrecv, szsend, szrecv, sysend, syrecv,
    rsend, rlrecv, rrrecv, fsend, flrecv, frrecv,
):
    dp = lax.axis_index("dp")
    tn = lax.axis_index("tensor")
    x, y = lax.div(dp, Y), lax.rem(dp, Y)
    z, c = lax.div(tn, 2), lax.rem(tn, 2)

    def dev(x_, y_, z_, c_):
        return (x_ * Y + y_, z_ * 2 + c_)

    def xs(k):
        return lax.rem(x + k, X)

    def ys(k):
        return lax.rem(y + k, Y)

    def zs(k):
        return lax.rem(z + k + Z, Z)

    partner = dev(x, y, z, 1 - c)
    z_up, z_dn = dev(x, y, zs(1), c), dev(x, y, zs(-1), c)
    x_up, x_dn = dev(xs(1), y, z, c), dev(xs(3), y, z, c)
    y_up, y_dn = dev(x, ys(1), z, c), dev(x, ys(3), z, c)
    y_others = [(ys(k), c) for k in (1, 2, 3)] + [(ys(k), 1 - c) for k in (0, 1, 2, 3)]

    load_a = pltpu.make_async_copy(a_hbm, a_ref, loads.at[0])
    load_g = pltpu.make_async_copy(g_hbm, g_ref, loads.at[1])
    load_len = pltpu.make_async_copy(len_hbm, len_ref, loads.at[2])
    load_len.start()
    load_a.start()
    load_g.start()

    barrier = pltpu.get_barrier_semaphore()
    peers = [dev(x, y2, z, c2) for y2, c2 in y_others]
    peers += [dev(x, y, zs(k), c) for k in range(1, Z)] + [x_up, x_dn]
    for peer in peers:
        pl.semaphore_signal(barrier, inc=1, device_id=peer, device_id_type=pl.DeviceIdType.MESH)
    rows = lax.broadcasted_iota(jnp.int32, (SLOT_LEN, F), 0)
    contract = (((1,), (1,)), ((), ()))
    load_len.wait()
    load_a.wait()
    load_g.wait()

    def gram(s):
        am = jnp.where(rows < len_ref[s], a_ref[s].astype(F32), 0.0)
        at[y, s] = am.T.astype(BF16)
        am = am.astype(BF16)
        g = g_ref[s]
        for m, v in enumerate((am, g)):
            full = lax.dot_general(v, v, contract, preferred_element_type=F32)
            gpack[s, :, m, 0] = full[:128, :128].reshape(Z, 16, 128)
            gpack[s, :, m, 1] = full[:128, 128:].reshape(Z, 16, 128)
            gpack[s, :, m, 2] = full[128:, 128:].reshape(Z, 16, 128)
    gram(0)
    pl.semaphore_wait(barrier, len(peers))

    xb0 = lax.div(z, 2)
    yt = 2 * lax.rem(z, 2) + c
    is_src = lax.rem(z, 2) == lax.div(y, 2)
    steps_y = lax.rem(y - yt + Y, Y)

    def first(q, h):
        return rcopy(
            g_hbm.at[h, :, pl.ds(q * W, W)], gbuf.at[xb0, q, h, steps_y], ysend.at[q, h],
            yrecv.at[q, steps_y], dev(x, yt, z, h),
        )

    def first_steps():
        @pl.when(steps_y == 0)
        def _():
            for q in range(NQ):
                pltpu.make_async_copy(
                    g_hbm.at[c, :, pl.ds(q * W, W)], gbuf.at[xb0, q, c, 0], yrecv.at[q, 0]
                ).start()
                first(q, 1 - c).start()

        @pl.when(steps_y == 1)
        def _():
            for q in range(NQ):
                first(q, 0).start()
                first(q, 1).start()

    def first_far(steps, q):
        @pl.when(steps_y == steps)
        def _():
            first(q, 0).start()
            first(q, 1).start()

    pair = rcopy(gpack.at[1 - c], gpair, gpsend, gprecv, partner)

    def pair_wait():
        pair.wait_recv()
        gsum[...] = gpack[c] + gpair[...]

    def ring_up(i):
        src = gsum.at[zs(4)] if i == 1 else sup.at[i - 2]
        return rcopy(src, gup.at[i - 1], gupsend.at[i - 1], guprecv.at[i - 1], z_up)

    def ring_dn(i):
        src = gsum.at[zs(-3)] if i == 1 else sdn.at[i - 2]
        return rcopy(src, gdn.at[i - 1], gdnsend.at[i - 1], gdnrecv.at[i - 1], z_dn)

    def ring(i):
        if i > 1:
            ring_up(i - 1).wait_recv()
            sup[i - 2] = gsum[zs(5 - i)] + gup[i - 2]
        ring_up(i).start()
        if i <= 3:
            if i > 1:
                ring_dn(i - 1).wait_recv()
                sdn[i - 2] = gsum[zs(i - 4)] + gdn[i - 2]
            ring_dn(i).start()

    def ring_end():
        ring_up(4).wait_recv()
        ring_dn(3).wait_recv()
        total = gsum[z] + gup[3] + gdn[2]
        prod = total[0] * total[1]
        square = jnp.sum(prod[0] + 2.0 * prod[1] + prod[2])
        sz[z] = jnp.full((8, 128), square, F32)

    def squares():
        for k in range(1, Z):
            rcopy(sz.at[z], sz.at[z], szsend, szrecv, dev(x, y, zs(k), c)).start()

    def squares_wait():
        wait_bytes(sz.at[pl.ds(0, 7)], szrecv)
        tile = sz[0]
        for k in range(1, Z):
            tile = tile + sz[k]
        mine = y * 2 + c
        sy[mine] = tile
        for y2, c2 in y_others:
            rcopy(sy.at[mine], sy.at[mine], sysend, syrecv, dev(x, y2, z, c2)).start()

    def norms_wait():
        wait_bytes(sy.at[pl.ds(0, 7)], syrecv)

    def act(h, way):
        sem = a_near.at[h] if h == way else a_other.at[h]
        rcopy(at.at[y, h], at.at[y, h], asend.at[way], sem, (y_up, y_dn)[way]).start()

    def acts(which):
        for way in range(2):
            act(way if which == 3 else 1 - way, way)

    def act_relay(h):
        part = at.at[ys(3 - 2 * h), h]
        wait_bytes(part, a_near.at[h])
        rcopy(part, part, afsend.at[h], a_far.at[h], (y_up, y_dn)[h]).start()

    def scale():
        for h in range(2):
            wait_bytes(at.at[ys(1 + 2 * h), h], a_other.at[h])
            wait_bytes(at.at[ys(2), h], a_far.at[h])
        for h in range(2):
            norm_ref[h] = jnp.max(jnp.sqrt(sy[y * 2 + h] + 1e-6))
        for h in range(2):
            for k in range(Y):
                factor = jnp.max(jnp.minimum(1.0, BOUND / jnp.sqrt(sy[ys(k) * 2 + h] + 1e-6)))
                scaled = (at[ys(k), h].astype(F32) * factor).astype(BF16)
                ats[h, :, pl.ds(k * SLOT_LEN, SLOT_LEN)] = scaled

    def chunk(xb, j):
        return gbuf.at[xb, :, c, j] if j < 2 else gbuf.at[xb, j - 2, c, pl.ds(2, 2)]

    def to_partner(xb, j):
        part = gbuf.at[xb, :, c, pl.ds(0, 2)] if j == 1 else chunk(xb, j)
        return rcopy(part, part, psend, precv.at[xb, j - 1], partner)

    def own_chunk(j):
        part = chunk(xb0, j)
        if j < 2:
            for q in range(NQ):
                wait_bytes(gbuf.at[xb0, q, c, j], yrecv.at[q, j])
        else:
            for k in (2, 3):
                wait_bytes(gbuf.at[xb0, j - 2, c, k], yrecv.at[j - 2, k])
        rcopy(part, part, kup.at[j], zrecv.at[xb0, j], z_up).start()
        rcopy(part, part, kdn.at[j], zrecv.at[xb0, j], z_dn).start()
        if j > 0:
            to_partner(xb0, j).start()

    def own_left(j):
        wait_bytes(chunk(xb0, j), kup.at[j])
        wait_bytes(chunk(xb0, j), kdn.at[j])

    def receive(side, d, j):
        xb = lax.div(zs(-d if side == 0 else d), 2)
        part = chunk(xb, j)
        wait_bytes(part, zrecv.at[xb, j])
        if d < 3 or (d == 3 and j % 2 == side):
            rcopy(part, part, zsend, zrecv.at[xb, j], (z_up, z_dn)[side]).start()
        if j > 0:
            to_partner(xb, j).start()

    def info(t):
        q_s = jnp.where(t < 2, t, jnp.where(t < 6, lax.div(t - 2, 2), t - 6))
        d_s = jnp.where(t < 2, 0, jnp.where(t < 6, 2, 4))
        q = jnp.where(is_src, q_s, lax.rem(lax.div(t, 2), 2))
        d = jnp.where(is_src, d_s, jnp.where(t < 4, 1, 3))
        z_from = lax.rem(jnp.where(lax.rem(t, 2) == 0, z + Z - d, z + d), Z)
        return lax.div(z_from, 2), q

    def relay_up(q, first, rows, slot):
        part = pl.ds(first, rows)
        return rcopy(s2.at[q, part], rl.at[q, part], rsend.at[0], rlrecv.at[q, slot], x_up)

    def relay_dn(q, first, rows, slot):
        return rcopy(
            s2.at[q, pl.ds(256 + first, rows)], rr.at[q, pl.ds(first, rows)], rsend.at[1],
            rrrecv.at[q, slot], x_dn,
        )

    def final_up(q, first, rows):
        part = pl.ds(first, rows)
        rcopy(s1.at[q, part], fl.at[q, part], fsend.at[0], flrecv.at[q], x_up).start()

    def final_dn(q, first, rows):
        part = pl.ds(first, rows)
        rcopy(s3.at[q, part], fr.at[q, part], fsend.at[1], frrecv.at[q], x_dn).start()

    def parts_of(t, run_part):
        @pl.when(t < 6)
        def _():
            run_part(0, 256, 0)

        @pl.when(t >= 6)
        def _():
            run_part(0, 128, 0)
            run_part(128, 128, 1)

    def product(xb, q, core, slot, slots):
        rows = gbuf[xb, q, core, pl.ds(slot, slots)].reshape(slots * SLOT_LEN, W)
        cols = ats[core, :, pl.ds(slot * SLOT_LEN, slots * SLOT_LEN)]
        return jnp.dot(cols, rows, preferred_element_type=F32)

    def others(xb, j):
        part = gbuf.at[xb, :, 1 - c, pl.ds(0, 2)] if j == 0 else gbuf.at[xb, j - 1, 1 - c, pl.ds(2, 2)]
        wait_bytes(part, precv.at[xb, j])

    def others_last(xb, q):
        wait_bytes(gbuf.at[xb, q, 1 - c, pl.ds(2, 2)], precv.at[xb, 1 + q])

    def ahead(t):
        xb, q = info(t)
        if t == 6:
            @pl.when(is_src)
            def _():
                others(xb, 0)

        pre[t - 6] = product(xb, q, c, 0, 2) + product(xb, q, 1 - c, 0, 2)

    def consume(t):
        xb, q = info(t)

        @pl.when(t < 6)
        def _():
            total[...] = product(xb, q, c, 0, 4)

            @pl.when(q == 0)
            def _():
                others(xb, 0)

            others_last(xb, q)
            total[...] = (total[...] + product(xb, q, 1 - c, 0, 4)) * (1.0 / SEQS)

        @pl.when(t >= 6)
        def _():
            late = lax.max(t - 6, 0)
            total[...] = pre[late] + product(xb, q, c, 2, 2)
            others_last(xb, q)
            total[...] = (total[...] + product(xb, q, 1 - c, 2, 2)) * (1.0 / SEQS)

        o = lax.rem(xb + X - x, X)

        @pl.when(o == 0)
        def _():
            own[q] = total[...]

        @pl.when(o == 2)
        def _():
            s2[q] = total[...].astype(BF16)

            def send(first, rows, slot):
                relay_up(q, first, rows, slot).start()
                relay_dn(q, first, rows, slot).start()

            parts_of(t, send)

        @pl.when(o == 1)
        def _():
            s1[q, pl.ds(256, 256)] = total[pl.ds(256, 256)].astype(BF16)
            final_up(q, 256, 256)
            hold[lax.rem(t, 3)] = total[pl.ds(0, 256)]

        @pl.when(o == 3)
        def _():
            s3[q, pl.ds(0, 256)] = total[pl.ds(0, 256)].astype(BF16)
            final_dn(q, 0, 256)
            hold[lax.rem(t, 3)] = total[pl.ds(256, 256)]

    def finish(t):
        xb, q = info(t)
        o = lax.rem(xb + X - x, X)
        s = lax.rem(t, 3)

        @pl.when(o == 1)
        def _():
            def add(first, rows, slot):
                part = pl.ds(first, rows)
                relay_up(q, first, rows, slot).wait_recv()
                s1[q, part] = (hold[s, part] + rl[q, part].astype(F32)).astype(BF16)
                final_up(q, first, rows)

            parts_of(t, add)

        @pl.when(o == 3)
        def _():
            def add(first, rows, slot):
                part = pl.ds(first, rows)
                relay_dn(q, first, rows, slot).wait_recv()
                s3[q, pl.ds(256 + first, rows)] = (hold[s, part] + rr[q, part].astype(F32)).astype(BF16)
                final_dn(q, 256 + first, rows)

            parts_of(t, add)

    calls = {
        "gram": lambda: gram(1), "E": ahead, "yl": first_steps, "yf": lambda q: first_far(3, q), "yg": lambda q: first_far(2, q), "o": own_chunk, "ol": own_left,
        "pairs": pair.start, "pairw": pair_wait, "ring": ring, "ringend": ring_end, "szs": squares,
        "szw": squares_wait, "syw": norms_wait, "aw": scale, "acts": acts, "arel": act_relay,
    }

    def run(plan):
        for name, *args in plan:
            if name == "r":
                receive(*args)
            else:
                calls[name](*args)

    rounds = {True: [[]], False: [[]]}
    for src, plan in ((True, SOURCE), (False, OTHER)):
        for item in plan:
            if item == ("C",):
                rounds[src].append([])
            else:
                rounds[src][-1].append(item)

    run(FIRST)

    @pl.when(is_src)
    def _():
        run(rounds[True][0])

    @pl.when(jnp.logical_not(is_src))
    def _():
        run(rounds[False][0])

    def round_of(t, _):
        for src in (True, False):
            for r in range(1, 8):
                if rounds[src][r]:
                    @pl.when(jnp.logical_and(t == r, is_src == src))
                    def _():
                        run(rounds[src][r])

        consume(t)

        @pl.when(t > 1)
        def _():
            finish(t - 2)

        return 0

    lax.fori_loop(0, 8, round_of, 0)
    finish(6)
    finish(7)

    @pl.when(is_src)
    def _():
        for j in range(4):
            if ("ol", j) not in SOURCE:
                own_left(j)
        wait_bytes(gbuf.at[pl.ds(0, 2), :, c], zsend)

    @pl.when(jnp.logical_not(is_src))
    def _():
        wait_bytes(gbuf.at[pl.ds(0, 3), :, c], zsend)

    wait_bytes(gbuf.at[:, :, c], psend)

    @pl.when(steps_y == 0)
    def _():
        for q in range(NQ):
            first(q, 1 - c).wait_send()

    @pl.when(steps_y >= 1)
    def _():
        for q in range(NQ):
            first(q, 0).wait_send()
            first(q, 1).wait_send()

    pair.wait_send()
    for i in range(1, 5):
        ring_up(i).wait_send()
    for i in range(1, 4):
        ring_dn(i).wait_send()
    wait_bytes(sz.at[pl.ds(0, 7)], szsend)
    wait_bytes(sy.at[pl.ds(0, 7)], sysend)
    wait_bytes(at.at[y], asend.at[0])
    wait_bytes(at.at[y], asend.at[1])
    for h in range(2):
        wait_bytes(at.at[y, h], afsend.at[h])
    wait_bytes(rl, rsend.at[0])
    wait_bytes(rr, rsend.at[1])

    for q in range(NQ):
        wait_bytes(fl.at[q], flrecv.at[q])
        wait_bytes(fr.at[q], frrecv.at[q])
        block = own[q] + fl[q].astype(F32) + fr[q].astype(F32)
        out_ref[pl.ds(q * W, W), :] = block.T.astype(BF16)
    wait_bytes(s1, fsend.at[0])
    wait_bytes(s3, fsend.at[1])


def local(activations, out_grads, lengths):
    dma, vmem = pltpu.SemaphoreType.DMA, pltpu.VMEM
    grams = (2, 3, 16, 128)
    scratch = [
        pltpu.SMEM((2,), jnp.int32),
        vmem((2, SLOT_LEN, F), BF16),
        vmem((2, SLOT_LEN, F), BF16),
        vmem((X, NQ, 2, Y, SLOT_LEN, W), BF16),
        vmem((Y, 2, F, SLOT_LEN), BF16),
        vmem((2, F, Y * SLOT_LEN), BF16),
        vmem((2, Z) + grams, F32),
        vmem((Z,) + grams, F32),
        vmem((Z,) + grams, F32),
        vmem((4,) + grams, F32),
        vmem((3,) + grams, F32),
        vmem((3,) + grams, F32),
        vmem((2,) + grams, F32),
        vmem((Z, 8, 128), F32),
        vmem((2 * Y, 8, 128), F32),
        vmem((3, 256, W), F32),
        vmem((F, W), F32),
        vmem((2, F, W), F32),
        vmem((NQ, F, W), F32),
        vmem((NQ, F, W), BF16),
        vmem((NQ, F, W), BF16),
        vmem((NQ, F, W), BF16),
        vmem((NQ, 256, W), BF16),
        vmem((NQ, 256, W), BF16),
        vmem((NQ, F, W), BF16),
        vmem((NQ, F, W), BF16),
        dma((3,)), dma((NQ, 2)), dma((NQ, Y)), dma((4,)), dma((4,)), dma, dma((X, 4)),
        dma, dma((X, 3)), dma((2,)), dma((2,)), dma((2,)), dma((2,)), dma((2,)),
        dma, dma, dma((4,)), dma((4,)), dma((3,)), dma((3,)), dma, dma, dma, dma,
        dma((2,)), dma((NQ, 2)), dma((NQ, 2)), dma((2,)), dma((NQ,)), dma((NQ,)),
    ]
    return pl.pallas_call(
        kernel,
        out_shape=(
            jax.ShapeDtypeStruct((F, F), BF16),
            jax.ShapeDtypeStruct((2,), F32),
        ),
        in_specs=[
            pl.BlockSpec(memory_space=pl.ANY),
            pl.BlockSpec(memory_space=pl.ANY),
            pl.BlockSpec(memory_space=pl.ANY),
        ],
        out_specs=(
            pl.BlockSpec(memory_space=pltpu.VMEM),
            pl.BlockSpec(memory_space=pltpu.SMEM),
        ),
        scratch_shapes=scratch,
        compiler_params=pltpu.CompilerParams(
            collective_id=0, has_side_effects=True, vmem_limit_bytes=40 * 1024 * 1024
        ),
        cost_estimate=pl.CostEstimate(flops=2 * 512 * 512 * 8192, bytes_accessed=3 * 2**19, transcendentals=0),
    )(*(pltpu.with_memory_space_constraint(v, pltpu.HBM) for v in (lengths, activations, out_grads)))


def solution(mesh):
    placed = (P("dp", None, "tensor"), P("dp", None, "tensor"), P("dp"))
    return jax.shard_map(
        local, mesh=mesh, in_specs=placed, out_specs=(P("dp", "tensor"), P("dp")), check_vma=False
    )
```

```python
import math

import jax
import jax.numpy as jnp
from jax import lax
from jax.experimental import pallas as pl
from jax.experimental.pallas import tpu as pltpu
from jax.sharding import PartitionSpec as P

D = 8192
K = 8192
SLOT_LEN = 256
SEQS = 32
X, Y, Z = 4, 4, 8
NQ = 2
W = 256
F = 512
BOUND = math.sqrt(K * D * SLOT_LEN / 2.0)
F32 = jnp.float32
BF16 = jnp.bfloat16

FIRST = (
    ("yl",),
)
SOURCE = (
    ("yf", 0), ("gram",), ("pairs",), ("o", 0), ("pairw",), ("ring", 1), ("yf", 1), ("ring", 2), ("o", 1),
    ("yg", 0), ("acts", 3), ("yg", 1), ("ring", 3), ("o", 2), ("ring", 4), ("acts", 1), ("ringend",),
    ("arel", 1), ("szs",), ("r", 1, 2, 0), ("o", 3), ("arel", 0), ("r", 0, 2, 0), ("szw",), ("r", 1, 2, 1),
    ("syw",), ("aw",), ("r", 0, 2, 1), ("r", 1, 2, 2), ("r", 0, 2, 2), ("C",), ("C",), ("C",), ("F", 0),
    ("r", 1, 2, 3), ("F", 1), ("C",), ("r", 0, 2, 3), ("r", 0, 4, 0), ("C",), ("F", 2), ("r", 1, 4, 1),
    ("C",), ("F", 3), ("r", 0, 4, 2), ("E", 6), ("C",), ("F", 4), ("E", 7), ("F", 5), ("r", 1, 4, 3), ("C",),
    ("F", 6), ("F", 7),
)
OTHER = (
    ("yf", 0), ("gram",), ("pairs",), ("pairw",), ("ring", 1), ("yf", 1), ("yg", 0), ("ring", 2), ("acts", 3),
    ("r", 0, 1, 0), ("yg", 1), ("ring", 3), ("r", 1, 1, 0), ("acts", 1), ("ring", 4), ("r", 1, 1, 1),
    ("r", 0, 1, 1), ("arel", 0), ("ringend",), ("szs",), ("arel", 1), ("r", 1, 1, 2), ("r", 0, 1, 2),
    ("szw",), ("syw",), ("aw",), ("C",), ("r", 1, 1, 3), ("r", 0, 1, 3), ("r", 0, 3, 0), ("r", 1, 3, 0),
    ("C",), ("C",), ("r", 1, 3, 1), ("F", 0), ("C",), ("F", 1), ("r", 0, 3, 1), ("r", 1, 3, 2),
    ("r", 0, 3, 2), ("C",), ("F", 2), ("r", 1, 3, 3), ("C",), ("F", 3), ("E", 6), ("r", 0, 3, 3), ("E", 7),
    ("C",), ("F", 4), ("C",), ("F", 5), ("F", 6), ("F", 7),
)

def rcopy(src, dst, send, recv, device):
    return pltpu.make_async_remote_copy(
        src_ref=src,
        dst_ref=dst,
        send_sem=send,
        recv_sem=recv,
        device_id=device,
        device_id_type=pl.DeviceIdType.MESH,
    )


def wait_bytes(ref, sem):
    pltpu.make_async_copy(ref, ref, sem).wait()


def kernel(
    len_hbm, a_hbm, g_hbm, out_ref, norm_ref,
    len_ref, a_ref, g_ref, gbuf, at, ats, gpack, gpair, gsum, gup, gdn, sup, sdn, sz, sy,
    hold, total, pre, own, s1, s2, s3, rl, rr, fl, fr,
    loads, ysend, yrecv, kup, kdn, zsend, zrecv, psend, precv, asend, a_near, a_other, a_far, afsend,
    gpsend, gprecv, gupsend, guprecv, gdnsend, gdnrecv, szsend, szrecv, sysend, syrecv,
    rsend, rlrecv, rrrecv, fsend, flrecv, frrecv,
):
    dp = lax.axis_index("dp")
    tn = lax.axis_index("tensor")
    x, y = lax.div(dp, Y), lax.rem(dp, Y)
    z, c = lax.div(tn, 2), lax.rem(tn, 2)

    def dev(x_, y_, z_, c_):
        return (x_ * Y + y_, z_ * 2 + c_)

    def xs(k):
        return lax.rem(x + k, X)

    def ys(k):
        return lax.rem(y + k, Y)

    def zs(k):
        return lax.rem(z + k + Z, Z)

    partner = dev(x, y, z, 1 - c)
    z_up, z_dn = dev(x, y, zs(1), c), dev(x, y, zs(-1), c)
    x_up, x_dn = dev(xs(1), y, z, c), dev(xs(3), y, z, c)
    y_up, y_dn = dev(x, ys(1), z, c), dev(x, ys(3), z, c)
    y_others = [(ys(k), c) for k in (1, 2, 3)] + [(ys(k), 1 - c) for k in (0, 1, 2, 3)]

    load_a = pltpu.make_async_copy(a_hbm, a_ref, loads.at[0])
    load_g = pltpu.make_async_copy(g_hbm, g_ref, loads.at[1])
    load_len = pltpu.make_async_copy(len_hbm, len_ref, loads.at[2])
    load_len.start()
    load_a.start()
    load_g.start()

    barrier = pltpu.get_barrier_semaphore()
    peers = [dev(x, y2, z, c2) for y2, c2 in y_others]
    peers += [dev(x, y, zs(k), c) for k in range(1, Z)] + [x_up, x_dn]
    for peer in peers:
        pl.semaphore_signal(barrier, inc=1, device_id=peer, device_id_type=pl.DeviceIdType.MESH)
    rows = lax.broadcasted_iota(jnp.int32, (SLOT_LEN, F), 0)
    contract = (((1,), (1,)), ((), ()))
    load_len.wait()
    load_a.wait()
    load_g.wait()

    def gram(s):
        am = jnp.where(rows < len_ref[s], a_ref[s].astype(F32), 0.0)
        at[y, s] = am.T.astype(BF16)
        am = am.astype(BF16)
        g = g_ref[s]
        for m, v in enumerate((am, g)):
            full = lax.dot_general(v, v, contract, preferred_element_type=F32)
            gpack[s, :, m, 0] = full[:128, :128].reshape(Z, 16, 128)
            gpack[s, :, m, 1] = full[:128, 128:].reshape(Z, 16, 128)
            gpack[s, :, m, 2] = full[128:, 128:].reshape(Z, 16, 128)
    gram(0)
    pl.semaphore_wait(barrier, len(peers))

    xb0 = lax.div(z, 2)
    yt = 2 * lax.rem(z, 2) + c
    is_src = lax.rem(z, 2) == lax.div(y, 2)
    steps_y = lax.rem(y - yt + Y, Y)

    def first(q, h):
        return rcopy(
            g_hbm.at[h, :, pl.ds(q * W, W)], gbuf.at[xb0, q, h, steps_y], ysend.at[q, h],
            yrecv.at[q, steps_y], dev(x, yt, z, h),
        )

    def first_steps():
        @pl.when(steps_y == 0)
        def _():
            for q in range(NQ):
                pltpu.make_async_copy(
                    g_hbm.at[c, :, pl.ds(q * W, W)], gbuf.at[xb0, q, c, 0], yrecv.at[q, 0]
                ).start()
                first(q, 1 - c).start()

        @pl.when(steps_y == 1)
        def _():
            for q in range(NQ):
                first(q, 0).start()
                first(q, 1).start()

    def first_far(steps, q):
        @pl.when(steps_y == steps)
        def _():
            first(q, 0).start()
            first(q, 1).start()

    pair = rcopy(gpack.at[1 - c], gpair, gpsend, gprecv, partner)

    def pair_wait():
        pair.wait_recv()
        gsum[...] = gpack[c] + gpair[...]

    def ring_up(i):
        src = gsum.at[zs(4)] if i == 1 else sup.at[i - 2]
        return rcopy(src, gup.at[i - 1], gupsend.at[i - 1], guprecv.at[i - 1], z_up)

    def ring_dn(i):
        src = gsum.at[zs(-3)] if i == 1 else sdn.at[i - 2]
        return rcopy(src, gdn.at[i - 1], gdnsend.at[i - 1], gdnrecv.at[i - 1], z_dn)

    def ring(i):
        if i > 1:
            ring_up(i - 1).wait_recv()
            sup[i - 2] = gsum[zs(5 - i)] + gup[i - 2]
        ring_up(i).start()
        if i <= 3:
            if i > 1:
                ring_dn(i - 1).wait_recv()
                sdn[i - 2] = gsum[zs(i - 4)] + gdn[i - 2]
            ring_dn(i).start()

    def ring_end():
        ring_up(4).wait_recv()
        ring_dn(3).wait_recv()
        total = gsum[z] + gup[3] + gdn[2]
        prod = total[0] * total[1]
        square = jnp.sum(prod[0] + 2.0 * prod[1] + prod[2])
        sz[z] = jnp.full((8, 128), square, F32)

    def squares():
        for k in range(1, Z):
            rcopy(sz.at[z], sz.at[z], szsend, szrecv, dev(x, y, zs(k), c)).start()

    def squares_wait():
        wait_bytes(sz.at[pl.ds(0, 7)], szrecv)
        tile = sz[0]
        for k in range(1, Z):
            tile = tile + sz[k]
        mine = y * 2 + c
        sy[mine] = tile
        for y2, c2 in y_others:
            rcopy(sy.at[mine], sy.at[mine], sysend, syrecv, dev(x, y2, z, c2)).start()

    def norms_wait():
        wait_bytes(sy.at[pl.ds(0, 7)], syrecv)

    def act(h, way):
        sem = a_near.at[h] if h == way else a_other.at[h]
        rcopy(at.at[y, h], at.at[y, h], asend.at[way], sem, (y_up, y_dn)[way]).start()

    def acts(which):
        for way in range(2):
            act(way if which == 3 else 1 - way, way)

    def act_relay(h):
        part = at.at[ys(3 - 2 * h), h]
        wait_bytes(part, a_near.at[h])
        rcopy(part, part, afsend.at[h], a_far.at[h], (y_up, y_dn)[h]).start()

    def scale():
        for h in range(2):
            wait_bytes(at.at[ys(1 + 2 * h), h], a_other.at[h])
            wait_bytes(at.at[ys(2), h], a_far.at[h])
        for h in range(2):
            norm_ref[h] = jnp.max(jnp.sqrt(sy[y * 2 + h] + 1e-6))
        for h in range(2):
            for k in range(Y):
                factor = jnp.max(jnp.minimum(1.0, BOUND / jnp.sqrt(sy[ys(k) * 2 + h] + 1e-6)))
                scaled = (at[ys(k), h].astype(F32) * factor).astype(BF16)
                ats[h, :, pl.ds(k * SLOT_LEN, SLOT_LEN)] = scaled

    def chunk(xb, j):
        return gbuf.at[xb, :, c, j] if j < 2 else gbuf.at[xb, j - 2, c, pl.ds(2, 2)]

    def to_partner(xb, j):
        part = gbuf.at[xb, :, c, pl.ds(0, 2)] if j == 1 else chunk(xb, j)
        return rcopy(part, part, psend, precv.at[xb, j - 1], partner)

    def own_chunk(j):
        part = chunk(xb0, j)
        if j < 2:
            for q in range(NQ):
                wait_bytes(gbuf.at[xb0, q, c, j], yrecv.at[q, j])
        else:
            for k in (2, 3):
                wait_bytes(gbuf.at[xb0, j - 2, c, k], yrecv.at[j - 2, k])
        rcopy(part, part, kup.at[j], zrecv.at[xb0, j], z_up).start()
        rcopy(part, part, kdn.at[j], zrecv.at[xb0, j], z_dn).start()
        if j > 0:
            to_partner(xb0, j).start()

    def own_left(j):
        wait_bytes(chunk(xb0, j), kup.at[j])
        wait_bytes(chunk(xb0, j), kdn.at[j])

    def receive(side, d, j):
        xb = lax.div(zs(-d if side == 0 else d), 2)
        part = chunk(xb, j)
        wait_bytes(part, zrecv.at[xb, j])
        if d < 3 or (d == 3 and j % 2 == side):
            rcopy(part, part, zsend, zrecv.at[xb, j], (z_up, z_dn)[side]).start()
        if j > 0:
            to_partner(xb, j).start()

    def info(t):
        q_s = jnp.where(t < 2, t, jnp.where(t < 6, lax.div(t - 2, 2), t - 6))
        d_s = jnp.where(t < 2, 0, jnp.where(t < 6, 2, 4))
        q = jnp.where(is_src, q_s, lax.rem(lax.div(t, 2), 2))
        d = jnp.where(is_src, d_s, jnp.where(t < 4, 1, 3))
        z_from = lax.rem(jnp.where(lax.rem(t, 2) == 0, z + Z - d, z + d), Z)
        return lax.div(z_from, 2), q

    def relay_up(q, first, rows, slot):
        part = pl.ds(first, rows)
        return rcopy(s2.at[q, part], rl.at[q, part], rsend.at[0], rlrecv.at[q, slot], x_up)

    def relay_dn(q, first, rows, slot):
        return rcopy(
            s2.at[q, pl.ds(256 + first, rows)], rr.at[q, pl.ds(first, rows)], rsend.at[1],
            rrrecv.at[q, slot], x_dn,
        )

    def final_up(q, first, rows):
        part = pl.ds(first, rows)
        rcopy(s1.at[q, part], fl.at[q, part], fsend.at[0], flrecv.at[q], x_up).start()

    def final_dn(q, first, rows):
        part = pl.ds(first, rows)
        rcopy(s3.at[q, part], fr.at[q, part], fsend.at[1], frrecv.at[q], x_dn).start()

    def parts_of(t, run_part):
        if isinstance(t, int):
            for first, rows, slot in ((0, 128, 0), (128, 128, 1)) if t >= 6 else ((0, 256, 0),):
                run_part(first, rows, slot)
            return

        @pl.when(t < 6)
        def _():
            run_part(0, 256, 0)

        @pl.when(t >= 6)
        def _():
            run_part(0, 128, 0)
            run_part(128, 128, 1)

    def product(xb, q, core, slot, slots):
        rows = gbuf[xb, q, core, pl.ds(slot, slots)].reshape(slots * SLOT_LEN, W)
        cols = ats[core, :, pl.ds(slot * SLOT_LEN, slots * SLOT_LEN)]
        return jnp.dot(cols, rows, preferred_element_type=F32)

    def others(xb, j):
        part = gbuf.at[xb, :, 1 - c, pl.ds(0, 2)] if j == 0 else gbuf.at[xb, j - 1, 1 - c, pl.ds(2, 2)]
        wait_bytes(part, precv.at[xb, j])

    def others_last(xb, q):
        wait_bytes(gbuf.at[xb, q, 1 - c, pl.ds(2, 2)], precv.at[xb, 1 + q])

    def ahead(t):
        xb, q = info(t)
        if t == 6:
            @pl.when(is_src)
            def _():
                others(xb, 0)

        pre[t - 6] = product(xb, q, c, 0, 2) + product(xb, q, 1 - c, 0, 2)

    def consume(t):
        xb, q = info(t)

        @pl.when(t < 6)
        def _():
            total[...] = product(xb, q, c, 0, 4)

            @pl.when(q == 0)
            def _():
                others(xb, 0)

            others_last(xb, q)
            total[...] = (total[...] + product(xb, q, 1 - c, 0, 4)) * (1.0 / SEQS)

        @pl.when(t >= 6)
        def _():
            late = lax.max(t - 6, 0)
            total[...] = pre[late] + product(xb, q, c, 2, 2)
            others_last(xb, q)
            total[...] = (total[...] + product(xb, q, 1 - c, 2, 2)) * (1.0 / SEQS)

        o = lax.rem(xb + X - x, X)

        @pl.when(o == 0)
        def _():
            own[q] = total[...]

        @pl.when(o == 2)
        def _():
            s2[q] = total[...].astype(BF16)

            def send(first, rows, slot):
                relay_up(q, first, rows, slot).start()
                relay_dn(q, first, rows, slot).start()

            parts_of(t, send)

        @pl.when(o == 1)
        def _():
            s1[q, pl.ds(256, 256)] = total[pl.ds(256, 256)].astype(BF16)
            final_up(q, 256, 256)
            hold[lax.rem(t, 3)] = total[pl.ds(0, 256)]

        @pl.when(o == 3)
        def _():
            s3[q, pl.ds(0, 256)] = total[pl.ds(0, 256)].astype(BF16)
            final_dn(q, 0, 256)
            hold[lax.rem(t, 3)] = total[pl.ds(256, 256)]

    def finish(t):
        xb, q = info(t)
        o = lax.rem(xb + X - x, X)
        s = t % 3

        @pl.when(o == 1)
        def _():
            def add(first, rows, slot):
                part = pl.ds(first, rows)
                relay_up(q, first, rows, slot).wait_recv()
                s1[q, part] = (hold[s, part] + rl[q, part].astype(F32)).astype(BF16)
                final_up(q, first, rows)

            parts_of(t, add)

        @pl.when(o == 3)
        def _():
            def add(first, rows, slot):
                part = pl.ds(first, rows)
                relay_dn(q, first, rows, slot).wait_recv()
                s3[q, pl.ds(256 + first, rows)] = (hold[s, part] + rr[q, part].astype(F32)).astype(BF16)
                final_dn(q, 256 + first, rows)

            parts_of(t, add)

    calls = {
        "gram": lambda: gram(1), "E": ahead, "F": finish, "yl": first_steps, "yf": lambda q: first_far(3, q), "yg": lambda q: first_far(2, q), "o": own_chunk, "ol": own_left,
        "pairs": pair.start, "pairw": pair_wait, "ring": ring, "ringend": ring_end, "szs": squares,
        "szw": squares_wait, "syw": norms_wait, "aw": scale, "acts": acts, "arel": act_relay,
    }

    def run(plan):
        for name, *args in plan:
            if name == "r":
                receive(*args)
            else:
                calls[name](*args)

    rounds = {True: [[]], False: [[]]}
    for src, plan in ((True, SOURCE), (False, OTHER)):
        for item in plan:
            if item == ("C",):
                rounds[src].append([])
            else:
                rounds[src][-1].append(item)

    run(FIRST)

    @pl.when(is_src)
    def _():
        run(rounds[True][0])

    @pl.when(jnp.logical_not(is_src))
    def _():
        run(rounds[False][0])

    def round_of(t, _):
        for src in (True, False):
            for r in range(1, 8):
                if rounds[src][r]:
                    @pl.when(jnp.logical_and(t == r, is_src == src))
                    def _():
                        run(rounds[src][r])

        consume(t)

        return 0

    lax.fori_loop(0, 8, round_of, 0)
    for src in (True, False):
        @pl.when(is_src == src)
        def _():
            run(rounds[src][8])


    @pl.when(is_src)
    def _():
        for j in range(4):
            if ("ol", j) not in SOURCE:
                own_left(j)
        wait_bytes(gbuf.at[pl.ds(0, 2), :, c], zsend)

    @pl.when(jnp.logical_not(is_src))
    def _():
        wait_bytes(gbuf.at[pl.ds(0, 3), :, c], zsend)

    wait_bytes(gbuf.at[:, :, c], psend)

    @pl.when(steps_y == 0)
    def _():
        for q in range(NQ):
            first(q, 1 - c).wait_send()

    @pl.when(steps_y >= 1)
    def _():
        for q in range(NQ):
            first(q, 0).wait_send()
            first(q, 1).wait_send()

    pair.wait_send()
    for i in range(1, 5):
        ring_up(i).wait_send()
    for i in range(1, 4):
        ring_dn(i).wait_send()
    wait_bytes(sz.at[pl.ds(0, 7)], szsend)
    wait_bytes(sy.at[pl.ds(0, 7)], sysend)
    wait_bytes(at.at[y], asend.at[0])
    wait_bytes(at.at[y], asend.at[1])
    for h in range(2):
        wait_bytes(at.at[y, h], afsend.at[h])
    wait_bytes(rl, rsend.at[0])
    wait_bytes(rr, rsend.at[1])

    for q in range(NQ):
        wait_bytes(fl.at[q], flrecv.at[q])
        wait_bytes(fr.at[q], frrecv.at[q])
        block = own[q] + fl[q].astype(F32) + fr[q].astype(F32)
        out_ref[pl.ds(q * W, W), :] = block.T.astype(BF16)
    wait_bytes(s1, fsend.at[0])
    wait_bytes(s3, fsend.at[1])


def local(activations, out_grads, lengths):
    dma, vmem = pltpu.SemaphoreType.DMA, pltpu.VMEM
    grams = (2, 3, 16, 128)
    scratch = [
        pltpu.SMEM((2,), jnp.int32),
        vmem((2, SLOT_LEN, F), BF16),
        vmem((2, SLOT_LEN, F), BF16),
        vmem((X, NQ, 2, Y, SLOT_LEN, W), BF16),
        vmem((Y, 2, F, SLOT_LEN), BF16),
        vmem((2, F, Y * SLOT_LEN), BF16),
        vmem((2, Z) + grams, F32),
        vmem((Z,) + grams, F32),
        vmem((Z,) + grams, F32),
        vmem((4,) + grams, F32),
        vmem((3,) + grams, F32),
        vmem((3,) + grams, F32),
        vmem((2,) + grams, F32),
        vmem((Z, 8, 128), F32),
        vmem((2 * Y, 8, 128), F32),
        vmem((3, 256, W), F32),
        vmem((F, W), F32),
        vmem((2, F, W), F32),
        vmem((NQ, F, W), F32),
        vmem((NQ, F, W), BF16),
        vmem((NQ, F, W), BF16),
        vmem((NQ, F, W), BF16),
        vmem((NQ, 256, W), BF16),
        vmem((NQ, 256, W), BF16),
        vmem((NQ, F, W), BF16),
        vmem((NQ, F, W), BF16),
        dma((3,)), dma((NQ, 2)), dma((NQ, Y)), dma((4,)), dma((4,)), dma, dma((X, 4)),
        dma, dma((X, 3)), dma((2,)), dma((2,)), dma((2,)), dma((2,)), dma((2,)),
        dma, dma, dma((4,)), dma((4,)), dma((3,)), dma((3,)), dma, dma, dma, dma,
        dma((2,)), dma((NQ, 2)), dma((NQ, 2)), dma((2,)), dma((NQ,)), dma((NQ,)),
    ]
    return pl.pallas_call(
        kernel,
        out_shape=(
            jax.ShapeDtypeStruct((F, F), BF16),
            jax.ShapeDtypeStruct((2,), F32),
        ),
        in_specs=[
            pl.BlockSpec(memory_space=pl.ANY),
            pl.BlockSpec(memory_space=pl.ANY),
            pl.BlockSpec(memory_space=pl.ANY),
        ],
        out_specs=(
            pl.BlockSpec(memory_space=pltpu.VMEM),
            pl.BlockSpec(memory_space=pltpu.SMEM),
        ),
        scratch_shapes=scratch,
        compiler_params=pltpu.CompilerParams(
            collective_id=0, has_side_effects=True, vmem_limit_bytes=40 * 1024 * 1024
        ),
        cost_estimate=pl.CostEstimate(flops=2 * 512 * 512 * 8192, bytes_accessed=3 * 2**19, transcendentals=0),
    )(*(pltpu.with_memory_space_constraint(v, pltpu.HBM) for v in (lengths, activations, out_grads)))


def solution(mesh):
    placed = (P("dp", None, "tensor"), P("dp", None, "tensor"), P("dp"))
    return jax.shard_map(
        local, mesh=mesh, in_specs=placed, out_specs=(P("dp", "tensor"), P("dp")), check_vma=False
    )
```

```python
import math

import jax
import jax.numpy as jnp
from jax import lax
from jax.experimental import pallas as pl
from jax.experimental.pallas import tpu as pltpu
from jax.sharding import PartitionSpec as P

D = 8192
K = 8192
SLOT_LEN = 256
SEQS = 32
X, Y, Z = 4, 4, 8
NQ = 2
W = 256
F = 512
BOUND = math.sqrt(K * D * SLOT_LEN / 2.0)
F32 = jnp.float32
BF16 = jnp.bfloat16

FIRST = (
    ("yl",), ("yf", 0), ("loaded",), ("gram0",),
)
SOURCE = (
    ("o", 0), ("gram",), ("pairs",), ("pairw",), ("yf", 1), ("ring", 1), ("yg", 0), ("ring", 2), ("o", 1),
    ("yg", 1), ("acts", 3), ("ring", 3), ("o", 2), ("ring", 4), ("acts", 1), ("ringend",), ("arel", 1),
    ("szs",), ("r", 1, 2, 0), ("o", 3), ("arel", 0), ("r", 0, 2, 0), ("szw",), ("r", 1, 2, 1), ("syw",),
    ("aw",), ("r", 0, 2, 1), ("r", 1, 2, 2), ("r", 0, 2, 2), ("C",), ("C",), ("C",), ("r", 1, 2, 3), ("C",),
    ("r", 0, 2, 3), ("r", 0, 4, 0), ("C",), ("r", 1, 4, 1), ("C",), ("r", 0, 4, 2), ("E", 6), ("E", 7),
    ("C",), ("r", 1, 4, 3), ("C",),
)
OTHER = (
    ("gram",), ("pairs",), ("pairw",), ("ring", 1), ("yf", 1), ("yg", 0), ("ring", 2), ("acts", 3),
    ("r", 0, 1, 0), ("yg", 1), ("ring", 3), ("r", 1, 1, 0), ("acts", 1), ("ring", 4), ("r", 1, 1, 1),
    ("r", 0, 1, 1), ("arel", 0), ("ringend",), ("szs",), ("arel", 1), ("r", 1, 1, 2), ("r", 0, 1, 2),
    ("szw",), ("syw",), ("aw",), ("C",), ("r", 1, 1, 3), ("r", 0, 1, 3), ("r", 0, 3, 0), ("r", 1, 3, 0),
    ("C",), ("C",), ("C",), ("r", 1, 3, 1), ("r", 0, 3, 1), ("r", 1, 3, 2), ("r", 0, 3, 2), ("C",),
    ("r", 1, 3, 3), ("C",), ("E", 6), ("r", 0, 3, 3), ("E", 7), ("C",), ("C",),
)

def rcopy(src, dst, send, recv, device):
    return pltpu.make_async_remote_copy(
        src_ref=src,
        dst_ref=dst,
        send_sem=send,
        recv_sem=recv,
        device_id=device,
        device_id_type=pl.DeviceIdType.MESH,
    )


def wait_bytes(ref, sem):
    pltpu.make_async_copy(ref, ref, sem).wait()


def kernel(
    len_hbm, a_hbm, g_hbm, out_ref, norm_ref,
    len_ref, a_ref, g_ref, gbuf, at, ats, gpack, gpair, gsum, gup, gdn, sup, sdn, sz, sy,
    hold, total, pre, own, s1, s2, s3, rl, rr, fl, fr,
    loads, ysend, yrecv, kup, kdn, zsend, zrecv, psend, precv, asend, a_near, a_other, a_far, afsend,
    gpsend, gprecv, gupsend, guprecv, gdnsend, gdnrecv, szsend, szrecv, sysend, syrecv,
    rsend, rlrecv, rrrecv, fsend, flrecv, frrecv,
):
    dp = lax.axis_index("dp")
    tn = lax.axis_index("tensor")
    x, y = lax.div(dp, Y), lax.rem(dp, Y)
    z, c = lax.div(tn, 2), lax.rem(tn, 2)

    def dev(x_, y_, z_, c_):
        return (x_ * Y + y_, z_ * 2 + c_)

    def xs(k):
        return lax.rem(x + k, X)

    def ys(k):
        return lax.rem(y + k, Y)

    def zs(k):
        return lax.rem(z + k + Z, Z)

    partner = dev(x, y, z, 1 - c)
    z_up, z_dn = dev(x, y, zs(1), c), dev(x, y, zs(-1), c)
    x_up, x_dn = dev(xs(1), y, z, c), dev(xs(3), y, z, c)
    y_up, y_dn = dev(x, ys(1), z, c), dev(x, ys(3), z, c)
    y_others = [(ys(k), c) for k in (1, 2, 3)] + [(ys(k), 1 - c) for k in (0, 1, 2, 3)]

    load_a = pltpu.make_async_copy(a_hbm, a_ref, loads.at[0])
    load_g = pltpu.make_async_copy(g_hbm, g_ref, loads.at[1])
    load_len = pltpu.make_async_copy(len_hbm, len_ref, loads.at[2])
    load_len.start()
    load_a.start()
    load_g.start()

    barrier = pltpu.get_barrier_semaphore()
    peers = [dev(x, y2, z, c2) for y2, c2 in y_others]
    peers += [dev(x, y, zs(k), c) for k in range(1, Z)] + [x_up, x_dn]
    for peer in peers:
        pl.semaphore_signal(barrier, inc=1, device_id=peer, device_id_type=pl.DeviceIdType.MESH)
    rows = lax.broadcasted_iota(jnp.int32, (SLOT_LEN, F), 0)
    contract = (((1,), (1,)), ((), ()))

    def loaded():
        load_len.wait()
        load_a.wait()
        load_g.wait()

    def gram(s):
        am = jnp.where(rows < len_ref[s], a_ref[s].astype(F32), 0.0)
        at[y, s] = am.T.astype(BF16)
        am = am.astype(BF16)
        g = g_ref[s]
        for m, v in enumerate((am, g)):
            full = lax.dot_general(v, v, contract, preferred_element_type=F32)
            gpack[s, :, m, 0] = full[:128, :128].reshape(Z, 16, 128)
            gpack[s, :, m, 1] = full[:128, 128:].reshape(Z, 16, 128)
            gpack[s, :, m, 2] = full[128:, 128:].reshape(Z, 16, 128)
    pl.semaphore_wait(barrier, len(peers))

    xb0 = lax.div(z, 2)
    yt = 2 * lax.rem(z, 2) + c
    is_src = lax.rem(z, 2) == lax.div(y, 2)
    steps_y = lax.rem(y - yt + Y, Y)

    def first(q, h):
        return rcopy(
            g_hbm.at[h, :, pl.ds(q * W, W)], gbuf.at[xb0, q, h, steps_y], ysend.at[q, h],
            yrecv.at[q, steps_y], dev(x, yt, z, h),
        )

    def first_steps():
        @pl.when(steps_y == 0)
        def _():
            for q in range(NQ):
                pltpu.make_async_copy(
                    g_hbm.at[c, :, pl.ds(q * W, W)], gbuf.at[xb0, q, c, 0], yrecv.at[q, 0]
                ).start()
                first(q, 1 - c).start()

        @pl.when(steps_y == 1)
        def _():
            for q in range(NQ):
                first(q, 0).start()
                first(q, 1).start()

    def first_far(steps, q):
        @pl.when(steps_y == steps)
        def _():
            first(q, 0).start()
            first(q, 1).start()

    pair = rcopy(gpack.at[1 - c], gpair, gpsend, gprecv, partner)

    def pair_wait():
        pair.wait_recv()
        gsum[...] = gpack[c] + gpair[...]

    def ring_up(i):
        src = gsum.at[zs(4)] if i == 1 else sup.at[i - 2]
        return rcopy(src, gup.at[i - 1], gupsend.at[i - 1], guprecv.at[i - 1], z_up)

    def ring_dn(i):
        src = gsum.at[zs(-3)] if i == 1 else sdn.at[i - 2]
        return rcopy(src, gdn.at[i - 1], gdnsend.at[i - 1], gdnrecv.at[i - 1], z_dn)

    def ring(i):
        if i > 1:
            ring_up(i - 1).wait_recv()
            sup[i - 2] = gsum[zs(5 - i)] + gup[i - 2]
        ring_up(i).start()
        if i <= 3:
            if i > 1:
                ring_dn(i - 1).wait_recv()
                sdn[i - 2] = gsum[zs(i - 4)] + gdn[i - 2]
            ring_dn(i).start()

    def ring_end():
        ring_up(4).wait_recv()
        ring_dn(3).wait_recv()
        total = gsum[z] + gup[3] + gdn[2]
        prod = total[0] * total[1]
        square = jnp.sum(prod[0] + 2.0 * prod[1] + prod[2])
        sz[z] = jnp.full((8, 128), square, F32)

    def squares():
        for k in range(1, Z):
            rcopy(sz.at[z], sz.at[z], szsend, szrecv, dev(x, y, zs(k), c)).start()

    def squares_wait():
        wait_bytes(sz.at[pl.ds(0, 7)], szrecv)
        tile = sz[0]
        for k in range(1, Z):
            tile = tile + sz[k]
        mine = y * 2 + c
        sy[mine] = tile
        for y2, c2 in y_others:
            rcopy(sy.at[mine], sy.at[mine], sysend, syrecv, dev(x, y2, z, c2)).start()

    def norms_wait():
        wait_bytes(sy.at[pl.ds(0, 7)], syrecv)

    def act(h, way):
        sem = a_near.at[h] if h == way else a_other.at[h]
        rcopy(at.at[y, h], at.at[y, h], asend.at[way], sem, (y_up, y_dn)[way]).start()

    def acts(which):
        for way in range(2):
            act(way if which == 3 else 1 - way, way)

    def act_relay(h):
        part = at.at[ys(3 - 2 * h), h]
        wait_bytes(part, a_near.at[h])
        rcopy(part, part, afsend.at[h], a_far.at[h], (y_up, y_dn)[h]).start()

    def scale():
        for h in range(2):
            wait_bytes(at.at[ys(1 + 2 * h), h], a_other.at[h])
            wait_bytes(at.at[ys(2), h], a_far.at[h])
        for h in range(2):
            norm_ref[h] = jnp.max(jnp.sqrt(sy[y * 2 + h] + 1e-6))
        for h in range(2):
            for k in range(Y):
                factor = jnp.max(jnp.minimum(1.0, BOUND / jnp.sqrt(sy[ys(k) * 2 + h] + 1e-6)))
                scaled = (at[ys(k), h].astype(F32) * factor).astype(BF16)
                ats[h, :, pl.ds(k * SLOT_LEN, SLOT_LEN)] = scaled

    def chunk(xb, j):
        return gbuf.at[xb, :, c, j] if j < 2 else gbuf.at[xb, j - 2, c, pl.ds(2, 2)]

    def to_partner(xb, j):
        part = gbuf.at[xb, :, c, pl.ds(0, 2)] if j == 1 else chunk(xb, j)
        return rcopy(part, part, psend, precv.at[xb, j - 1], partner)

    def own_chunk(j):
        part = chunk(xb0, j)
        if j < 2:
            for q in range(NQ):
                wait_bytes(gbuf.at[xb0, q, c, j], yrecv.at[q, j])
        else:
            for k in (2, 3):
                wait_bytes(gbuf.at[xb0, j - 2, c, k], yrecv.at[j - 2, k])
        rcopy(part, part, kup.at[j], zrecv.at[xb0, j], z_up).start()
        rcopy(part, part, kdn.at[j], zrecv.at[xb0, j], z_dn).start()
        if j > 0:
            to_partner(xb0, j).start()

    def own_left(j):
        wait_bytes(chunk(xb0, j), kup.at[j])
        wait_bytes(chunk(xb0, j), kdn.at[j])

    def receive(side, d, j):
        xb = lax.div(zs(-d if side == 0 else d), 2)
        part = chunk(xb, j)
        wait_bytes(part, zrecv.at[xb, j])
        if d < 3 or (d == 3 and j % 2 == side):
            rcopy(part, part, zsend, zrecv.at[xb, j], (z_up, z_dn)[side]).start()
        if j > 0:
            to_partner(xb, j).start()

    def info(t):
        q_s = jnp.where(t < 2, t, jnp.where(t < 6, lax.div(t - 2, 2), t - 6))
        d_s = jnp.where(t < 2, 0, jnp.where(t < 6, 2, 4))
        q = jnp.where(is_src, q_s, lax.rem(lax.div(t, 2), 2))
        d = jnp.where(is_src, d_s, jnp.where(t < 4, 1, 3))
        z_from = lax.rem(jnp.where(lax.rem(t, 2) == 0, z + Z - d, z + d), Z)
        return lax.div(z_from, 2), q

    def relay_up(q, first, rows, slot):
        part = pl.ds(first, rows)
        return rcopy(s2.at[q, part], rl.at[q, part], rsend.at[0], rlrecv.at[q, slot], x_up)

    def relay_dn(q, first, rows, slot):
        return rcopy(
            s2.at[q, pl.ds(256 + first, rows)], rr.at[q, pl.ds(first, rows)], rsend.at[1],
            rrrecv.at[q, slot], x_dn,
        )

    def final_up(q, first, rows):
        part = pl.ds(first, rows)
        rcopy(s1.at[q, part], fl.at[q, part], fsend.at[0], flrecv.at[q], x_up).start()

    def final_dn(q, first, rows):
        part = pl.ds(first, rows)
        rcopy(s3.at[q, part], fr.at[q, part], fsend.at[1], frrecv.at[q], x_dn).start()

    def parts_of(t, run_part):
        @pl.when(t < 6)
        def _():
            run_part(0, 256, 0)

        @pl.when(t >= 6)
        def _():
            run_part(0, 128, 0)
            run_part(128, 128, 1)

    def product(xb, q, core, slot, slots):
        rows = gbuf[xb, q, core, pl.ds(slot, slots)].reshape(slots * SLOT_LEN, W)
        cols = ats[core, :, pl.ds(slot * SLOT_LEN, slots * SLOT_LEN)]
        return jnp.dot(cols, rows, preferred_element_type=F32)

    def others(xb, j):
        part = gbuf.at[xb, :, 1 - c, pl.ds(0, 2)] if j == 0 else gbuf.at[xb, j - 1, 1 - c, pl.ds(2, 2)]
        wait_bytes(part, precv.at[xb, j])

    def others_last(xb, q):
        wait_bytes(gbuf.at[xb, q, 1 - c, pl.ds(2, 2)], precv.at[xb, 1 + q])

    def ahead(t):
        xb, q = info(t)
        if t == 6:
            @pl.when(is_src)
            def _():
                others(xb, 0)

        pre[t - 6] = product(xb, q, c, 0, 2) + product(xb, q, 1 - c, 0, 2)

    def consume(t):
        xb, q = info(t)

        @pl.when(t < 6)
        def _():
            total[...] = product(xb, q, c, 0, 4)

            @pl.when(q == 0)
            def _():
                others(xb, 0)

            others_last(xb, q)
            total[...] = (total[...] + product(xb, q, 1 - c, 0, 4)) * (1.0 / SEQS)

        @pl.when(t >= 6)
        def _():
            late = lax.max(t - 6, 0)
            total[...] = pre[late] + product(xb, q, c, 2, 2)
            others_last(xb, q)
            total[...] = (total[...] + product(xb, q, 1 - c, 2, 2)) * (1.0 / SEQS)

        o = lax.rem(xb + X - x, X)

        @pl.when(o == 0)
        def _():
            own[q] = total[...]

        @pl.when(o == 2)
        def _():
            s2[q] = total[...].astype(BF16)

            def send(first, rows, slot):
                relay_up(q, first, rows, slot).start()
                relay_dn(q, first, rows, slot).start()

            parts_of(t, send)

        @pl.when(o == 1)
        def _():
            s1[q, pl.ds(256, 256)] = total[pl.ds(256, 256)].astype(BF16)
            final_up(q, 256, 256)
            hold[lax.rem(t, 3)] = total[pl.ds(0, 256)]

        @pl.when(o == 3)
        def _():
            s3[q, pl.ds(0, 256)] = total[pl.ds(0, 256)].astype(BF16)
            final_dn(q, 0, 256)
            hold[lax.rem(t, 3)] = total[pl.ds(256, 256)]

    def finish(t):
        xb, q = info(t)
        o = lax.rem(xb + X - x, X)
        s = lax.rem(t, 3)

        @pl.when(o == 1)
        def _():
            def add(first, rows, slot):
                part = pl.ds(first, rows)
                relay_up(q, first, rows, slot).wait_recv()
                s1[q, part] = (hold[s, part] + rl[q, part].astype(F32)).astype(BF16)
                final_up(q, first, rows)

            parts_of(t, add)

        @pl.when(o == 3)
        def _():
            def add(first, rows, slot):
                part = pl.ds(first, rows)
                relay_dn(q, first, rows, slot).wait_recv()
                s3[q, pl.ds(256 + first, rows)] = (hold[s, part] + rr[q, part].astype(F32)).astype(BF16)
                final_dn(q, 256 + first, rows)

            parts_of(t, add)

    calls = {
        "loaded": loaded, "gram": lambda: gram(1), "gram0": lambda: gram(0), "E": ahead, "yl": first_steps, "yf": lambda q: first_far(3, q), "yg": lambda q: first_far(2, q), "o": own_chunk, "ol": own_left,
        "pairs": pair.start, "pairw": pair_wait, "ring": ring, "ringend": ring_end, "szs": squares,
        "szw": squares_wait, "syw": norms_wait, "aw": scale, "acts": acts, "arel": act_relay,
    }

    def run(plan):
        for name, *args in plan:
            if name == "r":
                receive(*args)
            else:
                calls[name](*args)

    rounds = {True: [[]], False: [[]]}
    for src, plan in ((True, SOURCE), (False, OTHER)):
        for item in plan:
            if item == ("C",):
                rounds[src].append([])
            else:
                rounds[src][-1].append(item)

    run(FIRST)

    @pl.when(is_src)
    def _():
        run(rounds[True][0])

    @pl.when(jnp.logical_not(is_src))
    def _():
        run(rounds[False][0])

    def round_of(t, _):
        for src in (True, False):
            for r in range(1, 8):
                if rounds[src][r]:
                    @pl.when(jnp.logical_and(t == r, is_src == src))
                    def _():
                        run(rounds[src][r])

        consume(t)

        @pl.when(t > 1)
        def _():
            finish(t - 2)

        return 0

    lax.fori_loop(0, 8, round_of, 0)
    finish(6)
    finish(7)

    @pl.when(is_src)
    def _():
        for j in range(4):
            if ("ol", j) not in SOURCE:
                own_left(j)
        wait_bytes(gbuf.at[pl.ds(0, 2), :, c], zsend)

    @pl.when(jnp.logical_not(is_src))
    def _():
        wait_bytes(gbuf.at[pl.ds(0, 3), :, c], zsend)

    wait_bytes(gbuf.at[:, :, c], psend)

    @pl.when(steps_y == 0)
    def _():
        for q in range(NQ):
            first(q, 1 - c).wait_send()

    @pl.when(steps_y >= 1)
    def _():
        for q in range(NQ):
            first(q, 0).wait_send()
            first(q, 1).wait_send()

    pair.wait_send()
    for i in range(1, 5):
        ring_up(i).wait_send()
    for i in range(1, 4):
        ring_dn(i).wait_send()
    wait_bytes(sz.at[pl.ds(0, 7)], szsend)
    wait_bytes(sy.at[pl.ds(0, 7)], sysend)
    wait_bytes(at.at[y], asend.at[0])
    wait_bytes(at.at[y], asend.at[1])
    for h in range(2):
        wait_bytes(at.at[y, h], afsend.at[h])
    wait_bytes(rl, rsend.at[0])
    wait_bytes(rr, rsend.at[1])

    for q in range(NQ):
        wait_bytes(fl.at[q], flrecv.at[q])
        wait_bytes(fr.at[q], frrecv.at[q])
        block = own[q] + fl[q].astype(F32) + fr[q].astype(F32)
        out_ref[pl.ds(q * W, W), :] = block.T.astype(BF16)
    wait_bytes(s1, fsend.at[0])
    wait_bytes(s3, fsend.at[1])


def local(activations, out_grads, lengths):
    dma, vmem = pltpu.SemaphoreType.DMA, pltpu.VMEM
    grams = (2, 3, 16, 128)
    scratch = [
        pltpu.SMEM((2,), jnp.int32),
        vmem((2, SLOT_LEN, F), BF16),
        vmem((2, SLOT_LEN, F), BF16),
        vmem((X, NQ, 2, Y, SLOT_LEN, W), BF16),
        vmem((Y, 2, F, SLOT_LEN), BF16),
        vmem((2, F, Y * SLOT_LEN), BF16),
        vmem((2, Z) + grams, F32),
        vmem((Z,) + grams, F32),
        vmem((Z,) + grams, F32),
        vmem((4,) + grams, F32),
        vmem((3,) + grams, F32),
        vmem((3,) + grams, F32),
        vmem((2,) + grams, F32),
        vmem((Z, 8, 128), F32),
        vmem((2 * Y, 8, 128), F32),
        vmem((3, 256, W), F32),
        vmem((F, W), F32),
        vmem((2, F, W), F32),
        vmem((NQ, F, W), F32),
        vmem((NQ, F, W), BF16),
        vmem((NQ, F, W), BF16),
        vmem((NQ, F, W), BF16),
        vmem((NQ, 256, W), BF16),
        vmem((NQ, 256, W), BF16),
        vmem((NQ, F, W), BF16),
        vmem((NQ, F, W), BF16),
        dma((3,)), dma((NQ, 2)), dma((NQ, Y)), dma((4,)), dma((4,)), dma, dma((X, 4)),
        dma, dma((X, 3)), dma((2,)), dma((2,)), dma((2,)), dma((2,)), dma((2,)),
        dma, dma, dma((4,)), dma((4,)), dma((3,)), dma((3,)), dma, dma, dma, dma,
        dma((2,)), dma((NQ, 2)), dma((NQ, 2)), dma((2,)), dma((NQ,)), dma((NQ,)),
    ]
    return pl.pallas_call(
        kernel,
        out_shape=(
            jax.ShapeDtypeStruct((F, F), BF16),
            jax.ShapeDtypeStruct((2,), F32),
        ),
        in_specs=[
            pl.BlockSpec(memory_space=pl.ANY),
            pl.BlockSpec(memory_space=pl.ANY),
            pl.BlockSpec(memory_space=pl.ANY),
        ],
        out_specs=(
            pl.BlockSpec(memory_space=pltpu.VMEM),
            pl.BlockSpec(memory_space=pltpu.SMEM),
        ),
        scratch_shapes=scratch,
        compiler_params=pltpu.CompilerParams(
            collective_id=0, has_side_effects=True, vmem_limit_bytes=40 * 1024 * 1024
        ),
        cost_estimate=pl.CostEstimate(flops=2 * 512 * 512 * 8192, bytes_accessed=3 * 2**19, transcendentals=0),
    )(*(pltpu.with_memory_space_constraint(v, pltpu.HBM) for v in (lengths, activations, out_grads)))


def solution(mesh):
    placed = (P("dp", None, "tensor"), P("dp", None, "tensor"), P("dp"))
    return jax.shard_map(
        local, mesh=mesh, in_specs=placed, out_specs=(P("dp", "tensor"), P("dp")), check_vma=False
    )
```

```python
import math

import jax
import jax.numpy as jnp
from jax import lax
from jax.experimental import pallas as pl
from jax.experimental.pallas import tpu as pltpu
from jax.sharding import PartitionSpec as P

D = 8192
K = 8192
SLOT_LEN = 256
SEQS = 32
X, Y, Z = 4, 4, 8
NQ = 2
W = 256
F = 512
BOUND = math.sqrt(K * D * SLOT_LEN / 2.0)
F32 = jnp.float32
BF16 = jnp.bfloat16

FIRST = (
    ("yl",), ("yf", 0), ("loaded",), ("gram0",),
)
SOURCE = (
    ("yf", 1), ("o", 0), ("gram",), ("pairs",), ("pairw",), ("ring", 1), ("yg", 0), ("ring", 2), ("o", 1),
    ("yg", 1), ("acts", 3), ("ring", 3), ("o", 2), ("ring", 4), ("acts", 1), ("ringend",), ("arel", 1),
    ("szs",), ("r", 1, 2, 0), ("o", 3), ("arel", 0), ("r", 0, 2, 0), ("szw",), ("r", 1, 2, 1), ("syw",),
    ("aw",), ("r", 0, 2, 1), ("r", 0, 2, 2), ("C",), ("r", 1, 2, 2), ("C",), ("C",), ("r", 1, 2, 3), ("C",),
    ("r", 0, 2, 3), ("r", 0, 4, 0), ("C",), ("r", 1, 4, 1), ("C",), ("r", 0, 4, 2), ("E", 6), ("E", 7),
    ("C",), ("r", 1, 4, 3), ("C",),
)
OTHER = (
    ("gram",), ("pairs",), ("pairw",), ("ring", 1), ("yf", 1), ("yg", 0), ("ring", 2), ("acts", 3),
    ("r", 0, 1, 0), ("yg", 1), ("ring", 3), ("r", 1, 1, 0), ("ring", 4), ("acts", 1), ("r", 1, 1, 1),
    ("r", 0, 1, 1), ("arel", 0), ("ringend",), ("szs",), ("arel", 1), ("r", 1, 1, 2), ("r", 0, 1, 2),
    ("szw",), ("syw",), ("aw",), ("C",), ("r", 1, 1, 3), ("r", 0, 1, 3), ("r", 0, 3, 0), ("r", 1, 3, 0),
    ("C",), ("C",), ("C",), ("r", 1, 3, 1), ("r", 0, 3, 1), ("r", 1, 3, 2), ("r", 0, 3, 2), ("C",),
    ("r", 1, 3, 3), ("C",), ("E", 6), ("r", 0, 3, 3), ("E", 7), ("C",), ("C",),
)

def rcopy(src, dst, send, recv, device):
    return pltpu.make_async_remote_copy(
        src_ref=src,
        dst_ref=dst,
        send_sem=send,
        recv_sem=recv,
        device_id=device,
        device_id_type=pl.DeviceIdType.MESH,
    )


def wait_bytes(ref, sem):
    pltpu.make_async_copy(ref, ref, sem).wait()


def kernel(
    len_hbm, a_hbm, g_hbm, out_ref, norm_ref,
    len_ref, a_ref, g_ref, gbuf, at, ats, gpack, gpair, gsum, gup, gdn, sup, sdn, sz, sy,
    hold, total, pre, own, s1, s2, s3, rl, rr, fl, fr,
    loads, ysend, yrecv, kup, kdn, zsend, zrecv, psend, precv, asend, a_near, a_other, a_far, afsend,
    gpsend, gprecv, gupsend, guprecv, gdnsend, gdnrecv, szsend, szrecv, sysend, syrecv,
    rsend, rlrecv, rrrecv, fsend, flrecv, frrecv,
):
    dp = lax.axis_index("dp")
    tn = lax.axis_index("tensor")
    x, y = lax.div(dp, Y), lax.rem(dp, Y)
    z, c = lax.div(tn, 2), lax.rem(tn, 2)

    def dev(x_, y_, z_, c_):
        return (x_ * Y + y_, z_ * 2 + c_)

    def xs(k):
        return lax.rem(x + k, X)

    def ys(k):
        return lax.rem(y + k, Y)

    def zs(k):
        return lax.rem(z + k + Z, Z)

    partner = dev(x, y, z, 1 - c)
    z_up, z_dn = dev(x, y, zs(1), c), dev(x, y, zs(-1), c)
    x_up, x_dn = dev(xs(1), y, z, c), dev(xs(3), y, z, c)
    y_up, y_dn = dev(x, ys(1), z, c), dev(x, ys(3), z, c)
    y_others = [(ys(k), c) for k in (1, 2, 3)] + [(ys(k), 1 - c) for k in (0, 1, 2, 3)]

    load_a = pltpu.make_async_copy(a_hbm, a_ref, loads.at[0])
    load_g = pltpu.make_async_copy(g_hbm, g_ref, loads.at[1])
    load_len = pltpu.make_async_copy(len_hbm, len_ref, loads.at[2])
    load_len.start()
    load_a.start()
    load_g.start()

    barrier = pltpu.get_barrier_semaphore()
    peers = [dev(x, y2, z, c2) for y2, c2 in y_others]
    peers += [dev(x, y, zs(k), c) for k in range(1, Z)] + [x_up, x_dn]
    for peer in peers:
        pl.semaphore_signal(barrier, inc=1, device_id=peer, device_id_type=pl.DeviceIdType.MESH)
    rows = lax.broadcasted_iota(jnp.int32, (SLOT_LEN, F), 0)
    contract = (((1,), (1,)), ((), ()))

    def loaded():
        load_len.wait()
        load_a.wait()
        load_g.wait()

    def gram(s):
        am = jnp.where(rows < len_ref[s], a_ref[s].astype(F32), 0.0)
        at[y, s] = am.T.astype(BF16)
        am = am.astype(BF16)
        g = g_ref[s]
        for m, v in enumerate((am, g)):
            full = lax.dot_general(v, v, contract, preferred_element_type=F32)
            gpack[s, :, m, 0] = full[:128, :128].reshape(Z, 16, 128)
            gpack[s, :, m, 1] = full[:128, 128:].reshape(Z, 16, 128)
            gpack[s, :, m, 2] = full[128:, 128:].reshape(Z, 16, 128)
    pl.semaphore_wait(barrier, len(peers))

    xb0 = lax.div(z, 2)
    yt = 2 * lax.rem(z, 2) + c
    is_src = lax.rem(z, 2) == lax.div(y, 2)
    steps_y = lax.rem(y - yt + Y, Y)

    def first(q, h):
        return rcopy(
            g_hbm.at[h, :, pl.ds(q * W, W)], gbuf.at[xb0, q, h, steps_y], ysend.at[q, h],
            yrecv.at[q, steps_y], dev(x, yt, z, h),
        )

    def first_steps():
        @pl.when(steps_y == 0)
        def _():
            for q in range(NQ):
                pltpu.make_async_copy(
                    g_hbm.at[c, :, pl.ds(q * W, W)], gbuf.at[xb0, q, c, 0], yrecv.at[q, 0]
                ).start()
                first(q, 1 - c).start()

        @pl.when(steps_y == 1)
        def _():
            for q in range(NQ):
                first(q, 0).start()
                first(q, 1).start()

    def first_far(steps, q):
        @pl.when(steps_y == steps)
        def _():
            first(q, 0).start()
            first(q, 1).start()

    pair = rcopy(gpack.at[1 - c], gpair, gpsend, gprecv, partner)

    def pair_wait():
        pair.wait_recv()
        gsum[...] = gpack[c] + gpair[...]

    def ring_up(i):
        src = gsum.at[zs(4)] if i == 1 else sup.at[i - 2]
        return rcopy(src, gup.at[i - 1], gupsend.at[i - 1], guprecv.at[i - 1], z_up)

    def ring_dn(i):
        src = gsum.at[zs(-3)] if i == 1 else sdn.at[i - 2]
        return rcopy(src, gdn.at[i - 1], gdnsend.at[i - 1], gdnrecv.at[i - 1], z_dn)

    def ring(i):
        if i > 1:
            ring_up(i - 1).wait_recv()
            sup[i - 2] = gsum[zs(5 - i)] + gup[i - 2]
        ring_up(i).start()
        if i <= 3:
            if i > 1:
                ring_dn(i - 1).wait_recv()
                sdn[i - 2] = gsum[zs(i - 4)] + gdn[i - 2]
            ring_dn(i).start()

    def ring_end():
        ring_up(4).wait_recv()
        ring_dn(3).wait_recv()
        total = gsum[z] + gup[3] + gdn[2]
        prod = total[0] * total[1]
        square = jnp.sum(prod[0] + 2.0 * prod[1] + prod[2])
        sz[z] = jnp.full((8, 128), square, F32)

    def squares():
        for k in range(1, Z):
            rcopy(sz.at[z], sz.at[z], szsend, szrecv, dev(x, y, zs(k), c)).start()

    def squares_wait():
        wait_bytes(sz.at[pl.ds(0, 7)], szrecv)
        tile = sz[0]
        for k in range(1, Z):
            tile = tile + sz[k]
        mine = y * 2 + c
        sy[mine] = tile
        for y2, c2 in y_others:
            rcopy(sy.at[mine], sy.at[mine], sysend, syrecv, dev(x, y2, z, c2)).start()

    def norms_wait():
        wait_bytes(sy.at[pl.ds(0, 7)], syrecv)

    def act(h, way):
        sem = a_near.at[h] if h == way else a_other.at[h]
        rcopy(at.at[y, h], at.at[y, h], asend.at[way], sem, (y_up, y_dn)[way]).start()

    def acts(which):
        for way in range(2):
            act(way if which == 3 else 1 - way, way)

    def act_relay(h):
        part = at.at[ys(3 - 2 * h), h]
        wait_bytes(part, a_near.at[h])
        rcopy(part, part, afsend.at[h], a_far.at[h], (y_up, y_dn)[h]).start()

    def scale():
        for h in range(2):
            wait_bytes(at.at[ys(1 + 2 * h), h], a_other.at[h])
            wait_bytes(at.at[ys(2), h], a_far.at[h])
        for h in range(2):
            norm_ref[h] = jnp.max(jnp.sqrt(sy[y * 2 + h] + 1e-6))
        for h in range(2):
            for k in range(Y):
                factor = jnp.max(jnp.minimum(1.0, BOUND / jnp.sqrt(sy[ys(k) * 2 + h] + 1e-6)))
                scaled = (at[ys(k), h].astype(F32) * factor).astype(BF16)
                ats[h, :, pl.ds(k * SLOT_LEN, SLOT_LEN)] = scaled

    def chunk(xb, j):
        return gbuf.at[xb, :, c, j] if j < 2 else gbuf.at[xb, j - 2, c, pl.ds(2, 2)]

    def to_partner(xb, j):
        part = gbuf.at[xb, :, c, pl.ds(0, 2)] if j == 1 else chunk(xb, j)
        return rcopy(part, part, psend, precv.at[xb, j - 1], partner)

    def own_chunk(j):
        part = chunk(xb0, j)
        if j < 2:
            for q in range(NQ):
                wait_bytes(gbuf.at[xb0, q, c, j], yrecv.at[q, j])
        else:
            for k in (2, 3):
                wait_bytes(gbuf.at[xb0, j - 2, c, k], yrecv.at[j - 2, k])
        rcopy(part, part, kup.at[j], zrecv.at[xb0, j], z_up).start()
        rcopy(part, part, kdn.at[j], zrecv.at[xb0, j], z_dn).start()
        if j > 0:
            to_partner(xb0, j).start()

    def own_left(j):
        wait_bytes(chunk(xb0, j), kup.at[j])
        wait_bytes(chunk(xb0, j), kdn.at[j])

    def receive(side, d, j):
        xb = lax.div(zs(-d if side == 0 else d), 2)
        part = chunk(xb, j)
        wait_bytes(part, zrecv.at[xb, j])
        if d < 3 or (d == 3 and j % 2 == side):
            rcopy(part, part, zsend, zrecv.at[xb, j], (z_up, z_dn)[side]).start()
        if j > 0:
            to_partner(xb, j).start()

    def info(t):
        q_s = jnp.where(t < 2, t, jnp.where(t < 6, lax.div(t - 2, 2), t - 6))
        d_s = jnp.where(t < 2, 0, jnp.where(t < 6, 2, 4))
        q = jnp.where(is_src, q_s, lax.rem(lax.div(t, 2), 2))
        d = jnp.where(is_src, d_s, jnp.where(t < 4, 1, 3))
        z_from = lax.rem(jnp.where(lax.rem(t, 2) == 0, z + Z - d, z + d), Z)
        return lax.div(z_from, 2), q

    def relay_up(q, first, rows, slot):
        part = pl.ds(first, rows)
        return rcopy(s2.at[q, part], rl.at[q, part], rsend.at[0], rlrecv.at[q, slot], x_up)

    def relay_dn(q, first, rows, slot):
        return rcopy(
            s2.at[q, pl.ds(256 + first, rows)], rr.at[q, pl.ds(first, rows)], rsend.at[1],
            rrrecv.at[q, slot], x_dn,
        )

    def final_up(q, first, rows):
        part = pl.ds(first, rows)
        rcopy(s1.at[q, part], fl.at[q, part], fsend.at[0], flrecv.at[q], x_up).start()

    def final_dn(q, first, rows):
        part = pl.ds(first, rows)
        rcopy(s3.at[q, part], fr.at[q, part], fsend.at[1], frrecv.at[q], x_dn).start()

    def parts_of(t, run_part):
        @pl.when(t < 6)
        def _():
            run_part(0, 256, 0)

        @pl.when(t >= 6)
        def _():
            run_part(0, 128, 0)
            run_part(128, 128, 1)

    def product(xb, q, core, slot, slots):
        rows = gbuf[xb, q, core, pl.ds(slot, slots)].reshape(slots * SLOT_LEN, W)
        cols = ats[core, :, pl.ds(slot * SLOT_LEN, slots * SLOT_LEN)]
        return jnp.dot(cols, rows, preferred_element_type=F32)

    def others(xb, j):
        part = gbuf.at[xb, :, 1 - c, pl.ds(0, 2)] if j == 0 else gbuf.at[xb, j - 1, 1 - c, pl.ds(2, 2)]
        wait_bytes(part, precv.at[xb, j])

    def others_last(xb, q):
        wait_bytes(gbuf.at[xb, q, 1 - c, pl.ds(2, 2)], precv.at[xb, 1 + q])

    def ahead(t):
        xb, q = info(t)
        if t == 6:
            @pl.when(is_src)
            def _():
                others(xb, 0)

        pre[t - 6] = product(xb, q, c, 0, 2) + product(xb, q, 1 - c, 0, 2)

    def consume(t):
        xb, q = info(t)

        @pl.when(t < 6)
        def _():
            total[...] = product(xb, q, c, 0, 4)

            @pl.when(q == 0)
            def _():
                others(xb, 0)

            others_last(xb, q)
            total[...] = (total[...] + product(xb, q, 1 - c, 0, 4)) * (1.0 / SEQS)

        @pl.when(t >= 6)
        def _():
            late = lax.max(t - 6, 0)
            total[...] = pre[late] + product(xb, q, c, 2, 2)
            others_last(xb, q)
            total[...] = (total[...] + product(xb, q, 1 - c, 2, 2)) * (1.0 / SEQS)

        o = lax.rem(xb + X - x, X)

        @pl.when(o == 0)
        def _():
            own[q] = total[...]

        @pl.when(o == 2)
        def _():
            s2[q] = total[...].astype(BF16)

            def send(first, rows, slot):
                relay_up(q, first, rows, slot).start()
                relay_dn(q, first, rows, slot).start()

            parts_of(t, send)

        @pl.when(o == 1)
        def _():
            s1[q, pl.ds(256, 256)] = total[pl.ds(256, 256)].astype(BF16)
            final_up(q, 256, 256)
            hold[lax.rem(t, 3)] = total[pl.ds(0, 256)]

        @pl.when(o == 3)
        def _():
            s3[q, pl.ds(0, 256)] = total[pl.ds(0, 256)].astype(BF16)
            final_dn(q, 0, 256)
            hold[lax.rem(t, 3)] = total[pl.ds(256, 256)]

    def finish(t):
        xb, q = info(t)
        o = lax.rem(xb + X - x, X)
        s = lax.rem(t, 3)

        @pl.when(o == 1)
        def _():
            def add(first, rows, slot):
                part = pl.ds(first, rows)
                relay_up(q, first, rows, slot).wait_recv()
                s1[q, part] = (hold[s, part] + rl[q, part].astype(F32)).astype(BF16)
                final_up(q, first, rows)

            parts_of(t, add)

        @pl.when(o == 3)
        def _():
            def add(first, rows, slot):
                part = pl.ds(first, rows)
                relay_dn(q, first, rows, slot).wait_recv()
                s3[q, pl.ds(256 + first, rows)] = (hold[s, part] + rr[q, part].astype(F32)).astype(BF16)
                final_dn(q, 256 + first, rows)

            parts_of(t, add)

    calls = {
        "loaded": loaded, "gram": lambda: gram(1), "gram0": lambda: gram(0), "E": ahead, "yl": first_steps, "yf": lambda q: first_far(3, q), "yg": lambda q: first_far(2, q), "o": own_chunk, "ol": own_left,
        "pairs": pair.start, "pairw": pair_wait, "ring": ring, "ringend": ring_end, "szs": squares,
        "szw": squares_wait, "syw": norms_wait, "aw": scale, "acts": acts, "arel": act_relay,
    }

    def run(plan):
        for name, *args in plan:
            if name == "r":
                receive(*args)
            else:
                calls[name](*args)

    rounds = {True: [[]], False: [[]]}
    for src, plan in ((True, SOURCE), (False, OTHER)):
        for item in plan:
            if item == ("C",):
                rounds[src].append([])
            else:
                rounds[src][-1].append(item)

    run(FIRST)

    @pl.when(is_src)
    def _():
        run(rounds[True][0])

    @pl.when(jnp.logical_not(is_src))
    def _():
        run(rounds[False][0])

    def round_of(t, _):
        for src in (True, False):
            for r in range(1, 8):
                if rounds[src][r]:
                    @pl.when(jnp.logical_and(t == r, is_src == src))
                    def _():
                        run(rounds[src][r])

        consume(t)

        @pl.when(t > 1)
        def _():
            finish(t - 2)

        return 0

    lax.fori_loop(0, 8, round_of, 0)
    finish(6)
    finish(7)

    @pl.when(is_src)
    def _():
        for j in range(4):
            if ("ol", j) not in SOURCE:
                own_left(j)
        wait_bytes(gbuf.at[pl.ds(0, 2), :, c], zsend)

    @pl.when(jnp.logical_not(is_src))
    def _():
        wait_bytes(gbuf.at[pl.ds(0, 3), :, c], zsend)

    wait_bytes(gbuf.at[:, :, c], psend)

    @pl.when(steps_y == 0)
    def _():
        for q in range(NQ):
            first(q, 1 - c).wait_send()

    @pl.when(steps_y >= 1)
    def _():
        for q in range(NQ):
            first(q, 0).wait_send()
            first(q, 1).wait_send()

    pair.wait_send()
    for i in range(1, 5):
        ring_up(i).wait_send()
    for i in range(1, 4):
        ring_dn(i).wait_send()
    wait_bytes(sz.at[pl.ds(0, 7)], szsend)
    wait_bytes(sy.at[pl.ds(0, 7)], sysend)
    wait_bytes(at.at[y], asend.at[0])
    wait_bytes(at.at[y], asend.at[1])
    for h in range(2):
        wait_bytes(at.at[y, h], afsend.at[h])
    wait_bytes(rl, rsend.at[0])
    wait_bytes(rr, rsend.at[1])

    for q in range(NQ):
        wait_bytes(fl.at[q], flrecv.at[q])
        wait_bytes(fr.at[q], frrecv.at[q])
        block = own[q] + fl[q].astype(F32) + fr[q].astype(F32)
        out_ref[pl.ds(q * W, W), :] = block.T.astype(BF16)
    wait_bytes(s1, fsend.at[0])
    wait_bytes(s3, fsend.at[1])


def local(activations, out_grads, lengths):
    dma, vmem = pltpu.SemaphoreType.DMA, pltpu.VMEM
    grams = (2, 3, 16, 128)
    scratch = [
        pltpu.SMEM((2,), jnp.int32),
        vmem((2, SLOT_LEN, F), BF16),
        vmem((2, SLOT_LEN, F), BF16),
        vmem((X, NQ, 2, Y, SLOT_LEN, W), BF16),
        vmem((Y, 2, F, SLOT_LEN), BF16),
        vmem((2, F, Y * SLOT_LEN), BF16),
        vmem((2, Z) + grams, F32),
        vmem((Z,) + grams, F32),
        vmem((Z,) + grams, F32),
        vmem((4,) + grams, F32),
        vmem((3,) + grams, F32),
        vmem((3,) + grams, F32),
        vmem((2,) + grams, F32),
        vmem((Z, 8, 128), F32),
        vmem((2 * Y, 8, 128), F32),
        vmem((3, 256, W), F32),
        vmem((F, W), F32),
        vmem((2, F, W), F32),
        vmem((NQ, F, W), F32),
        vmem((NQ, F, W), BF16),
        vmem((NQ, F, W), BF16),
        vmem((NQ, F, W), BF16),
        vmem((NQ, 256, W), BF16),
        vmem((NQ, 256, W), BF16),
        vmem((NQ, F, W), BF16),
        vmem((NQ, F, W), BF16),
        dma((3,)), dma((NQ, 2)), dma((NQ, Y)), dma((4,)), dma((4,)), dma, dma((X, 4)),
        dma, dma((X, 3)), dma((2,)), dma((2,)), dma((2,)), dma((2,)), dma((2,)),
        dma, dma, dma((4,)), dma((4,)), dma((3,)), dma((3,)), dma, dma, dma, dma,
        dma((2,)), dma((NQ, 2)), dma((NQ, 2)), dma((2,)), dma((NQ,)), dma((NQ,)),
    ]
    return pl.pallas_call(
        kernel,
        out_shape=(
            jax.ShapeDtypeStruct((F, F), BF16),
            jax.ShapeDtypeStruct((2,), F32),
        ),
        in_specs=[
            pl.BlockSpec(memory_space=pl.ANY),
            pl.BlockSpec(memory_space=pl.ANY),
            pl.BlockSpec(memory_space=pl.ANY),
        ],
        out_specs=(
            pl.BlockSpec(memory_space=pltpu.VMEM),
            pl.BlockSpec(memory_space=pltpu.SMEM),
        ),
        scratch_shapes=scratch,
        compiler_params=pltpu.CompilerParams(
            collective_id=0, has_side_effects=True, vmem_limit_bytes=40 * 1024 * 1024
        ),
        cost_estimate=pl.CostEstimate(flops=2 * 512 * 512 * 8192, bytes_accessed=3 * 2**19, transcendentals=0),
    )(*(pltpu.with_memory_space_constraint(v, pltpu.HBM) for v in (lengths, activations, out_grads)))


def solution(mesh):
    placed = (P("dp", None, "tensor"), P("dp", None, "tensor"), P("dp"))
    return jax.shard_map(
        local, mesh=mesh, in_specs=placed, out_specs=(P("dp", "tensor"), P("dp")), check_vma=False
    )
```
